32 devices in a mesh: dp: 16 (over z, y, core), tensor: 2 (over x).
Axes of the slice: x: 2, y: 2, z: 4, core: 2. Of those that a mesh axis runs over, the one named last changes fastest.
Arguments:
- tokens: bfloat16 [4096, 2048], P('dp'), may hold values from -6 to 6
- attn_gain: bfloat16 [2048], P('dp'), may hold values from 0.25 to 1.75
- w_query: bfloat16 [2048, 2048], P('dp', 'tensor'), may hold values from -0.125 to 0.125
- w_key: bfloat16 [2048, 512], P('dp', 'tensor'), may hold values from -0.125 to 0.125
- w_value: bfloat16 [2048, 512], P('dp', 'tensor'), may hold values from -0.125 to 0.125
- w_out: bfloat16 [2048, 2048], P('tensor', 'dp'), may hold values from -0.5 to 0.5
- mlp_gain: bfloat16 [2048], P('dp'), may hold values from 0.25 to 1.75
- w_gate: bfloat16 [2048, 8192], P('dp', 'tensor'), may hold values from -0.125 to 0.125
- w_up: bfloat16 [2048, 8192], P('dp', 'tensor'), may hold values from -0.125 to 0.125
- w_down: bfloat16 [8192, 2048], P('tensor', 'dp'), may hold values from -0.0625 to 0.0625
- segment_ids: int32 [4096], P('dp'), may hold values from 0 to 31, never falling along the last dimension, each value on 1 to 256 neighbouring positions
- cotangent: bfloat16 [4096, 2048], P('dp'), may hold values from -6 to 6
Outputs:
- output: bfloat16 [4096, 2048], P('dp')
- input_grad: float32 [4096, 2048], P('dp')
- attn_gain_grad: float32 [2048], P('dp')
- query_grad: float32 [2048, 2048], P('dp', 'tensor')
- key_grad: float32 [2048, 512], P('dp', 'tensor')
- value_grad: float32 [2048, 512], P('dp', 'tensor')
- out_grad: float32 [2048, 2048], P('tensor', 'dp')
- mlp_gain_grad: float32 [2048], P('dp')
- gate_grad: float32 [2048, 8192], P('dp', 'tensor')
- up_grad: float32 [2048, 8192], P('dp', 'tensor')
- down_grad: float32 [8192, 2048], P('tensor', 'dp')
The draws below stay inside these ranges and needn't reach their ends.
Inputs may be any that keep to these rules, and one draw needn't show every extreme that they name: `segment_ids`: segment numbers never fall along the tokens, every number from 0 up is used, and each document spans 1 to 256 tokens, one exactly 256.
All inputs are finite; a program needn't handle non-finite values.
Results may differ from the reference program's by a relative error of at most 0.015.
Values may be sent and summed in bfloat16 or wider, within the bound.
A program may use at most 256 MiB of HBM per device.

```python
import math
import jax
import jax.numpy as jnp
import numpy as np
from jax import lax

D = 2048
HEADS = 32
KV_HEADS = 8
HEAD_DIM = 64
FF = 8192
SEQ = 256
TOKENS = 4096
N_DP = 16


def raised(drawn, stream_key, source, target, parts, factor):
    def block_of(dim):
        return (jnp.arange(drawn.shape[dim]) // (drawn.shape[dim] // parts)).reshape((-1,) + (1,) * (drawn.ndim - 1 - dim))

    first = jax.random.permutation(stream_key, parts)[block_of(target)]
    far = (block_of(target) + parts // 2) % parts
    return jnp.where((block_of(source) == first) | (block_of(source) == far), factor * drawn, drawn)


def shard_levels(own_key, extent, cuts, low, top_value):
    gain, own = 1.0, jax.random.fold_in(own_key, 6)
    for axis_at, shards_of in cuts:
        steps = jnp.exp(jax.random.uniform(jax.random.fold_in(own, axis_at), (shards_of,), jnp.float32, low / len(cuts), top_value / len(cuts)))
        gain = gain * jnp.repeat(steps, extent[axis_at] // shards_of).reshape([-1 if axis == axis_at else 1 for axis in range(len(extent))])
    return gain


def profile(amount, total, bound, skew):
    loads = [(1 << 20) // math.isqrt(standing ** skew) + 1 for standing in range(2, amount + 1)]
    rest, counts = total - bound - (amount - 1), [1] * (amount - 1)
    while rest > 0:
        free = [i for i in range(amount - 1) if counts[i] < bound]
        mass, remaining = sum([loads[i] for i in free]), rest
        for i in free:
            addition = min(bound - counts[i], max(1, remaining * loads[i] // mass), rest)
            counts[i] = counts[i] + addition
            rest = rest - addition
    return np.array([bound] + counts)


def ragged_sizes(stream_key, amount, total, bound, lean):
    if amount == 2:
        one = jax.random.randint(stream_key, (), max(1, total - bound), min(bound, total - 1) + 1)
        return jnp.stack([one, total - one])
    sizes = jnp.asarray(profile(amount, total, bound, lean), jnp.int32)
    couples = (amount - 1) // 2
    source_of, receiver = sizes[1:1 + 2 * couples:2], sizes[2:2 + 2 * couples:2]
    room = jnp.minimum(source_of - 1, bound - receiver)
    moved = jax.random.randint(jax.random.fold_in(stream_key, 1), (couples,), 0, 1 << 20) % (room + 1)
    sizes = sizes.at[1:1 + 2 * couples:2].set(source_of - moved).at[2:2 + 2 * couples:2].set(receiver + moved)
    return sizes[jax.random.permutation(jax.random.fold_in(stream_key, 2), amount)]


def normal_values(rng, extent, deviation, most, split=(), kind=jnp.bfloat16):
    entries = jax.random.normal(rng, extent, jnp.float32) * deviation
    if len(split) > 0:
        entries = shard_levels(rng, extent, split, -0.22, 0.18) * entries
    return jnp.clip(entries, min=-most, max=most).astype(kind)


def bell_draw_with(stream_key, dims, spread, reach, cuts, heavy, held_as=jnp.bfloat16):
    result = spread * jax.random.normal(stream_key, dims, jnp.float32)
    if cuts:
        result = result * shard_levels(stream_key, dims, cuts, -0.22, 0.18)
    return jnp.clip(raised(result, jax.random.fold_in(stream_key, 3), *heavy), -reach, reach).astype(held_as)


def setup_inputs(seed: int = 0) -> dict:
    streams_of = jax.random.split(jax.random.key(seed), 13)
    return {
        "tokens": bell_draw_with(streams_of[0], (TOKENS, D), 1.0, 6.0, ((0, 16),), (0, 1, 16, 2.0)),
        "attn_gain": jnp.clip(1.0 + 0.15 * jax.random.normal(streams_of[1], (D,), jnp.float32), 0.25, 1.75).astype(jnp.bfloat16),
        "w_query": normal_values(streams_of[2], (D, HEADS * HEAD_DIM), D ** -0.5, 0.125, ((0, 16), (1, 2))),
        "w_key": normal_values(streams_of[3], (D, KV_HEADS * HEAD_DIM), D ** -0.5, 0.125, ((0, 16), (1, 2))),
        "w_value": normal_values(streams_of[4], (D, KV_HEADS * HEAD_DIM), D ** -0.5, 0.125, ((0, 16), (1, 2))),
        "w_out": normal_values(streams_of[5], (HEADS * HEAD_DIM, D), (HEADS * HEAD_DIM // 16) ** -0.5, 0.5, ((0, 2), (1, 16))),
        "mlp_gain": jnp.clip(1.0 + 0.15 * jax.random.normal(streams_of[6], (D,), jnp.float32), 0.25, 1.75).astype(jnp.bfloat16),
        "w_gate": normal_values(streams_of[7], (D, FF), D ** -0.5, 0.125, ((0, 16), (1, 2))),
        "w_up": normal_values(streams_of[8], (D, FF), D ** -0.5, 0.125, ((0, 16), (1, 2))),
        "w_down": normal_values(streams_of[9], (FF, D), FF ** -0.5, 0.0625, ((0, 2), (1, 16))),
        "segment_ids": jnp.searchsorted(jnp.cumsum(ragged_sizes(streams_of[10], TOKENS // (SEQ // 2), TOKENS, SEQ, 1)), jnp.arange(TOKENS), side="right").astype(jnp.int32),
        "cotangent": bell_draw_with(streams_of[11], (TOKENS, D), 1.0, 6.0, ((0, 16),), (0, 1, 16, 2.0)),
    }


@jax.custom_vjp
def low(v):
    return lax.optimization_barrier(v.astype(jnp.bfloat16)).astype(jnp.float32)

@jax.custom_vjp
def low_back(v):
    return v

def low_keep(v):
    return (low(v), None)

def low_pass(kept, grad):
    return (grad,)

def back_keep(v):
    return (v, None)

def back_low(kept, grad):
    return (low(grad),)
low.defvjp(low_keep, low_pass)
low_back.defvjp(back_keep, back_low)
EPSILON = 1e-05
THETA = 500000.0
HIGHEST = lax.Precision.HIGHEST

def positions(segment_ids, length):
    segments = segment_ids.reshape(-1, length)
    places = jnp.arange(length, dtype=jnp.int32)[None, :]
    earlier = jnp.concatenate([segments[:, :1], segments[:, :-1]], axis=1)
    begins = jnp.where((segments != earlier) | (places == 0), places, jnp.zeros_like(places))
    return places - lax.cummax(begins, axis=1)

def rotary(position):
    halves = HEAD_DIM // 2
    inverse = THETA ** (-2.0 * jnp.arange(halves, dtype=jnp.float32) / HEAD_DIM)
    angles = position.astype(jnp.float32)[..., None] * inverse
    return (jnp.cos(angles), jnp.sin(angles))

def rotate(values, cosine, sine_table):
    halves = values.shape[-1] // 2
    front_half = values[..., :halves]
    back_half = values[..., halves:]
    cos_wide = cosine[..., None, :]
    sin_wide = sine_table[..., None, :]
    return jnp.concatenate([front_half * cos_wide - back_half * sin_wide, back_half * cos_wide + front_half * sin_wide], axis=-1)

def inv_root(values):
    return lax.rsqrt(lax.optimization_barrier(jnp.mean(values * values, axis=-1, keepdims=True)) + EPSILON)

def attend(packed):
    query_states, key_states, value_states, segments = packed
    length, head_count, head_dim = query_states.shape
    kv_count = key_states.shape[1]
    grouped = query_states.reshape(length, kv_count, head_count // kv_count, head_dim)
    scores = jnp.einsum('qkgd,pkd->kgqp', grouped, key_states, precision=HIGHEST) * head_dim ** (-0.5)
    scores = low_back(scores)
    places = jnp.arange(length)
    allowed = (segments[:, None] == segments[None, :]) & (places[None, :] <= places[:, None])
    scores = jnp.where(allowed, scores, -1e+30)
    highest = lax.optimization_barrier(jnp.max(scores, axis=-1, keepdims=True))
    exponent = jnp.exp(scores - highest)
    attn_probs = exponent / lax.optimization_barrier(jnp.sum(exponent, axis=-1, keepdims=True))
    mixture = jnp.einsum('kgqp,pkd->qkgd', low(attn_probs), value_states, precision=HIGHEST)
    return mixture.reshape(length, head_count * head_dim)

def layer(tokens, attn_gain, w_query, w_key, w_value, w_out, mlp_gain, w_gate, w_up, w_down, segments, cosine, sine_table):
    seq_count, length = segments.shape
    normed = low(tokens * inv_root(tokens) * attn_gain)
    query_pre = low_back(jnp.dot(normed, w_query, precision=HIGHEST))
    key_pre = low_back(jnp.dot(normed, w_key, precision=HIGHEST))
    value_states = low(low_back(jnp.dot(normed, w_value, precision=HIGHEST)))
    query_states = low(rotate(query_pre.reshape(seq_count, length, HEADS, HEAD_DIM), cosine, sine_table))
    key_states = low(rotate(key_pre.reshape(seq_count, length, KV_HEADS, HEAD_DIM), cosine, sine_table))
    value_states = value_states.reshape(seq_count, length, KV_HEADS, HEAD_DIM)
    mixture = lax.map(jax.checkpoint(attend), (query_states, key_states, value_states, segments))
    mixture = low(low_back(mixture.reshape(seq_count * length, HEADS * HEAD_DIM)))
    hidden = tokens + low_back(jnp.dot(mixture, w_out, precision=HIGHEST))
    normed_two = low(hidden * inv_root(hidden) * mlp_gain)
    gate_proj = low_back(jnp.dot(normed_two, w_gate, precision=HIGHEST))
    up_proj = low_back(jnp.dot(normed_two, w_up, precision=HIGHEST))
    activated = low(gate_proj / (1.0 + jnp.exp(-gate_proj)) * up_proj)
    return hidden + low_back(jnp.dot(activated, w_down, precision=HIGHEST))

def reference(tokens, attn_gain, w_query, w_key, w_value, w_out, mlp_gain, w_gate, w_up, w_down, segment_ids, cotangent):
    length = SEQ
    group_size = min(N_DP, max(1, 4096 // length))
    batches = N_DP // group_size
    cosine, sine_table = rotary(positions(segment_ids, length))
    params = tuple((weight.astype(jnp.float32) for weight in (attn_gain, w_query, w_key, w_value, w_out, mlp_gain, w_gate, w_up, w_down)))
    inputs = tokens.astype(jnp.float32).reshape(batches, group_size * length, D)
    grads_in = cotangent.astype(jnp.float32).reshape(batches, group_size * length, D)
    segments = segment_ids.reshape(batches, group_size, length)
    cos_groups = cosine.reshape(batches, group_size, length, HEAD_DIM // 2)
    sin_groups = sine_table.reshape(batches, group_size, length, HEAD_DIM // 2)

    def step(summed_grads, packed):
        batch_in, batch_seg, batch_cos, batch_sin, batch_grad = packed

        def forward(values, *weights):
            return layer(values, *weights, batch_seg, batch_cos, batch_sin)
        result_rows, pull_back = jax.vjp(forward, batch_in, *params)
        grads = pull_back(batch_grad)
        summed_grads = tuple((first_term + second_term for first_term, second_term in zip(summed_grads, grads[1:])))
        return (summed_grads, (result_rows.astype(jnp.bfloat16), grads[0]))
    zeros = tuple((jnp.zeros_like(weight) for weight in params))
    summed_grads, (outputs, input_grads) = lax.scan(step, zeros, (inputs, segments, cos_groups, sin_groups, grads_in))
    return (outputs.reshape(-1, D), input_grads.reshape(-1, D)) + summed_grads
```

```python
import functools

import jax
import jax.numpy as jnp
from jax import lax
from jax.experimental import pallas as pl
from jax.experimental.pallas import tpu as pltpu
from jax.sharding import PartitionSpec as P

HEAD_DIM = 64
EPSILON = 1e-05
THETA = 500000.0
MESH = pl.DeviceIdType.MESH
ANY = pl.BlockSpec(memory_space=pl.ANY)
VMEM = pl.BlockSpec(memory_space=pltpu.VMEM)
F32 = jnp.float32
BF16 = jnp.bfloat16
DMA = pltpu.SemaphoreType.DMA


class Place:
    def __init__(self, mid):
        self.mid = mid
        self.d = lax.axis_index("dp")
        self.x = lax.axis_index("tensor")
        self.c = self.d % 2
        self.m = (self.d // 2) % mid
        self.z = self.d // (2 * mid)
        self.lo = self.z % 2

    def dp(self, z, m, c):
        return (z * self.mid + m) * 2 + c

    def peer(self, k):
        return xor(self.z, k // 2), xor(self.c, k % 2)

    def other_m(self, j):
        return (self.m + 1 + j) % self.mid


def xor(a, k):
    if k == 0:
        return a
    low = a % 2
    high = a // 2
    if k % 2:
        low = 1 - low
    if k // 2:
        high = 1 - high
    return high * 2 + low


def remote(src, dst, send, recv, device):
    copy = pltpu.make_async_remote_copy(
        src_ref=src, dst_ref=dst, send_sem=send, recv_sem=recv, device_id=device, device_id_type=MESH
    )
    return copy


def greet(devices):
    barrier = pltpu.get_barrier_semaphore()
    for device in devices:
        pl.semaphore_signal(barrier, inc=1, device_id=device, device_id_type=MESH)
    pl.semaphore_wait(barrier, len(devices))


def gather_kernel(
    mid, tok, cot, ids, wa, wm, tokg, cotg, idsg, fa, fm,
    tok_s, tok_r, ids_s, ids_r, a_s, a_r, af_s, m_s, m_r, mf_s, loc,
):
    p = Place(mid)
    half = tok.shape[0] // 2
    greet(
        [(p.dp(z, p.m, c), p.x) for z, c in map(p.peer, range(1, 8))]
        + [(p.dp(p.z, p.other_m(j), p.c), p.x) for j in range(mid - 1)]
        + [(p.d, 1 - p.x)]
    )
    seq = p.lo * 2 + p.c
    z_near = (p.dp(xor(p.z, 1), p.m, p.c), p.x)
    c_near = (p.dp(p.z, p.m, 1 - p.c), p.x)
    x_near = (p.d, 1 - p.x)
    mine = pl.ds(p.x * half, half)
    theirs = pl.ds((1 - p.x) * half, half)
    far_seq = (1 - p.lo) * 2 + p.c
    sends = []

    def go(copy):
        copy.start()
        sends.append(copy)

    locals_ = []

    def here(src, dst, number):
        copy = pltpu.make_async_copy(src, dst, loc.at[number])
        copy.start()
        locals_.append(copy)

    for n, (src, dst) in enumerate(((tok, tokg), (cot, cotg))):
        go(remote(src.at[mine], dst.at[seq, mine], tok_s.at[n, 0], tok_r.at[n, 0], z_near))
        go(remote(src, dst.at[seq], tok_s.at[n, 1], tok_r.at[n, 1], c_near))
        here(src, dst.at[seq], n)
        if n == 0:
            go(remote(ids, idsg.at[seq], ids_s.at[0], ids_r.at[0], z_near))
            go(remote(ids, idsg.at[seq], ids_s.at[1], ids_r.at[1], c_near))
            here(ids, idsg.at[seq], 2)
            block = p.lo * 2 + p.c
            here(wa.at[block], fa.at[p.d], 3)
            here(wm.at[block], fm.at[p.d], 4)
            for src_w, dst_w, s_sem, r_sem, f_sem in ((wa, fa, a_s, a_r, af_s), (wm, fm, m_s, m_r, mf_s)):
                for k in range(7, 0, -1):
                    z, c = p.peer(k)
                    go(
                        remote(
                            src_w.at[(z % 2) * 2 + c], dst_w.at[p.d], s_sem.at[k], r_sem.at[p.d],
                            (p.dp(z, p.m, c), p.x),
                        )
                    )
                for j in range(mid - 1):
                    go(
                        remote(
                            src_w.at[block], dst_w.at[p.d], f_sem.at[0, j], r_sem.at[p.d],
                            (p.dp(p.z, p.other_m(j), p.c), p.x),
                        )
                    )

    def arrived(dst, sem):
        pltpu.make_async_copy(dst, dst, sem).wait()

    arrived(idsg.at[far_seq], ids_r.at[0])
    go(remote(idsg.at[far_seq], idsg.at[far_seq], ids_s.at[2], ids_r.at[2], c_near))
    for n, dst in enumerate((tokg, cotg)):
        arrived(dst.at[far_seq, mine], tok_r.at[n, 0])
        go(remote(dst.at[far_seq, mine], dst.at[far_seq, mine], tok_s.at[n, 2], tok_r.at[n, 2], x_near))
        go(remote(dst.at[far_seq, mine], dst.at[far_seq, mine], tok_s.at[n, 3], tok_r.at[n, 3], c_near))
    for n, dst in enumerate((tokg, cotg)):
        arrived(dst.at[far_seq, theirs], tok_r.at[n, 2])
        go(remote(dst.at[far_seq, theirs], dst.at[far_seq, theirs], tok_s.at[n, 4], tok_r.at[n, 4], c_near))
    for dst_w, r_sem, f_sem in ((fa, a_r, af_s), (fm, m_r, mf_s)):
        for k in range(7, 0, -1):
            z, c = p.peer(k)
            src_d = p.dp(z, p.m, c)
            arrived(dst_w.at[src_d], r_sem.at[src_d])
            for j in range(mid - 1):
                go(
                    remote(
                        dst_w.at[src_d], dst_w.at[src_d], f_sem.at[k, j], r_sem.at[src_d],
                        (p.dp(p.z, p.other_m(j), p.c), p.x),
                    )
                )
    c_seq = p.lo * 2 + 1 - p.c
    cc_seq = (1 - p.lo) * 2 + 1 - p.c
    arrived(idsg.at[c_seq], ids_r.at[1])
    arrived(idsg.at[cc_seq], ids_r.at[2])
    for n, dst in enumerate((tokg, cotg)):
        arrived(dst.at[c_seq], tok_r.at[n, 1])
        arrived(dst.at[cc_seq, mine], tok_r.at[n, 3])
        arrived(dst.at[cc_seq, theirs], tok_r.at[n, 4])
    for dst_w, r_sem in ((fa, a_r), (fm, m_r)):
        for k in range(8):
            z, c = p.peer(k)
            for j in range(mid - 1):
                src_d = p.dp(z, p.other_m(j), c)
                arrived(dst_w.at[src_d], r_sem.at[src_d])
    for copy in locals_:
        copy.wait()
    for copy in sends:
        copy.wait_send()


def gather(mid, tok, cot, ids, wa, wm):
    n = mid * 8
    return pl.pallas_call(
        functools.partial(gather_kernel, mid),
        out_shape=(
            jax.ShapeDtypeStruct((4,) + tok.shape, BF16),
            jax.ShapeDtypeStruct((4,) + cot.shape, BF16),
            jax.ShapeDtypeStruct((4,) + ids.shape, ids.dtype),
            jax.ShapeDtypeStruct((n,) + wa.shape[1:], BF16),
            jax.ShapeDtypeStruct((n,) + wm.shape[1:], BF16),
        ),
        in_specs=[ANY] * 5,
        out_specs=(ANY,) * 5,
        scratch_shapes=[
            DMA((2, 5)), DMA((2, 5)), DMA((3,)), DMA((3,)),
            DMA((8,)), DMA((n,)), DMA((8, mid - 1)),
            DMA((8,)), DMA((n,)), DMA((8, mid - 1)),
            DMA((5,)),
        ],
        compiler_params=pltpu.CompilerParams(collective_id=0, has_side_effects=True),
    )(tok, cot, ids, wa, wm)


def scatter_kernel(mid, rows, g, out, ybuf, sums, y_s, y_r, z_s, z_r, loc):
    p = Place(mid)
    greet(
        [(p.dp(z, p.m, c), p.x) for z, c in map(p.peer, range(1, 8))]
        + [(p.dp(p.z, p.other_m(j), p.c), p.x) for j in range(mid - 1)]
    )
    sends = []
    order = list(range(7, -1, -1))
    for k in order:
        z, c = p.peer(k)
        for j in range(mid - 1):
            m = p.other_m(j)
            copy = remote(
                g.at[p.dp(z, m, c)], ybuf.at[mid - 2 - j, k], y_s.at[k, j], y_r.at[k, mid - 2 - j],
                (p.dp(p.z, m, p.c), p.x),
            )
            copy.start()
            sends.append(copy)
    step = 16
    for k in order:
        z, c = p.peer(k)
        for j in range(mid - 1):
            pltpu.make_async_copy(ybuf.at[j, k], ybuf.at[j, k], y_r.at[k, j]).wait()
        own = p.dp(z, p.m, c)

        def add(i, carry):
            at = pl.ds(pl.multiple_of(i * step, step), step)
            total = g[own, at, :].astype(F32)
            for j in range(mid - 1):
                total = total + ybuf[j, k, at, :].astype(F32)
            sums[k, at, :] = total.astype(BF16)
            return carry

        lax.fori_loop(0, rows // step, add, 0)
        me = p.z * 2 + p.c
        if k == 0:
            copy = pltpu.make_async_copy(sums.at[k], out.at[me], loc)
            copy.start()
            copy.wait()
        else:
            copy = remote(sums.at[k], out.at[me], z_s.at[k], z_r.at[me], (p.dp(z, p.m, c), p.x))
            copy.start()
            sends.append(copy)
    for k in range(1, 8):
        z, c = p.peer(k)
        src = z * 2 + c
        pltpu.make_async_copy(out.at[src], out.at[src], z_r.at[src]).wait()
    for copy in sends:
        copy.wait_send()


def scatter(mid, g):
    n, rows, width = g.shape
    return pl.pallas_call(
        functools.partial(scatter_kernel, mid, rows),
        out_shape=jax.ShapeDtypeStruct((8, rows, width), BF16),
        in_specs=[VMEM],
        out_specs=ANY,
        scratch_shapes=[
            pltpu.VMEM((mid - 1, 8, rows, width), BF16),
            pltpu.VMEM((8, rows, width), BF16),
            DMA((8, mid - 1)), DMA((8, mid - 1)), DMA((8,)), DMA((8,)), DMA,
        ],
        compiler_params=pltpu.CompilerParams(
            collective_id=1, has_side_effects=True, vmem_limit_bytes=56 << 20
        ),
    )(g)


def group_devices(p):
    far = xor(p.z, 1)
    return {
        (0, 1): (p.d, 1 - p.x),
        (1, 0): (p.dp(far, p.m, p.c), p.x),
        (1, 1): (p.dp(far, p.m, p.c), 1 - p.x),
    }, (p.dp(p.z, p.m, 1 - p.c), p.x)


def reduce_to_owner(p, part, abuf, sums, bbuf, sems, sends, finish):
    a_s, a_r, b_s, b_r = sems
    chips, sibling = group_devices(p)
    order = ((1, 1), (0, 1), (1, 0), (0, 0))
    for n, (fz, fx) in enumerate(order):
        lo, x = xor(p.lo, fz), xor(p.x, fx)
        copy = remote(part.at[(lo * 2 + 1 - p.c) * 2 + x], abuf.at[n], a_s.at[n], a_r.at[n], sibling)
        copy.start()
        sends.append(copy)
    rows = part.shape[1]
    step = 16
    for n, (fz, fx) in enumerate(order):
        lo, x = xor(p.lo, fz), xor(p.x, fx)
        own = (lo * 2 + p.c) * 2 + x
        pltpu.make_async_copy(abuf.at[n], abuf.at[n], a_r.at[n]).wait()
        if n == 3:
            break

        def add(i, carry):
            at = pl.ds(pl.multiple_of(i * step, step), step)
            sums[n, at, :] = (part[own, at, :].astype(F32) + abuf[n, at, :].astype(F32)).astype(BF16)
            return carry

        lax.fori_loop(0, rows // step, add, 0)
        copy = remote(sums.at[n], bbuf.at[n], b_s.at[n], b_r.at[n], chips[(fz, fx)])
        copy.start()
        sends.append(copy)
    mine = (p.lo * 2 + p.c) * 2 + p.x
    for n in range(3):
        pltpu.make_async_copy(bbuf.at[n], bbuf.at[n], b_r.at[n]).wait()

    def last(i, carry):
        at = pl.ds(pl.multiple_of(i * step, step), step)
        total = part[mine, at, :].astype(F32) + abuf[3, at, :].astype(F32)
        for n in range(3):
            total = total + bbuf[n, at, :].astype(F32)
        finish(at, total)
        return carry

    lax.fori_loop(0, rows // step, last, 0)


def share_with_group(p, gathered, sems, sends):
    s, r = sems
    chips, sibling = group_devices(p)
    mine = (p.lo * 2 + p.c) * 2 + p.x
    order = ((1, 1), (0, 1), (1, 0))
    for n, flips in enumerate(order):
        copy = remote(gathered.at[mine], gathered.at[mine], s.at[n], r.at[n], chips[flips])
        copy.start()
        sends.append(copy)
    copy = remote(gathered.at[mine], gathered.at[mine], s.at[3], r.at[3], sibling)
    copy.start()
    sends.append(copy)
    for n, (fz, fx) in enumerate(order):
        at = (xor(p.lo, fz) * 2 + p.c) * 2 + xor(p.x, fx)
        pltpu.make_async_copy(gathered.at[at], gathered.at[at], r.at[n]).wait()
        copy = remote(gathered.at[at], gathered.at[at], s.at[4 + n], r.at[4 + n], sibling)
        copy.start()
        sends.append(copy)
    for n, (fz, fx) in enumerate(order + ((0, 0),)):
        at = (xor(p.lo, fz) * 2 + 1 - p.c) * 2 + xor(p.x, fx)
        number = 3 if n == 3 else 4 + n
        pltpu.make_async_copy(gathered.at[at], gathered.at[at], r.at[number]).wait()


def group_greet(p):
    chips, sibling = group_devices(p)
    greet(list(chips.values()) + [sibling])


def forward_mid_kernel(mid, part, x, gain, hidden, normed, abuf, sums, bbuf, a_s, a_r, b_s, b_r, g_s, g_r):
    p = Place(mid)
    group_greet(p)
    sends = []
    mine = (p.lo * 2 + p.c) * 2 + p.x

    def finish(at, total):
        value = x[at, :].astype(F32) + total
        hidden[at, :] = value
        root = lax.rsqrt(jnp.mean(value * value, axis=-1, keepdims=True) + EPSILON)
        normed[mine, at, :] = (value * root * gain[...].astype(F32)).astype(BF16)

    reduce_to_owner(p, part, abuf, sums, bbuf, (a_s, a_r, b_s, b_r), sends, finish)
    share_with_group(p, normed, (g_s, g_r), sends)
    for copy in sends:
        copy.wait_send()


def rs_scratch(rows, width):
    return [
        pltpu.VMEM((4, rows, width), BF16),
        pltpu.VMEM((3, rows, width), BF16),
        pltpu.VMEM((3, rows, width), BF16),
        DMA((4,)), DMA((4,)), DMA((3,)), DMA((3,)),
    ]


def forward_mid(mid, part, x, gain):
    eight, rows, width = part.shape
    return pl.pallas_call(
        functools.partial(forward_mid_kernel, mid),
        out_shape=(
            jax.ShapeDtypeStruct((rows, width), F32),
            jax.ShapeDtypeStruct((eight, rows, width), BF16),
        ),
        in_specs=[VMEM] * 3,
        out_specs=(VMEM,) * 2,
        scratch_shapes=rs_scratch(rows, width) + [DMA((7,)), DMA((7,))],
        compiler_params=pltpu.CompilerParams(
            collective_id=2, has_side_effects=True, vmem_limit_bytes=56 << 20
        ),
    )(part, x, gain)


def backward_mid_kernel(
    mid, part, out_part, hid, cot, gain, grad_hidden, low, output, gain_grad,
    abuf, sums, bbuf, a_s, a_r, b_s, b_r, abuf2, sums2, bbuf2, a_s2, a_r2, b_s2, b_r2, g_s, g_r, o_s, o_r,
):
    p = Place(mid)
    group_greet(p)
    sends = []
    mine = (p.lo * 2 + p.c) * 2 + p.x
    rows, width = hid.shape
    gain_grad[...] = jnp.zeros_like(gain_grad)

    def finish(at, total):
        value = hid[at, :]
        root = lax.rsqrt(jnp.mean(value * value, axis=-1, keepdims=True) + EPSILON)
        scaled = total * gain[...].astype(F32)
        back = root * scaled - value * root**3 * jnp.mean(value * scaled, axis=-1, keepdims=True)
        grads = cot[at, :].astype(F32) + back
        grad_hidden[at, :] = grads
        low[mine, at, :] = grads.astype(BF16)
        term = total * value * root
        gain_grad[...] += term[:8] + term[8:]

    reduce_to_owner(p, part, abuf, sums, bbuf, (a_s, a_r, b_s, b_r), sends, finish)
    share_with_group(p, low, (g_s, g_r), sends)

    def finish_out(at, total):
        there = pl.ds(pl.multiple_of(p.x * rows + at.start, 16), 16)
        output[there, :] = (hid[at, :] + total).astype(BF16)

    reduce_to_owner(p, out_part, abuf2, sums2, bbuf2, (a_s2, a_r2, b_s2, b_r2), sends, finish_out)
    half = pl.ds(pl.multiple_of(p.x * rows, rows), rows)
    copy = remote(output.at[half], output.at[half], o_s, o_r, (p.d, 1 - p.x))
    copy.start()
    sends.append(copy)
    copy.wait_recv()
    for copy in sends:
        copy.wait_send()


def backward_mid(mid, part, out_part, hid, cot, gain):
    eight, rows, width = part.shape
    return pl.pallas_call(
        functools.partial(backward_mid_kernel, mid),
        out_shape=(
            jax.ShapeDtypeStruct((rows, width), F32),
            jax.ShapeDtypeStruct((eight, rows, width), BF16),
            jax.ShapeDtypeStruct((2 * rows, width), BF16),
            jax.ShapeDtypeStruct((8, width), F32),
        ),
        in_specs=[VMEM] * 5,
        out_specs=(VMEM,) * 4,
        scratch_shapes=rs_scratch(rows, width) * 2 + [DMA((7,)), DMA((7,)), DMA, DMA],
        compiler_params=pltpu.CompilerParams(
            collective_id=3, has_side_effects=True, vmem_limit_bytes=56 << 20
        ),
    )(part, out_part, hid, cot, gain)


def last_kernel(
    mid, part, grad_hidden, x, gain, result, gain_grad, abuf, sums, bbuf, a_s, a_r, b_s, b_r, o_s, o_r
):
    p = Place(mid)
    group_greet(p)
    sends = []
    rows, width = x.shape
    gain_grad[...] = jnp.zeros_like(gain_grad)

    def finish(at, total):
        value = x[at, :].astype(F32)
        root = lax.rsqrt(jnp.mean(value * value, axis=-1, keepdims=True) + EPSILON)
        scaled = total * gain[...].astype(F32)
        back = root * scaled - value * root**3 * jnp.mean(value * scaled, axis=-1, keepdims=True)
        there = pl.ds(pl.multiple_of(p.x * rows + at.start, 16), 16)
        result[there, :] = (grad_hidden[at, :] + back).astype(BF16)
        term = total * value * root
        gain_grad[...] += term[:8] + term[8:]

    reduce_to_owner(p, part, abuf, sums, bbuf, (a_s, a_r, b_s, b_r), sends, finish)
    half = pl.ds(pl.multiple_of(p.x * rows, rows), rows)
    copy = remote(result.at[half], result.at[half], o_s, o_r, (p.d, 1 - p.x))
    copy.start()
    sends.append(copy)
    copy.wait_recv()
    for copy in sends:
        copy.wait_send()


def last(mid, part, grad_hidden, x, gain):
    eight, rows, width = part.shape
    return pl.pallas_call(
        functools.partial(last_kernel, mid),
        out_shape=(
            jax.ShapeDtypeStruct((2 * rows, width), BF16),
            jax.ShapeDtypeStruct((8, width), F32),
        ),
        in_specs=[VMEM] * 4,
        out_specs=(VMEM,) * 2,
        scratch_shapes=rs_scratch(rows, width) + [DMA, DMA],
        compiler_params=pltpu.CompilerParams(
            collective_id=4, has_side_effects=True, vmem_limit_bytes=56 << 20
        ),
    )(part, grad_hidden, x, gain)


def positions(segments):
    length = segments.shape[1]
    places = jnp.arange(length, dtype=jnp.int32)[None, :]
    earlier = jnp.concatenate([segments[:, :1], segments[:, :-1]], axis=1)
    begins = jnp.where((segments != earlier) | (places == 0), places, jnp.zeros_like(places))
    before = places[0][:, None] >= places[0][None, :]
    return places - jnp.max(jnp.where(before[None], begins[:, None, :], 0), axis=-1)


def rotary(position):
    halves = HEAD_DIM // 2
    inverse = THETA ** (-2.0 * jnp.arange(halves, dtype=jnp.float32) / HEAD_DIM)
    angles = position.astype(jnp.float32)[..., None] * inverse
    return (jnp.cos(angles), jnp.sin(angles))


def rotate(values, cosine, sine_table):
    halves = values.shape[-1] // 2
    front_half = values[..., :halves]
    back_half = values[..., halves:]
    cos_wide = cosine[..., None, :]
    sin_wide = sine_table[..., None, :]
    return jnp.concatenate(
        [
            front_half * cos_wide - back_half * sin_wide,
            back_half * cos_wide + front_half * sin_wide,
        ],
        axis=-1,
    )


def dot(a, b, dims):
    return lax.dot_general(a, b, (dims, ((), ())), preferred_element_type=F32)


def local(
    mid, tokens, attn_gain, w_query, w_key, w_value, w_out, mlp_gain, w_gate, w_up, w_down, segment_ids, cotangent
):
    length, width = tokens.shape
    half = length // 2
    rows = w_query.shape[0]
    x_at = lax.axis_index("tensor")

    def blocks(w):
        return w.reshape(rows, 4, w.shape[1] // 4).transpose(1, 0, 2)

    wm = jnp.concatenate([blocks(w_gate), blocks(w_up), blocks(w_down.T)], axis=-1)
    wa = jnp.concatenate([blocks(w_query), blocks(w_key), blocks(w_value), blocks(w_out.T)], axis=-1)
    ids = jnp.broadcast_to(segment_ids.reshape(1, length), (8, length))
    gains = lax.all_gather(jnp.stack([attn_gain, mlp_gain]), "dp", axis=1, tiled=True)
    gain_one, gain_two = gains[:1].astype(F32), gains[1:].astype(F32)
    tokg, cotg, idsg, fa, fm = gather(mid, tokens, cotangent, ids, wa, wm)
    fa = fa.reshape(width, -1)
    fm = fm.reshape(width, -1)
    units = w_gate.shape[1] // 4
    qw, kw = w_query.shape[1] // 4, w_key.shape[1] // 4
    heads = qw // HEAD_DIM
    gate_w, up_w, down_t = fm[:, :units], fm[:, units : 2 * units], fm[:, 2 * units :]
    qkv_w, out_t = fa[:, : qw + 2 * kw], fa[:, qw + 2 * kw :]

    segments = idsg[:, 0, :]
    cosine, sine = rotary(positions(segments))
    xs = tokg.reshape(4 * length, width)
    inputs = xs.astype(F32)
    root_one = lax.rsqrt(jnp.mean(inputs * inputs, axis=-1, keepdims=True) + EPSILON)
    normed = (inputs * root_one * gain_one).astype(BF16)
    qkv = dot(normed, qkv_w, ((1,), (0,)))
    q = rotate(qkv[:, :qw].reshape(4, length, heads, HEAD_DIM), cosine, sine).astype(BF16)
    k = rotate(qkv[:, qw : qw + kw].reshape(4, length, 1, HEAD_DIM), cosine, sine).astype(BF16)[:, :, 0]
    v = qkv[:, qw + kw :].reshape(4, length, HEAD_DIM).astype(BF16)
    places = jnp.arange(length)
    allowed = (segments[:, :, None] == segments[:, None, :]) & (places[None, :, None] >= places[None, None, :])
    scaling = HEAD_DIM ** (-0.5)
    scores = jnp.einsum("sqgd,spd->sgqp", q, k, preferred_element_type=F32) * scaling
    scores = jnp.where(allowed[:, None], scores, -1e30)
    highest = jnp.max(scores, axis=-1, keepdims=True)
    exponent = jnp.exp(scores - highest)
    probs = exponent / jnp.sum(exponent, axis=-1, keepdims=True)
    probs_low = probs.astype(BF16)
    mixture = jnp.einsum("sgqp,spd->sqgd", probs_low, v, preferred_element_type=F32)
    mixture = mixture.astype(BF16).reshape(4 * length, qw)
    attn_part = dot(mixture, out_t, ((1,), (1,))).astype(BF16)
    own_x = lax.dynamic_slice_in_dim(tokens, x_at * half, half, 0)
    own_cot = lax.dynamic_slice_in_dim(cotangent, x_at * half, half, 0)
    hidden, n2 = forward_mid(mid, attn_part.reshape(8, half, width), own_x, gain_two)
    n2 = n2.reshape(4 * length, width)

    gate = dot(n2, gate_w, ((1,), (0,)))
    up = dot(n2, up_w, ((1,), (0,)))
    sigmoid = 1.0 / (1.0 + jnp.exp(-gate))
    silu = gate / (1.0 + jnp.exp(-gate))
    activated = (silu * up).astype(BF16)
    out_part = dot(activated, down_t, ((1,), (1,))).astype(BF16)
    cots = cotg.reshape(4 * length, width)
    grad_act = dot(cots, down_t, ((1,), (0,)))
    grad_gate = (grad_act * up * sigmoid * (1.0 + gate * (1.0 - sigmoid))).astype(BF16)
    grad_up = (grad_act * silu).astype(BF16)
    grad_gu = jnp.concatenate([grad_gate, grad_up], axis=1)
    part_two = dot(grad_gu, fm[:, : 2 * units], ((1,), (1,))).astype(BF16)
    down_g = dot(cots, activated, ((0,), (0,))).astype(BF16)
    gu_g = dot(n2, grad_gu, ((0,), (0,))).astype(BF16)

    grad_hidden, ghl, output, gain_two_grad = backward_mid(
        mid, part_two.reshape(8, half, width), out_part.reshape(8, half, width), hidden, own_cot, gain_two
    )
    ghl = ghl.reshape(4 * length, width)
    grad_mix = dot(ghl, out_t, ((1,), (0,))).astype(BF16)
    gm = grad_mix.reshape(4, length, heads, HEAD_DIM)
    out_g = dot(ghl, mixture, ((0,), (0,))).astype(BF16)
    grad_probs = jnp.einsum("sqgd,spd->sgqp", gm, v, preferred_element_type=F32)
    grad_v = jnp.einsum("sgqp,sqgd->spd", probs_low, gm, preferred_element_type=F32).astype(BF16)
    centered = jnp.sum(probs * grad_probs, axis=-1, keepdims=True)
    gs = (probs * (grad_probs - centered)).astype(BF16)
    gq_rot = jnp.einsum("sgqp,spd->sqgd", gs, k, preferred_element_type=F32) * scaling
    gk_rot = jnp.einsum("sgqp,sqgd->spd", gs, q, preferred_element_type=F32) * scaling
    gq = rotate(gq_rot, cosine, -sine).astype(BF16).reshape(4 * length, qw)
    gk = rotate(gk_rot[:, :, None], cosine, -sine).astype(BF16).reshape(4 * length, kw)
    gqkv = jnp.concatenate([gq, gk, grad_v.reshape(4 * length, kw)], axis=1)
    part_one = dot(gqkv, qkv_w, ((1,), (1,))).astype(BF16)
    qkv_g = dot(normed, gqkv, ((0,), (0,))).astype(BF16)
    input_grad, gain_one_grad = last(mid, part_one.reshape(8, half, width), grad_hidden, own_x, gain_one)
    grads = jnp.concatenate([gu_g, down_g, qkv_g, out_g], axis=1).reshape(8 * mid, rows, -1)
    parts = scatter(mid, grads).reshape(2, 4, rows, -1).astype(F32)
    total = parts[0] + parts[1]

    def across(block):
        return block.transpose(1, 0, 2).reshape(rows, -1)

    def down(block):
        return block.transpose(0, 2, 1).reshape(-1, rows)

    at = [units, 2 * units, 3 * units, 3 * units + qw, 3 * units + qw + kw, 3 * units + qw + 2 * kw]
    t_gate, t_up, t_down, t_q, t_k, t_v, t_out = jnp.split(total, at, axis=-1)
    gain_grads = jnp.stack([jnp.sum(gain_one_grad, axis=0), jnp.sum(gain_two_grad, axis=0)])
    gain_grads = lax.psum_scatter(lax.psum(gain_grads, "tensor"), "dp", scatter_dimension=1, tiled=True)
    return (
        output,
        input_grad.astype(F32),
        gain_grads[0],
        across(t_q),
        across(t_k),
        across(t_v),
        down(t_out),
        gain_grads[1],
        across(t_gate),
        across(t_up),
        down(t_down),
    )


def solution(mesh):
    in_specs = (
        P("dp", None), P("dp"), P("dp", "tensor"), P("dp", "tensor"), P("dp", "tensor"), P("tensor", "dp"),
        P("dp"), P("dp", "tensor"), P("dp", "tensor"), P("tensor", "dp"), P("dp"), P("dp", None),
    )
    out_specs = (
        P("dp", None), P("dp", None), P("dp"), P("dp", "tensor"), P("dp", "tensor"), P("dp", "tensor"),
        P("tensor", "dp"), P("dp"), P("dp", "tensor"), P("dp", "tensor"), P("tensor", "dp"),
    )
    return jax.shard_map(
        functools.partial(local, mesh.shape["dp"] // 8),
        mesh=mesh, in_specs=in_specs, out_specs=out_specs, check_vma=False,
    )
```

```python
import functools

import jax
import jax.numpy as jnp
from jax import lax
from jax.experimental import pallas as pl
from jax.experimental.pallas import tpu as pltpu
from jax.sharding import PartitionSpec as P

HEAD_DIM = 64
EPSILON = 1e-05
THETA = 500000.0
MESH = pl.DeviceIdType.MESH
ANY = pl.BlockSpec(memory_space=pl.ANY)
VMEM = pl.BlockSpec(memory_space=pltpu.VMEM)
F32 = jnp.float32
BF16 = jnp.bfloat16
DMA = pltpu.SemaphoreType.DMA


class Place:
    def __init__(self, mid):
        self.mid = mid
        self.d = lax.axis_index("dp")
        self.x = lax.axis_index("tensor")
        self.c = self.d % 2
        self.m = (self.d // 2) % mid
        self.z = self.d // (2 * mid)
        self.lo = self.z % 2

    def dp(self, z, m, c):
        return (z * self.mid + m) * 2 + c

    def peer(self, k):
        return xor(self.z, k // 2), xor(self.c, k % 2)

    def other_m(self, j):
        return (self.m + 1 + j) % self.mid


def xor(a, k):
    if k == 0:
        return a
    low = a % 2
    high = a // 2
    if k % 2:
        low = 1 - low
    if k // 2:
        high = 1 - high
    return high * 2 + low


def remote(src, dst, send, recv, device):
    copy = pltpu.make_async_remote_copy(
        src_ref=src, dst_ref=dst, send_sem=send, recv_sem=recv, device_id=device, device_id_type=MESH
    )
    return copy


def greet(devices):
    barrier = pltpu.get_barrier_semaphore()
    for device in devices:
        pl.semaphore_signal(barrier, inc=1, device_id=device, device_id_type=MESH)
    pl.semaphore_wait(barrier, len(devices))


def arrived(dst, sem):
    pltpu.make_async_copy(dst, dst, sem).wait()


class Gather:
    def __init__(self, p, w, full, sems, waves):
        self.p, self.w, self.full, self.waves = p, w, full, waves
        self.z_s, self.r, self.f_s, self.loc = sems
        self.rows = w.shape[1] // waves
        self.block = p.lo * 2 + p.c
        self.order = list(range(7, 0, -1))
        self.pushes, self.sends = {}, []

    def at(self, wave):
        return pl.ds(wave * self.rows, self.rows)

    def push(self, wave):
        p, at = self.p, self.at(wave)
        for k in self.order:
            z, c = p.peer(k)
            copy = remote(
                self.w.at[(z % 2) * 2 + c, at], self.full.at[p.d, at], self.z_s.at[k, wave], self.r.at[p.d, wave],
                (p.dp(z, p.m, c), p.x),
            )
            copy.start()
            self.pushes[k, wave] = copy
        self.forward_one(self.w.at[self.block, at], p.d, wave, 0)

    def forward_one(self, src, d, wave, k):
        p = self.p
        for j in range(p.mid - 1):
            copy = remote(
                src, self.full.at[d, self.at(wave)], self.f_s.at[k, wave, j], self.r.at[d, wave],
                (p.dp(p.z, p.other_m(j), p.c), p.x),
            )
            copy.start()
            self.sends.append(copy)

    def forward(self, wave):
        p = self.p
        for k in self.order:
            z, c = p.peer(k)
            d = p.dp(z, p.m, c)
            here = self.full.at[d, self.at(wave)]
            arrived(here, self.r.at[d, wave])
            self.forward_one(here, d, wave, k)

    def start_own(self):
        self.own = pltpu.make_async_copy(self.w.at[self.block], self.full.at[self.p.d], self.loc)
        self.own.start()

    def pushed(self, wave):
        for k in self.order:
            self.pushes[k, wave].wait_send()

    def finish(self):
        p = self.p
        for wave in range(self.waves):
            for k in range(8):
                z, c = p.peer(k)
                for j in range(p.mid - 1):
                    d = p.dp(z, p.other_m(j), c)
                    arrived(self.full.at[d, self.at(wave)], self.r.at[d, wave])
        self.own.wait()
        for copy in self.sends:
            copy.wait_send()


def gather_steps(*gathers, lag=2):
    for g in gathers:
        g.start_own()
    items = [(g, wave) for g in gathers for wave in range(g.waves)]
    for n, (g, wave) in enumerate(items):
        if n >= lag:
            before, old = items[n - lag]
            before.pushed(old)
            before.forward(old)
        g.push(wave)
        yield
    for g, wave in items[max(0, len(items) - lag) :]:
        g.pushed(wave)
        g.forward(wave)
        yield
    for g in gathers:
        g.finish()


def gather_sems(mid, waves):
    return [DMA((8, waves)), DMA((8 * mid, waves)), DMA((8, waves, mid - 1)), DMA]


class Scatter:
    def __init__(self, p, g, own, other, out, sems, waves):
        self.p, self.g, self.own, self.other, self.out, self.waves = p, g, own, other, out, waves
        self.y_s, self.y_r, self.z_s, self.z_r, self.load, self.loc = sems
        self.full_rows = own.shape[1]
        self.rows = self.full_rows // waves
        self.order = list(range(7, -1, -1))
        self.y_sends, self.z_sends, self.loads = {}, [], {}

    def piece(self, d, wave):
        return self.g.at[pl.ds(pl.multiple_of(d * self.full_rows + wave * self.rows, 16), self.rows)]

    def at(self, wave):
        return pl.ds(wave * self.rows, self.rows)

    def start_loads(self):
        p = self.p
        for wave in range(self.waves):
            for k in self.order:
                z, c = p.peer(k)
                copy = pltpu.make_async_copy(
                    self.piece(p.dp(z, p.m, c), wave), self.own.at[k, self.at(wave)], self.load.at[k, wave]
                )
                copy.start()
                self.loads[k, wave] = copy

    def y_send(self, wave):
        p = self.p
        for k in self.order:
            z, c = p.peer(k)
            for j in range(p.mid - 1):
                m = p.other_m(j)
                there = p.mid - 2 - j
                copy = remote(
                    self.piece(p.dp(z, m, c), wave), self.other.at[there, k, self.at(wave)],
                    self.y_s.at[k, wave, j], self.y_r.at[k, wave, there], (p.dp(p.z, m, p.c), p.x),
                )
                copy.start()
                self.y_sends[k, wave, j] = copy

    def z_push(self, wave):
        p = self.p
        at = self.at(wave)
        me = p.z * 2 + p.c
        for k in self.order:
            z, c = p.peer(k)
            for j in range(p.mid - 1):
                arrived(self.other.at[j, k, at], self.y_r.at[k, wave, j])
            self.loads[k, wave].wait()

            def add(i, carry):
                here = pl.ds(pl.multiple_of(wave * self.rows + i * 16, 16), 16)
                total = self.own[k, here, :].astype(F32)
                for j in range(p.mid - 1):
                    total = total + self.other[j, k, here, :].astype(F32)
                self.own[k, here, :] = total.astype(BF16)
                return carry

            lax.fori_loop(0, self.rows // 16, add, 0)
            src, dst = self.own.at[k, at], self.out.at[me, at]
            if k == 0:
                copy = pltpu.make_async_copy(src, dst, self.loc.at[wave])
                copy.start()
                self.z_sends.append((copy, True))
            else:
                copy = remote(src, dst, self.z_s.at[k, wave], self.z_r.at[me, wave], (p.dp(z, p.m, c), p.x))
                copy.start()
                self.z_sends.append((copy, False))

    def y_sent(self, wave):
        for k in self.order:
            for j in range(self.p.mid - 1):
                self.y_sends[k, wave, j].wait_send()

    def finish(self):
        p = self.p
        for wave in range(self.waves):
            for k in range(1, 8):
                z, c = p.peer(k)
                src = z * 2 + c
                arrived(self.out.at[src, self.at(wave)], self.z_r.at[src, wave])
        for copy, here in self.z_sends:
            copy.wait() if here else copy.wait_send()


def scatter_steps(*scatters, lag=2):
    for s in scatters:
        s.start_loads()
    items = [(s, wave) for s in scatters for wave in range(s.waves)]
    for n, (s, wave) in enumerate(items):
        if n >= lag:
            before, old = items[n - lag]
            before.y_sent(old)
        s.y_send(wave)
        if n >= 1:
            before, old = items[n - 1]
            before.z_push(old)
        yield
    s, wave = items[-1]
    s.z_push(wave)
    yield
    for s, wave in items[max(0, len(items) - lag) :]:
        s.y_sent(wave)
    for s in scatters:
        s.finish()


def scatter_scratch(mid, rows, width, waves):
    return [
        pltpu.VMEM((8, rows, width), BF16),
        pltpu.VMEM((mid - 1, 8, rows, width), BF16),
        DMA((8, waves, mid - 1)), DMA((8, waves, mid - 1)), DMA((8, waves)), DMA((8, waves)), DMA((8, waves)),
        DMA((waves,)),
    ]


def waves_of(rows, most):
    return max(w for w in range(1, most + 1) if rows % (16 * w) == 0)


def drive(*streams):
    left = list(streams)
    while left:
        for stream in list(left):
            try:
                next(stream)
            except StopIteration:
                left.remove(stream)


def chain(*streams):
    for stream in streams:
        yield from stream


def all_devices(p):
    return (
        [(p.dp(z, p.m, c), p.x) for z, c in map(p.peer, range(1, 8))]
        + [(p.dp(p.z, p.other_m(j), p.c), p.x) for j in range(p.mid - 1)]
        + [(p.d, 1 - p.x), (p.dp(xor(p.z, 1), p.m, p.c), 1 - p.x)]
    )


def token_steps(p, tok, cot, ids, tokg, cotg, idsg, tok_s, tok_r, ids_s, ids_r, loc):
    half = tok.shape[0] // 2
    seq = p.lo * 2 + p.c
    z_near = (p.dp(xor(p.z, 1), p.m, p.c), p.x)
    c_near = (p.dp(p.z, p.m, 1 - p.c), p.x)
    x_near = (p.d, 1 - p.x)
    mine = pl.ds(pl.multiple_of(p.x * half, 16), half)
    theirs = pl.ds(pl.multiple_of((1 - p.x) * half, 16), half)
    far_seq = (1 - p.lo) * 2 + p.c
    c_seq = p.lo * 2 + 1 - p.c
    cc_seq = (1 - p.lo) * 2 + 1 - p.c
    sends = []

    def go(copy):
        copy.start()
        sends.append(copy)

    here = []
    go(remote(ids, idsg.at[seq], ids_s.at[0], ids_r.at[0], z_near))
    go(remote(ids, idsg.at[seq], ids_s.at[1], ids_r.at[1], c_near))
    for n, (src, dst) in enumerate(((tok, tokg), (cot, cotg))):
        go(remote(src.at[mine], dst.at[seq, mine], tok_s.at[n, 0], tok_r.at[n, 0], z_near))
        go(remote(src, dst.at[seq], tok_s.at[n, 1], tok_r.at[n, 1], c_near))
    for n, (src, dst) in enumerate(((tok, tokg.at[seq]), (cot, cotg.at[seq]), (ids, idsg.at[seq]))):
        copy = pltpu.make_async_copy(src, dst, loc.at[n])
        copy.start()
        here.append(copy)
    yield
    arrived(idsg.at[far_seq], ids_r.at[0])
    go(remote(idsg.at[far_seq], idsg.at[far_seq], ids_s.at[2], ids_r.at[2], c_near))
    for n, dst in enumerate((tokg, cotg)):
        arrived(dst.at[far_seq, mine], tok_r.at[n, 0])
        go(remote(dst.at[far_seq, mine], dst.at[far_seq, mine], tok_s.at[n, 2], tok_r.at[n, 2], x_near))
        go(remote(dst.at[far_seq, mine], dst.at[far_seq, mine], tok_s.at[n, 3], tok_r.at[n, 3], c_near))
        yield
    for n, dst in enumerate((tokg, cotg)):
        arrived(dst.at[far_seq, theirs], tok_r.at[n, 2])
        go(remote(dst.at[far_seq, theirs], dst.at[far_seq, theirs], tok_s.at[n, 4], tok_r.at[n, 4], c_near))
        yield
    arrived(idsg.at[c_seq], ids_r.at[1])
    arrived(idsg.at[cc_seq], ids_r.at[2])
    for n, dst in enumerate((tokg, cotg)):
        arrived(dst.at[c_seq], tok_r.at[n, 1])
        arrived(dst.at[cc_seq, mine], tok_r.at[n, 3])
        arrived(dst.at[cc_seq, theirs], tok_r.at[n, 4])
    for copy in here:
        copy.wait()
    for copy in sends:
        copy.wait_send()


def first_kernel(mid, waves, tok, cot, ids, wa, tokg, cotg, idsg, fa, tok_s, tok_r, ids_s, ids_r, loc, *a_sems):
    p = Place(mid)
    greet(all_devices(p))
    drive(
        token_steps(p, tok, cot, ids, tokg, cotg, idsg, tok_s, tok_r, ids_s, ids_r, loc),
        gather_steps(Gather(p, wa, fa, a_sems, waves)),
    )


def first(mid, tok, cot, ids, wa):
    waves = waves_of(wa.shape[1], 4)
    return pl.pallas_call(
        functools.partial(first_kernel, mid, waves),
        out_shape=(
            jax.ShapeDtypeStruct((4,) + tok.shape, BF16),
            jax.ShapeDtypeStruct((4,) + cot.shape, BF16),
            jax.ShapeDtypeStruct((4,) + ids.shape, ids.dtype),
            jax.ShapeDtypeStruct((8 * mid,) + wa.shape[1:], BF16),
        ),
        in_specs=[ANY] * 4,
        out_specs=(ANY,) * 4,
        scratch_shapes=[DMA((2, 5)), DMA((2, 5)), DMA((3,)), DMA((3,)), DMA((3,))] + gather_sems(mid, waves),
        compiler_params=pltpu.CompilerParams(collective_id=0, has_side_effects=True),
    )(tok, cot, ids, wa)


def group_devices(p):
    far = xor(p.z, 1)
    return {
        (0, 1): (p.d, 1 - p.x),
        (1, 0): (p.dp(far, p.m, p.c), p.x),
        (1, 1): (p.dp(far, p.m, p.c), 1 - p.x),
    }, (p.dp(p.z, p.m, 1 - p.c), p.x)


def reduce_steps(p, part, scratch, finish):
    abuf, sums, bbuf, a_s, a_r, b_s, b_r = scratch
    chips, sibling = group_devices(p)
    order = ((1, 1), (0, 1), (1, 0), (0, 0))
    sends = []
    for n, (fz, fx) in enumerate(order):
        lo, x = xor(p.lo, fz), xor(p.x, fx)
        copy = remote(part.at[(lo * 2 + 1 - p.c) * 2 + x], abuf.at[n], a_s.at[n], a_r.at[n], sibling)
        copy.start()
        sends.append(copy)
    yield
    rows = part.shape[1]
    step = 16
    for n, (fz, fx) in enumerate(order):
        lo, x = xor(p.lo, fz), xor(p.x, fx)
        own = (lo * 2 + p.c) * 2 + x
        arrived(abuf.at[n], a_r.at[n])
        if n == 3:
            break

        def add(i, carry):
            at = pl.ds(pl.multiple_of(i * step, step), step)
            sums[n, at, :] = (part[own, at, :].astype(F32) + abuf[n, at, :].astype(F32)).astype(BF16)
            return carry

        lax.fori_loop(0, rows // step, add, 0)
        copy = remote(sums.at[n], bbuf.at[n], b_s.at[n], b_r.at[n], chips[(fz, fx)])
        copy.start()
        sends.append(copy)
    yield
    yield
    mine = (p.lo * 2 + p.c) * 2 + p.x
    for n in range(3):
        arrived(bbuf.at[n], b_r.at[n])

    def last(i, carry):
        at = pl.ds(pl.multiple_of(i * step, step), step)
        total = part[mine, at, :].astype(F32) + abuf[3, at, :].astype(F32)
        for n in range(3):
            total = total + bbuf[n, at, :].astype(F32)
        finish(at, total)
        return carry

    lax.fori_loop(0, rows // step, last, 0)
    for copy in sends:
        copy.wait_send()


def share_steps(p, gathered, s, r):
    chips, sibling = group_devices(p)
    mine = (p.lo * 2 + p.c) * 2 + p.x
    order = ((1, 1), (0, 1), (1, 0))
    sends = []
    for n, flips in enumerate(order):
        copy = remote(gathered.at[mine], gathered.at[mine], s.at[n], r.at[n], chips[flips])
        copy.start()
        sends.append(copy)
    copy = remote(gathered.at[mine], gathered.at[mine], s.at[3], r.at[3], sibling)
    copy.start()
    sends.append(copy)
    yield
    yield
    for n, (fz, fx) in enumerate(order):
        at = (xor(p.lo, fz) * 2 + p.c) * 2 + xor(p.x, fx)
        arrived(gathered.at[at], r.at[n])
        copy = remote(gathered.at[at], gathered.at[at], s.at[4 + n], r.at[4 + n], sibling)
        copy.start()
        sends.append(copy)
    yield
    for n, (fz, fx) in enumerate(order + ((0, 0),)):
        at = (xor(p.lo, fz) * 2 + 1 - p.c) * 2 + xor(p.x, fx)
        number = 3 if n == 3 else 4 + n
        arrived(gathered.at[at], r.at[number])
    for copy in sends:
        copy.wait_send()


def swap_steps(p, both, o_s, o_r):
    rows = both.shape[0] // 2
    half = pl.ds(pl.multiple_of(p.x * rows, 16), rows)
    copy = remote(both.at[half], both.at[half], o_s, o_r, (p.d, 1 - p.x))
    copy.start()
    yield
    copy.wait()


def norm_root(value):
    return lax.rsqrt(jnp.mean(value * value, axis=-1, keepdims=True) + EPSILON)


def norm_back(value, scaled):
    root = norm_root(value)
    return root * scaled - value * root**3 * jnp.mean(value * scaled, axis=-1, keepdims=True)


def second_kernel(mid, waves, part, x, wm, hidden, normed, fm, *scratch):
    p = Place(mid)
    greet(all_devices(p))
    mine = (p.lo * 2 + p.c) * 2 + p.x

    def finish(at, total):
        value = x[at, :].astype(F32) + total
        hidden[at, :] = value
        normed[mine, at, :] = (value * norm_root(value)).astype(BF16)

    drive(
        chain(reduce_steps(p, part, scratch[:7], finish), share_steps(p, normed, scratch[7], scratch[8])),
        gather_steps(Gather(p, wm, fm, scratch[9:], waves)),
    )


def reduce_scratch(rows, width):
    return [
        pltpu.VMEM((4, rows, width), BF16),
        pltpu.VMEM((3, rows, width), BF16),
        pltpu.VMEM((3, rows, width), BF16),
        DMA((4,)), DMA((4,)), DMA((3,)), DMA((3,)),
    ]


def second(mid, part, x, wm):
    eight, rows, width = part.shape
    waves = waves_of(wm.shape[1], 8)
    return pl.pallas_call(
        functools.partial(second_kernel, mid, waves),
        out_shape=(
            jax.ShapeDtypeStruct((rows, width), F32),
            jax.ShapeDtypeStruct((eight, rows, width), BF16),
            jax.ShapeDtypeStruct((8 * mid,) + wm.shape[1:], BF16),
        ),
        in_specs=[VMEM] * 2 + [ANY],
        out_specs=(VMEM, VMEM, ANY),
        scratch_shapes=reduce_scratch(rows, width) + [DMA((7,)), DMA((7,))] + gather_sems(mid, waves),
        compiler_params=pltpu.CompilerParams(
            collective_id=1, has_side_effects=True, vmem_limit_bytes=56 << 20
        ),
    )(part, x, wm)


def third_kernel(
    mid, waves, part, out_part, hid, cot, gu, down, grad_hidden, low, output, gu_out, down_out, *scratch
):
    p = Place(mid)
    greet(all_devices(p))
    mine = (p.lo * 2 + p.c) * 2 + p.x
    rows = hid.shape[0]

    def finish(at, total):
        grads = cot[at, :].astype(F32) + norm_back(hid[at, :], total)
        grad_hidden[at, :] = grads
        low[mine, at, :] = grads.astype(BF16)

    def finish_out(at, total):
        there = pl.ds(pl.multiple_of(p.x * rows + at.start, 16), 16)
        output[there, :] = (hid[at, :] + total).astype(BF16)

    r1, r2 = scratch[:7], scratch[7:14]
    g_s, g_r, o_s, o_r = scratch[14:18]
    gu_s, down_s = scratch[18:26], scratch[26:34]
    drive(
        chain(
            reduce_steps(p, part, r1, finish),
            share_steps(p, low, g_s, g_r),
            reduce_steps(p, out_part, r2, finish_out),
            swap_steps(p, output, o_s, o_r),
        ),
        scatter_steps(
            Scatter(p, down, down_s[0], down_s[1], down_out, down_s[2:], waves),
            Scatter(p, gu, gu_s[0], gu_s[1], gu_out, gu_s[2:], waves),
        ),
    )


def third(mid, part, out_part, hid, cot, gu, down):
    eight, rows, width = part.shape
    n = 8 * mid
    w_rows = gu.shape[0] // n
    waves = waves_of(w_rows, 4)
    return pl.pallas_call(
        functools.partial(third_kernel, mid, waves),
        out_shape=(
            jax.ShapeDtypeStruct((rows, width), F32),
            jax.ShapeDtypeStruct((eight, rows, width), BF16),
            jax.ShapeDtypeStruct((2 * rows, width), BF16),
            jax.ShapeDtypeStruct((8, w_rows, gu.shape[1]), BF16),
            jax.ShapeDtypeStruct((8, w_rows, down.shape[1]), BF16),
        ),
        in_specs=[VMEM] * 4 + [ANY] * 2,
        out_specs=(VMEM,) * 3 + (ANY,) * 2,
        scratch_shapes=reduce_scratch(rows, width) * 2
        + [DMA((7,)), DMA((7,)), DMA, DMA]
        + scatter_scratch(mid, w_rows, gu.shape[1], waves)
        + scatter_scratch(mid, w_rows, down.shape[1], waves),
        compiler_params=pltpu.CompilerParams(
            collective_id=2, has_side_effects=True, vmem_limit_bytes=60 << 20
        ),
    )(part, out_part, hid, cot, gu, down)


def fourth_kernel(mid, waves, part, grad_hidden, x, ga, result, ga_out, *scratch):
    p = Place(mid)
    greet(all_devices(p))
    rows = x.shape[0]

    def finish(at, total):
        there = pl.ds(pl.multiple_of(p.x * rows + at.start, 16), 16)
        value = x[at, :].astype(F32)
        result[there, :] = (grad_hidden[at, :] + norm_back(value, total)).astype(BF16)

    own = scratch[9:]
    drive(
        chain(reduce_steps(p, part, scratch[:7], finish), swap_steps(p, result, scratch[7], scratch[8])),
        scatter_steps(Scatter(p, ga, own[0], own[1], ga_out, own[2:], waves)),
    )


def fourth(mid, part, grad_hidden, x, ga):
    eight, rows, width = part.shape
    w_rows = ga.shape[0] // (8 * mid)
    waves = waves_of(w_rows, 4)
    return pl.pallas_call(
        functools.partial(fourth_kernel, mid, waves),
        out_shape=(
            jax.ShapeDtypeStruct((2 * rows, width), BF16),
            jax.ShapeDtypeStruct((8, w_rows, ga.shape[1]), BF16),
        ),
        in_specs=[VMEM] * 3 + [ANY],
        out_specs=(VMEM, ANY),
        scratch_shapes=reduce_scratch(rows, width)
        + [DMA, DMA]
        + scatter_scratch(mid, w_rows, ga.shape[1], waves),
        compiler_params=pltpu.CompilerParams(
            collective_id=3, has_side_effects=True, vmem_limit_bytes=56 << 20
        ),
    )(part, grad_hidden, x, ga)


def positions(segments):
    length = segments.shape[1]
    places = jnp.arange(length, dtype=jnp.int32)[None, :]
    earlier = jnp.concatenate([segments[:, :1], segments[:, :-1]], axis=1)
    begins = jnp.where((segments != earlier) | (places == 0), places, jnp.zeros_like(places))
    before = places[0][:, None] >= places[0][None, :]
    return places - jnp.max(jnp.where(before[None], begins[:, None, :], 0), axis=-1)


def rotary(position):
    halves = HEAD_DIM // 2
    inverse = THETA ** (-2.0 * jnp.arange(halves, dtype=jnp.float32) / HEAD_DIM)
    angles = position.astype(jnp.float32)[..., None] * inverse
    return (jnp.cos(angles), jnp.sin(angles))


def rotate(values, cosine, sine_table):
    halves = values.shape[-1] // 2
    front_half = values[..., :halves]
    back_half = values[..., halves:]
    cos_wide = cosine[..., None, :]
    sin_wide = sine_table[..., None, :]
    return jnp.concatenate(
        [
            front_half * cos_wide - back_half * sin_wide,
            back_half * cos_wide + front_half * sin_wide,
        ],
        axis=-1,
    )


def dot(a, b, dims):
    return lax.dot_general(a, b, (dims, ((), ())), preferred_element_type=F32)


def local(
    mid, tokens, attn_gain, w_query, w_key, w_value, w_out, mlp_gain, w_gate, w_up, w_down, segment_ids, cotangent
):
    length, width = tokens.shape
    half = length // 2
    rows = w_query.shape[0]
    x_at = lax.axis_index("tensor")

    def blocks(w):
        return w.reshape(rows, 4, w.shape[1] // 4).transpose(1, 0, 2)

    gain_one, gain_two = attn_gain.astype(F32)[:, None], mlp_gain.astype(F32)[:, None]

    def scaled(w, gain):
        return blocks((w.astype(F32) * gain).astype(BF16))

    wm = jnp.concatenate([scaled(w_gate, gain_two), scaled(w_up, gain_two), blocks(w_down.T)], axis=-1)
    wa = jnp.concatenate(
        [scaled(w_query, gain_one), scaled(w_key, gain_one), scaled(w_value, gain_one), blocks(w_out.T)], axis=-1
    )
    ids = jnp.broadcast_to(segment_ids.reshape(1, length), (8, length))
    tokg, cotg, idsg, fa = first(mid, tokens, cotangent, ids, wa)
    fa = fa.reshape(width, -1)
    units = w_gate.shape[1] // 4
    qw, kw = w_query.shape[1] // 4, w_key.shape[1] // 4
    heads = qw // HEAD_DIM
    qkv_w, out_t = fa[:, : qw + 2 * kw], fa[:, qw + 2 * kw :]

    segments = idsg[:, 0, :]
    cosine, sine = rotary(positions(segments))
    xs = tokg.reshape(4 * length, width)
    inputs = xs.astype(F32)
    root_one = lax.rsqrt(jnp.mean(inputs * inputs, axis=-1, keepdims=True) + EPSILON)
    normed = (inputs * root_one).astype(BF16)
    qkv = dot(normed, qkv_w, ((1,), (0,)))
    q = rotate(qkv[:, :qw].reshape(4, length, heads, HEAD_DIM), cosine, sine).astype(BF16)
    k = rotate(qkv[:, qw : qw + kw].reshape(4, length, 1, HEAD_DIM), cosine, sine).astype(BF16)[:, :, 0]
    v = qkv[:, qw + kw :].reshape(4, length, HEAD_DIM).astype(BF16)
    places = jnp.arange(length)
    allowed = (segments[:, :, None] == segments[:, None, :]) & (places[None, :, None] >= places[None, None, :])
    scaling = HEAD_DIM ** (-0.5)
    scores = jnp.einsum("sqgd,spd->sgqp", q, k, preferred_element_type=F32) * scaling
    scores = jnp.where(allowed[:, None], scores, -1e30)
    highest = jnp.max(scores, axis=-1, keepdims=True)
    exponent = jnp.exp(scores - highest)
    probs = exponent / jnp.sum(exponent, axis=-1, keepdims=True)
    probs_low = probs.astype(BF16)
    mixture = jnp.einsum("sgqp,spd->sqgd", probs_low, v, preferred_element_type=F32)
    mixture = mixture.astype(BF16).reshape(4 * length, qw)
    attn_part = dot(mixture, out_t, ((1,), (1,))).astype(BF16)
    own_x = lax.dynamic_slice_in_dim(tokens, x_at * half, half, 0)
    own_cot = lax.dynamic_slice_in_dim(cotangent, x_at * half, half, 0)
    hidden, n2, fm = second(mid, attn_part.reshape(8, half, width), own_x, wm)
    n2 = n2.reshape(4 * length, width)
    fm = fm.reshape(width, -1)
    gate_w, up_w, down_t = fm[:, :units], fm[:, units : 2 * units], fm[:, 2 * units :]

    gate = dot(n2, gate_w, ((1,), (0,)))
    up = dot(n2, up_w, ((1,), (0,)))
    sigmoid = 1.0 / (1.0 + jnp.exp(-gate))
    silu = gate / (1.0 + jnp.exp(-gate))
    activated = (silu * up).astype(BF16)
    out_part = dot(activated, down_t, ((1,), (1,))).astype(BF16)
    cots = cotg.reshape(4 * length, width)
    grad_act = dot(cots, down_t, ((1,), (0,)))
    grad_gate = (grad_act * up * sigmoid * (1.0 + gate * (1.0 - sigmoid))).astype(BF16)
    grad_up = (grad_act * silu).astype(BF16)
    grad_gu = jnp.concatenate([grad_gate, grad_up], axis=1)
    part_two = dot(grad_gu, fm[:, : 2 * units], ((1,), (1,))).astype(BF16)
    down_g = dot(cots, activated, ((0,), (0,))).astype(BF16)
    gu_g = dot(n2, grad_gu, ((0,), (0,))).astype(BF16)

    grad_hidden, ghl, output, gu_parts, down_parts = third(
        mid, part_two.reshape(8, half, width), out_part.reshape(8, half, width), hidden, own_cot, gu_g, down_g
    )
    ghl = ghl.reshape(4 * length, width)
    grad_mix = dot(ghl, out_t, ((1,), (0,))).astype(BF16)
    gm = grad_mix.reshape(4, length, heads, HEAD_DIM)
    out_g = dot(ghl, mixture, ((0,), (0,))).astype(BF16)
    grad_probs = jnp.einsum("sqgd,spd->sgqp", gm, v, preferred_element_type=F32)
    grad_v = jnp.einsum("sgqp,sqgd->spd", probs_low, gm, preferred_element_type=F32).astype(BF16)
    centered = jnp.sum(probs * grad_probs, axis=-1, keepdims=True)
    gs = (probs * (grad_probs - centered)).astype(BF16)
    gq_rot = jnp.einsum("sgqp,spd->sqgd", gs, k, preferred_element_type=F32) * scaling
    gk_rot = jnp.einsum("sgqp,sqgd->spd", gs, q, preferred_element_type=F32) * scaling
    gq = rotate(gq_rot, cosine, -sine).astype(BF16).reshape(4 * length, qw)
    gk = rotate(gk_rot[:, :, None], cosine, -sine).astype(BF16).reshape(4 * length, kw)
    gqkv = jnp.concatenate([gq, gk, grad_v.reshape(4 * length, kw)], axis=1)
    part_one = dot(gqkv, qkv_w, ((1,), (1,))).astype(BF16)
    qkv_g = dot(normed, gqkv, ((0,), (0,))).astype(BF16)
    grads = jnp.concatenate([qkv_g, out_g], axis=1)
    input_grad, a_parts = fourth(mid, part_one.reshape(8, half, width), grad_hidden, own_x, grads)

    def total(parts):
        parts = parts.reshape(2, 4, rows, -1).astype(F32)
        return parts[0] + parts[1]

    def across(block):
        return block.transpose(1, 0, 2).reshape(rows, -1)

    def down(block):
        return block.transpose(0, 2, 1).reshape(-1, rows)

    t_gate, t_up = jnp.split(total(gu_parts), 2, axis=-1)
    t_q, t_k, t_v, t_out = jnp.split(total(a_parts), [qw, qw + kw, qw + 2 * kw], axis=-1)
    t_gate, t_up, t_q, t_k, t_v = (across(t) for t in (t_gate, t_up, t_q, t_k, t_v))

    def gain_grad(*pairs):
        return sum(jnp.sum(w.astype(F32) * g, axis=1) for w, g in pairs)

    gain_grads = jnp.stack(
        [gain_grad((w_query, t_q), (w_key, t_k), (w_value, t_v)), gain_grad((w_gate, t_gate), (w_up, t_up))]
    )
    gain_grads = lax.psum(gain_grads, "tensor")
    return (
        output,
        input_grad.astype(F32),
        gain_grads[0],
        t_q * gain_one,
        t_k * gain_one,
        t_v * gain_one,
        down(t_out),
        gain_grads[1],
        t_gate * gain_two,
        t_up * gain_two,
        down(total(down_parts)),
    )


def solution(mesh):
    in_specs = (
        P("dp", None), P("dp"), P("dp", "tensor"), P("dp", "tensor"), P("dp", "tensor"), P("tensor", "dp"),
        P("dp"), P("dp", "tensor"), P("dp", "tensor"), P("tensor", "dp"), P("dp"), P("dp", None),
    )
    out_specs = (
        P("dp", None), P("dp", None), P("dp"), P("dp", "tensor"), P("dp", "tensor"), P("dp", "tensor"),
        P("tensor", "dp"), P("dp"), P("dp", "tensor"), P("dp", "tensor"), P("tensor", "dp"),
    )
    return jax.shard_map(
        functools.partial(local, mesh.shape["dp"] // 8),
        mesh=mesh, in_specs=in_specs, out_specs=out_specs, check_vma=False,
    )
```

```python
import functools

import jax
import jax.numpy as jnp
from jax import lax
from jax.experimental import pallas as pl
from jax.experimental.pallas import tpu as pltpu
from jax.sharding import PartitionSpec as P

HEAD_DIM = 64
EPSILON = 1e-05
THETA = 500000.0
MESH = pl.DeviceIdType.MESH
ANY = pl.BlockSpec(memory_space=pl.ANY)
VMEM = pl.BlockSpec(memory_space=pltpu.VMEM)
F32 = jnp.float32
BF16 = jnp.bfloat16
DMA = pltpu.SemaphoreType.DMA
COT_AT = 7
OUT_AT = 4


class Place:
    def __init__(self, mid):
        self.mid = mid
        self.d = lax.axis_index("dp")
        self.x = lax.axis_index("tensor")
        self.c = self.d % 2
        self.m = (self.d // 2) % mid
        self.z = self.d // (2 * mid)
        self.lo = self.z % 2

    def dp(self, z, m, c):
        return (z * self.mid + m) * 2 + c

    def peer(self, k):
        return xor(self.z, k // 2), xor(self.c, k % 2)

    def other_m(self, j):
        return (self.m + 1 + j) % self.mid


def xor(a, k):
    if k == 0:
        return a
    low = a % 2
    high = a // 2
    if k % 2:
        low = 1 - low
    if k // 2:
        high = 1 - high
    return high * 2 + low


def remote(src, dst, send, recv, device):
    copy = pltpu.make_async_remote_copy(
        src_ref=src, dst_ref=dst, send_sem=send, recv_sem=recv, device_id=device, device_id_type=MESH
    )
    return copy


def greet(devices):
    barrier = pltpu.get_barrier_semaphore()
    for device in devices:
        pl.semaphore_signal(barrier, inc=1, device_id=device, device_id_type=MESH)
    pl.semaphore_wait(barrier, len(devices))


def arrived(dst, sem):
    pltpu.make_async_copy(dst, dst, sem).wait()


class Gather:
    def __init__(self, p, w, full, sems, waves):
        self.p, self.w, self.full, self.waves = p, w, full, waves
        self.z_s, self.r, self.f_s, self.loc = sems
        self.rows = w.shape[1] // waves
        self.block = p.lo * 2 + p.c
        self.order = list(range(7, 0, -1))
        self.pushes, self.sends = {}, []

    def at(self, wave):
        return pl.ds(wave * self.rows, self.rows)

    def there(self, d, wave):
        return self.full.at[pl.ds(pl.multiple_of(d * self.w.shape[1] + wave * self.rows, 16), self.rows)]

    def push(self, wave):
        p, at = self.p, self.at(wave)
        for k in self.order:
            z, c = p.peer(k)
            copy = remote(
                self.w.at[(z % 2) * 2 + c, at], self.there(p.d, wave), self.z_s.at[k, wave], self.r.at[p.d, wave],
                (p.dp(z, p.m, c), p.x),
            )
            copy.start()
            self.pushes[k, wave] = copy
        self.forward_one(self.w.at[self.block, at], p.d, wave, 0)

    def forward_one(self, src, d, wave, k):
        p = self.p
        for j in range(p.mid - 1):
            copy = remote(
                src, self.there(d, wave), self.f_s.at[k, wave, j], self.r.at[d, wave],
                (p.dp(p.z, p.other_m(j), p.c), p.x),
            )
            copy.start()
            self.sends.append(copy)

    def forward(self, wave):
        p = self.p
        for k in self.order:
            z, c = p.peer(k)
            d = p.dp(z, p.m, c)
            here = self.there(d, wave)
            arrived(here, self.r.at[d, wave])
            self.forward_one(here, d, wave, k)
        if wave == self.waves - 1:
            self.all_forwarded = True

    def start_own(self):
        self.all_forwarded = False
        rows = self.w.shape[1]
        at = pl.ds(pl.multiple_of(self.p.d * rows, 16), rows)
        self.own = pltpu.make_async_copy(self.w.at[self.block], self.full.at[at], self.loc)
        self.own.start()

    def pushed(self, wave):
        for k in self.order:
            self.pushes[k, wave].wait_send()

    def landed(self):
        p = self.p
        for wave in range(self.waves):
            for k in range(8):
                z, c = p.peer(k)
                for j in range(p.mid - 1):
                    d = p.dp(z, p.other_m(j), c)
                    arrived(self.there(d, wave), self.r.at[d, wave])
        self.own.wait()
        self.done = True

    def finish(self):
        if not getattr(self, "done", False):
            self.landed()
        for copy in self.sends:
            copy.wait_send()


def gather_steps(*gathers, lag=2):
    for g in gathers:
        g.start_own()
    items = [(g, wave) for g in gathers for wave in range(g.waves)]
    for n, (g, wave) in enumerate(items):
        if n >= lag:
            before, old = items[n - lag]
            before.pushed(old)
            before.forward(old)
        g.push(wave)
        yield
    for g, wave in items[max(0, len(items) - lag) :]:
        g.pushed(wave)
        g.forward(wave)
        yield
    for g in gathers:
        g.finish()


def gather_sems(mid, waves):
    return [DMA((8, waves)), DMA((8 * mid, waves)), DMA((8, waves, mid - 1)), DMA]


class Scatter:
    def __init__(self, p, g, own, other, out, sems, waves):
        self.p, self.g, self.own, self.other, self.out, self.waves = p, g, own, other, out, waves
        self.y_s, self.y_r, self.z_s, self.z_r, self.load, self.loc = sems
        self.full_rows = own.shape[1]
        self.rows = self.full_rows // waves
        self.order = list(range(7, -1, -1))
        self.y_sends, self.z_sends, self.loads = {}, [], {}
        self.ready = True

    def piece(self, d, wave):
        return self.g.at[pl.ds(pl.multiple_of(d * self.full_rows + wave * self.rows, 16), self.rows)]

    def at(self, wave):
        return pl.ds(wave * self.rows, self.rows)

    def start_loads(self):
        p = self.p
        for wave in range(self.waves):
            for k in self.order:
                z, c = p.peer(k)
                copy = pltpu.make_async_copy(
                    self.piece(p.dp(z, p.m, c), wave), self.own.at[k, self.at(wave)], self.load.at[k, wave]
                )
                copy.start()
                self.loads[k, wave] = copy

    def y_send(self, wave):
        p = self.p
        for k in self.order:
            z, c = p.peer(k)
            for j in range(p.mid - 1):
                m = p.other_m(j)
                there = p.mid - 2 - j
                copy = remote(
                    self.piece(p.dp(z, m, c), wave), self.other.at[there, k, self.at(wave)],
                    self.y_s.at[k, wave, j], self.y_r.at[k, wave, there], (p.dp(p.z, m, p.c), p.x),
                )
                copy.start()
                self.y_sends[k, wave, j] = copy

    def z_push(self, wave):
        p = self.p
        at = self.at(wave)
        me = p.z * 2 + p.c
        for k in self.order:
            z, c = p.peer(k)
            for j in range(p.mid - 1):
                arrived(self.other.at[j, k, at], self.y_r.at[k, wave, j])
            self.loads[k, wave].wait()

            def add(i, carry):
                here = pl.ds(pl.multiple_of(wave * self.rows + i * 16, 16), 16)
                total = self.own[k, here, :].astype(F32)
                for j in range(p.mid - 1):
                    total = total + self.other[j, k, here, :].astype(F32)
                self.own[k, here, :] = total.astype(BF16)
                return carry

            lax.fori_loop(0, self.rows // 16, add, 0)
            src, dst = self.own.at[k, at], self.out.at[me, at]
            if k == 0:
                copy = pltpu.make_async_copy(src, dst, self.loc.at[wave])
                copy.start()
                self.z_sends.append((copy, True))
            else:
                copy = remote(src, dst, self.z_s.at[k, wave], self.z_r.at[me, wave], (p.dp(z, p.m, c), p.x))
                copy.start()
                self.z_sends.append((copy, False))

    def y_sent(self, wave):
        for k in self.order:
            for j in range(self.p.mid - 1):
                self.y_sends[k, wave, j].wait_send()

    def finish(self):
        p = self.p
        for wave in range(self.waves):
            for k in range(1, 8):
                z, c = p.peer(k)
                src = z * 2 + c
                arrived(self.out.at[src, self.at(wave)], self.z_r.at[src, wave])
        for copy, here in self.z_sends:
            copy.wait() if here else copy.wait_send()


def scatter_steps(*scatters, lag=2):
    items = [(s, wave) for s in scatters for wave in range(s.waves)]
    pushed = 0
    for n, (s, wave) in enumerate(items):
        if not s.ready:
            while pushed < n:
                before, old = items[pushed]
                before.z_push(old)
                pushed += 1
            while not s.ready:
                yield
        if wave == 0:
            s.start_loads()
        if n >= lag:
            before, old = items[n - lag]
            before.y_sent(old)
        s.y_send(wave)
        while pushed < n:
            before, old = items[pushed]
            before.z_push(old)
            pushed += 1
        yield
    s, wave = items[-1]
    s.z_push(wave)
    yield
    for s, wave in items[max(0, len(items) - lag) :]:
        s.y_sent(wave)
    for s in scatters:
        s.finish()


def scatter_scratch(mid, rows, width, waves):
    return [
        pltpu.VMEM((8, rows, width), BF16),
        pltpu.VMEM((mid - 1, 8, rows, width), BF16),
        DMA((8, waves, mid - 1)), DMA((8, waves, mid - 1)), DMA((8, waves)), DMA((8, waves)), DMA((8, waves)),
        DMA((waves,)),
    ]


def waves_of(rows, most):
    return max(w for w in range(1, most + 1) if rows % (16 * w) == 0)


def drive(*streams):
    left = list(streams)
    while left:
        for stream in list(left):
            try:
                next(stream)
            except StopIteration:
                left.remove(stream)


def after(steps, stream):
    for _ in range(steps):
        yield
    yield from stream


def chain(*streams):
    for stream in streams:
        yield from stream


def all_devices(p):
    return (
        [(p.dp(z, p.m, c), p.x) for z, c in map(p.peer, range(1, 8))]
        + [(p.dp(p.z, p.other_m(j), p.c), p.x) for j in range(p.mid - 1)]
        + [(p.d, 1 - p.x)]
    )


def token_steps(p, tok, tokg, t_s, t_r, loc, whole):
    rows = tok.shape[0]
    half = rows // 2
    seq = p.lo * 2 + p.c
    z_near = (p.dp(xor(p.z, 1), p.m, p.c), p.x)
    c_near = (p.dp(p.z, p.m, 1 - p.c), p.x)
    x_near = (p.d, 1 - p.x)
    mine = pl.ds(pl.multiple_of(p.x * half, 16), half)
    theirs = pl.ds(pl.multiple_of((1 - p.x) * half, 16), half)
    if whole:
        mine = pl.ds(0, rows)
    far_seq = (1 - p.lo) * 2 + p.c
    c_seq = p.lo * 2 + 1 - p.c
    cc_seq = (1 - p.lo) * 2 + 1 - p.c
    sends = []

    def go(copy):
        copy.start()
        sends.append(copy)

    go(remote(tok.at[mine], tokg.at[seq, mine], t_s.at[0], t_r.at[0], z_near))
    go(remote(tok, tokg.at[seq], t_s.at[1], t_r.at[1], c_near))
    here = pltpu.make_async_copy(tok, tokg.at[seq], loc)
    here.start()
    yield
    arrived(tokg.at[far_seq, mine], t_r.at[0])
    if not whole:
        go(remote(tokg.at[far_seq, mine], tokg.at[far_seq, mine], t_s.at[2], t_r.at[2], x_near))
    go(remote(tokg.at[far_seq, mine], tokg.at[far_seq, mine], t_s.at[3], t_r.at[3], c_near))
    yield
    if not whole:
        arrived(tokg.at[far_seq, theirs], t_r.at[2])
        go(remote(tokg.at[far_seq, theirs], tokg.at[far_seq, theirs], t_s.at[4], t_r.at[4], c_near))
        yield
    here.wait()
    arrived(tokg.at[c_seq], t_r.at[1])
    arrived(tokg.at[cc_seq, mine], t_r.at[3])
    if not whole:
        arrived(tokg.at[cc_seq, theirs], t_r.at[4])
    for copy in sends:
        copy.wait_send()


def token_sems():
    return [DMA((5,)), DMA((5,)), DMA]


def lanes_of(shape):
    return lax.broadcasted_iota(jnp.int32, shape, 1)


def wide_tables(table):
    lanes = lanes_of(table.shape)
    half = HEAD_DIM // 2
    cosine = jnp.where(lanes < half, table, 0.0)
    sine = pltpu.roll(jnp.where((lanes >= half) & (lanes < 2 * half), table, 0.0), 128 - half, 1)
    spread = cosine + pltpu.roll(cosine, half, 1)
    spread = spread + pltpu.roll(spread, 2 * half, 1)
    signed = pltpu.roll(sine, half, 1) - sine
    signed = signed + pltpu.roll(signed, 2 * half, 1)
    return spread, signed


def turn(values, cosine, signed):
    half = HEAD_DIM // 2
    lanes = lanes_of(values.shape) % HEAD_DIM
    swapped = jnp.where(lanes < half, pltpu.roll(values, 128 - half, 1), pltpu.roll(values, half, 1))
    return values * cosine + swapped * signed


def attention_steps(p, tokg, tabg, fa, n1, qkv, probs, mixture, part, gather_a):
    length = tokg.shape[1]
    qw = mixture.shape[1]
    heads = qw // HEAD_DIM
    scaling = HEAD_DIM ** (-0.5)
    for s in range(4):

        def norm(i, carry):
            at = pl.ds(pl.multiple_of(i * 32, 32), 32)
            value = tokg[s, at, :].astype(F32)
            n1[pl.ds(pl.multiple_of(s * length + i * 32, 32), 32), :] = (value * norm_root(value)).astype(BF16)
            return carry

        lax.fori_loop(0, length // 32, norm, 0)
    yield
    while not gather_a.all_forwarded:
        yield
    gather_a.landed()
    for s in range(4):
        here = pl.ds(s * length, length)
        table = tabg[s]
        cosine, signed = wide_tables(table)
        pre = dot(n1[here, :], fa[:, : qw + 128], ((1,), (0,)))
        for b in range(qw // 128):
            at = slice(128 * b, 128 * b + 128)
            qkv[here, at] = turn(pre[:, at], cosine, signed).astype(BF16)
        last = pre[:, qw:]
        keys = turn(last, cosine, signed)
        lanes = lanes_of(last.shape)
        qkv[here, qw:] = jnp.where(lanes < HEAD_DIM, keys, last).astype(BF16)
        key = qkv[here, qw : qw + HEAD_DIM]
        value = qkv[here, qw + HEAD_DIM :]
        begin = table[:, 2 * HEAD_DIM // 2 : 2 * HEAD_DIM // 2 + 1]
        columns = lanes_of((length, length))
        allowed = (columns.astype(F32) >= begin) & (
            columns <= lax.broadcasted_iota(jnp.int32, (length, length), 0)
        )
        for h in range(heads):
            at = slice(HEAD_DIM * h, HEAD_DIM * h + HEAD_DIM)
            scores = dot(qkv[here, at], key, ((1,), (1,))) * scaling
            scores = jnp.where(allowed, scores, -1e30)
            exponent = jnp.exp(scores - jnp.max(scores, axis=-1, keepdims=True))
            share = exponent / jnp.sum(exponent, axis=-1, keepdims=True)
            probs[s, h] = share
            mixture[here, at] = dot(share.astype(BF16), value, ((1,), (0,))).astype(BF16)
        half = length // 2
        for x in range(2):
            rows = pl.ds(s * length + x * half, half)
            part[s * 2 + x] = dot(mixture[rows, :], fa[:, qw + 128 :], ((1,), (1,))).astype(BF16)
        yield


def first_kernel(
    mid, a_waves, waves, tok, cot, table, wa, wg, wu, wd,
    cotg, tabg, fa, fg, fu, fd, n1, qkv, probs, mixture, hidden, n2, *scratch
):
    p = Place(mid)
    scratch = list(scratch)

    def take(count):
        taken = scratch[:count]
        del scratch[:count]
        return taken

    tokg, part = take(2)
    tok_sems, cot_sems, tab_sems = take(3), take(3), take(3)
    reduce_refs, share_refs = take(10), take(2)
    greet(all_devices(p))
    gather_a = Gather(p, wa, fa, take(4), a_waves)
    rest = [Gather(p, w, f, take(4), waves) for w, f in ((wg, fg), (wu, fu), (wd, fd))]
    seq = p.lo * 2 + p.c
    mine = seq * 2 + p.x
    half = hidden.shape[0]

    def finish(at, total):
        there = pl.ds(pl.multiple_of(p.x * half + at.start, 16), 16)
        value = tokg[seq, there, :].astype(F32) + total
        hidden[at, :] = value
        n2[mine, at, :] = (value * norm_root(value)).astype(BF16)

    tab = token_steps(p, table, tabg, *tab_sems, whole=True)
    tokens = token_steps(p, tok, tokg, *tok_sems, whole=False)
    next(tokens)
    next(tab)
    drive(
        gather_steps(gather_a, *rest),
        chain(
            tokens,
            attention_steps(p, tokg, tabg, fa, n1, qkv, probs, mixture, part, gather_a),
            reduce_steps(p, part, reduce_refs, finish),
            share_steps(p, n2, *share_refs),
        ),
        tab,
        after(COT_AT, token_steps(p, cot, cotg, *cot_sems, whole=False)),
    )


def first(mid, tok, cot, table, wa, wg, wu, wd, qw):
    a_waves, waves = waves_of(wa.shape[1], 4), waves_of(wg.shape[1], 4)
    length, width = tok.shape
    n = 8 * mid
    heads = qw // HEAD_DIM

    def full(w):
        return jax.ShapeDtypeStruct((n * w.shape[1], w.shape[2]), BF16)

    return pl.pallas_call(
        functools.partial(first_kernel, mid, a_waves, waves),
        out_shape=(
            jax.ShapeDtypeStruct((4,) + cot.shape, BF16),
            jax.ShapeDtypeStruct((4,) + table.shape, F32),
            full(wa), full(wg), full(wu), full(wd),
            jax.ShapeDtypeStruct((4 * length, width), BF16),
            jax.ShapeDtypeStruct((4 * length, qw + 128), BF16),
            jax.ShapeDtypeStruct((4, heads, length, length), F32),
            jax.ShapeDtypeStruct((4 * length, qw), BF16),
            jax.ShapeDtypeStruct((length // 2, width), F32),
            jax.ShapeDtypeStruct((8, length // 2, width), BF16),
        ),
        in_specs=[ANY] * 7,
        out_specs=(ANY, VMEM, VMEM, ANY, ANY, ANY) + (VMEM,) * 6,
        scratch_shapes=[
            pltpu.VMEM((4, length, width), BF16),
            pltpu.VMEM((8, length // 2, width), BF16),
        ]
        + token_sems() * 3
        + reduce_scratch(length // 2, width)
        + [DMA((7,)), DMA((7,))]
        + gather_sems(mid, a_waves)
        + gather_sems(mid, waves) * 3,
        compiler_params=pltpu.CompilerParams(
            collective_id=0, has_side_effects=True, vmem_limit_bytes=60 << 20
        ),
    )(tok, cot, table, wa, wg, wu, wd)


def reduce_steps(p, part, scratch, finish):
    abuf, sums, bbuf, cbuf, a_s, a_r, b_s, b_r, c_s, c_r = scratch
    sibling = (p.dp(p.z, p.m, 1 - p.c), p.x)
    x_near = (p.d, 1 - p.x)
    z_near = (p.dp(xor(p.z, 1), p.m, p.c), p.x)
    order = ((1, 1), (0, 1), (1, 0), (0, 0))
    sends = []

    def owner(n, c):
        fz, fx = order[n]
        return (xor(p.lo, fz) * 2 + c) * 2 + xor(p.x, fx)

    def go(copy):
        copy.start()
        sends.append(copy)

    for n in range(4):
        go(remote(part.at[owner(n, 1 - p.c)], abuf.at[n], a_s.at[n], a_r.at[n], sibling))
    yield
    rows = part.shape[1]
    step = 16

    def add(n, *more):
        own = owner(n, p.c)

        def body(i, carry):
            at = pl.ds(pl.multiple_of(i * step, step), step)
            total = part[own, at, :].astype(F32) + abuf[n, at, :].astype(F32)
            for other in more:
                total = total + other[at, :].astype(F32)
            sums[n, at, :] = total.astype(BF16)
            return carry

        lax.fori_loop(0, rows // step, body, 0)

    for n in range(2):
        arrived(abuf.at[n], a_r.at[n])
        add(n)
        go(remote(sums.at[n], bbuf.at[n], b_s.at[n], b_r.at[n], x_near))
    yield
    arrived(abuf.at[2], a_r.at[2])
    arrived(bbuf.at[0], b_r.at[0])
    add(2, bbuf.at[0])
    go(remote(sums.at[2], cbuf, c_s, c_r, z_near))
    yield
    arrived(abuf.at[3], a_r.at[3])
    arrived(bbuf.at[1], b_r.at[1])
    arrived(cbuf, c_r)
    mine = owner(3, p.c)

    def last(i, carry):
        at = pl.ds(pl.multiple_of(i * step, step), step)
        total = part[mine, at, :].astype(F32) + abuf[3, at, :].astype(F32)
        finish(at, total + bbuf[1, at, :].astype(F32) + cbuf[at, :].astype(F32))
        return carry

    lax.fori_loop(0, rows // step, last, 0)
    for copy in sends:
        copy.wait_send()


def share_steps(p, gathered, s, r):
    sibling = (p.dp(p.z, p.m, 1 - p.c), p.x)
    x_near = (p.d, 1 - p.x)
    z_near = (p.dp(xor(p.z, 1), p.m, p.c), p.x)
    sends = []

    def at(fz, fx, c):
        return gathered.at[(xor(p.lo, fz) * 2 + c) * 2 + xor(p.x, fx)]

    def go(ref, number, device):
        copy = remote(ref, ref, s.at[number], r.at[number], device)
        copy.start()
        sends.append(copy)

    own = at(0, 0, p.c)
    go(own, 0, z_near)
    go(own, 1, x_near)
    go(own, 2, sibling)
    yield
    far = at(1, 0, p.c)
    arrived(far, r.at[0])
    go(far, 3, x_near)
    go(far, 4, sibling)
    beside = at(0, 1, p.c)
    arrived(beside, r.at[1])
    go(beside, 5, sibling)
    yield
    across = at(1, 1, p.c)
    arrived(across, r.at[3])
    go(across, 6, sibling)
    yield
    for number, (fz, fx) in ((2, (0, 0)), (4, (1, 0)), (5, (0, 1)), (6, (1, 1))):
        arrived(at(fz, fx, 1 - p.c), r.at[number])
    for copy in sends:
        copy.wait_send()


def swap_steps(p, both, o_s, o_r):
    rows = both.shape[0] // 2
    half = pl.ds(pl.multiple_of(p.x * rows, 16), rows)
    copy = remote(both.at[half], both.at[half], o_s, o_r, (p.d, 1 - p.x))
    copy.start()
    yield
    copy.wait()


def norm_root(value):
    return lax.rsqrt(jnp.mean(value * value, axis=-1, keepdims=True) + EPSILON)


def norm_back(value, scaled):
    root = norm_root(value)
    return root * scaled - value * root**3 * jnp.mean(value * scaled, axis=-1, keepdims=True)


def reduce_scratch(rows, width):
    return [
        pltpu.VMEM((4, rows, width), BF16),
        pltpu.VMEM((3, rows, width), BF16),
        pltpu.VMEM((2, rows, width), BF16),
        pltpu.VMEM((rows, width), BF16),
        DMA((4,)), DMA((4,)), DMA((2,)), DMA((2,)), DMA, DMA,
    ]


def attention_back_steps(p, low, qkv, probs, p_buf, p_sem, mixture, fa, tabg, n1, n1_copy, gqkv, part, ga, a_scatter):
    length = qkv.shape[0] // 4
    half = length // 2
    qw = mixture.shape[1]
    heads = qw // HEAD_DIM
    scaling = HEAD_DIM ** (-0.5)

    def fetch(s):
        return pltpu.make_async_copy(probs.at[s], p_buf.at[s % 2], p_sem.at[s % 2])

    fetch(0).start()
    for s in range(4):
        if s < 3:
            fetch(s + 1).start()
        fetch(s).wait()
        here = pl.ds(s * length, length)
        cosine, signed = wide_tables(tabg[s])
        grads = low[2 * s : 2 * s + 2].reshape(length, low.shape[2])
        grad_mix = dot(grads, fa[:, qw + 128 :], ((1,), (0,))).astype(BF16)
        key = qkv[here, qw : qw + HEAD_DIM]
        value = qkv[here, qw + HEAD_DIM :]
        grad_value = jnp.zeros((length, HEAD_DIM), F32)
        grad_key = jnp.zeros((length, HEAD_DIM), F32)
        grad_query = []
        for h in range(heads):
            at = slice(HEAD_DIM * h, HEAD_DIM * h + HEAD_DIM)
            share = p_buf[s % 2, h]
            gm = grad_mix[:, at]
            gp = dot(gm, value, ((1,), (1,)))
            grad_value = grad_value + dot(share.astype(BF16), gm, ((0,), (0,)))
            centered = jnp.sum(share * gp, axis=-1, keepdims=True)
            gs = (share * (gp - centered)).astype(BF16)
            grad_query.append(dot(gs, key, ((1,), (0,))) * scaling)
            grad_key = grad_key + dot(gs, qkv[here, at], ((0,), (0,))) * scaling
        for b in range(qw // 128):
            pair = jnp.concatenate(grad_query[2 * b : 2 * b + 2], axis=1)
            gqkv[here, 128 * b : 128 * b + 128] = turn(pair, cosine, -signed).astype(BF16)
        pair = jnp.concatenate([grad_key, grad_value], axis=1)
        lanes = lanes_of(pair.shape)
        gqkv[here, qw:] = jnp.where(lanes < HEAD_DIM, turn(pair, cosine, -signed), pair).astype(BF16)
        for x in range(2):
            rows = pl.ds(s * length + x * half, half)
            part[s * 2 + x] = dot(gqkv[rows, :], fa[:, : qw + 128], ((1,), (1,))).astype(BF16)
        yield


def weight_grad_steps(low, mixture, n1, n1_copy, gqkv, ga, a_scatter):
    qw = mixture.shape[1]
    n1_copy.wait()
    width = low.shape[2]
    tile = 256

    def body(i, carry):
        at = pl.ds(pl.multiple_of(i * tile, tile), tile)
        rows = n1[:, :, at].reshape(-1, tile)
        ga[at, : qw + 128] = dot(rows, gqkv[...], ((0,), (0,))).astype(BF16)
        rows = low[:, :, at].reshape(-1, tile)
        ga[at, qw + 128 :] = dot(rows, mixture[...], ((0,), (0,))).astype(BF16)
        return carry

    lax.fori_loop(0, width // tile, body, 0)
    a_scatter.ready = True
    yield


def last_kernel(
    mid, a_waves, d_waves, g_waves, part_two, out_part, n1, probs, hid, cot, x, qkv, mixture, fa, tabg, gu, down,
    output, result, gu_out, down_out, ga_out, *scratch
):
    p = Place(mid)
    scratch = list(scratch)

    def take(count):
        taken = scratch[:count]
        del scratch[:count]
        return taken

    first_buf, second_buf, grad_hidden, low, gqkv, ga, p_buf, p_sem, in_sems = take(9)
    r1, r2, r3 = take(10), take(10), take(10)
    g_sems, o_sems, i_sems = take(2), take(2), take(2)
    gu_s, down_s, ga_s = take(8), take(8), take(8)
    loads = [
        pltpu.make_async_copy(part_two, first_buf, in_sems.at[0]),
        pltpu.make_async_copy(out_part, second_buf, in_sems.at[1]),
        pltpu.make_async_copy(n1, second_buf, in_sems.at[2]),
    ]
    loads[0].start()
    loads[1].start()
    greet(all_devices(p))
    mine = (p.lo * 2 + p.c) * 2 + p.x
    rows = hid.shape[0]

    def there(at):
        return pl.ds(pl.multiple_of(p.x * rows + at.start, 16), 16)

    def finish(at, total):
        grads = cot[at, :].astype(F32) + norm_back(hid[at, :], total)
        grad_hidden[at, :] = grads
        low[mine, at, :] = grads.astype(BF16)

    def finish_out(at, total):
        output[there(at), :] = (hid[at, :] + total).astype(BF16)

    def finish_in(at, total):
        result[there(at), :] = (grad_hidden[at, :] + norm_back(x[at, :].astype(F32), total)).astype(BF16)

    scatter_d = Scatter(p, down, down_s[0], down_s[1], down_out, down_s[2:], d_waves)
    scatter_g = Scatter(p, gu, gu_s[0], gu_s[1], gu_out, gu_s[2:], g_waves)
    scatter_a = Scatter(p, ga, ga_s[0], ga_s[1], ga_out, ga_s[2:], a_waves)
    scatter_a.ready = False

    def outputs():
        loads[1].wait()
        yield from reduce_steps(p, second_buf, r2, finish_out)
        loads[2].start()
        yield from swap_steps(p, output, *o_sems)

    out = outputs()

    def chained():
        loads[0].wait()
        yield from reduce_steps(p, first_buf, r1, finish)
        yield from share_steps(p, low, *g_sems)
        yield from attention_back_steps(
            p, low, qkv, probs, p_buf, p_sem, mixture, fa, tabg, second_buf, loads[2], gqkv, first_buf, ga, scatter_a
        )
        for _ in out:
            pass
        last = reduce_steps(p, first_buf, r3, finish_in)
        next(last)
        yield from weight_grad_steps(low, mixture, second_buf, loads[2], gqkv, ga, scatter_a)
        yield from last
        yield from swap_steps(p, result, *i_sems)

    drive(scatter_steps(scatter_d, scatter_g, scatter_a), chained(), after(OUT_AT, out))


def last(mid, part_two, out_part, n1, probs, hid, cot, x, qkv, mixture, fa, tabg, gu, down):
    eight, rows, width = part_two.shape
    n = 8 * mid
    w_rows = gu.shape[0] // n
    a_waves, d_waves, g_waves = waves_of(w_rows, 4), waves_of(w_rows, 4), waves_of(w_rows, 8)
    return pl.pallas_call(
        functools.partial(last_kernel, mid, a_waves, d_waves, g_waves),
        out_shape=(
            jax.ShapeDtypeStruct((2 * rows, width), BF16),
            jax.ShapeDtypeStruct((2 * rows, width), BF16),
            jax.ShapeDtypeStruct((8, w_rows, gu.shape[1]), BF16),
            jax.ShapeDtypeStruct((8, w_rows, down.shape[1]), BF16),
            jax.ShapeDtypeStruct((8, w_rows, fa.shape[1]), BF16),
        ),
        in_specs=[ANY] * 4 + [VMEM] * 7 + [ANY] * 2,
        out_specs=(VMEM,) * 2 + (ANY,) * 3,
        scratch_shapes=[
            pltpu.VMEM((eight, rows, width), BF16),
            pltpu.VMEM((eight, rows, width), BF16),
            pltpu.VMEM((rows, width), F32),
            pltpu.VMEM((eight, rows, width), BF16),
            pltpu.VMEM(qkv.shape, BF16),
            pltpu.VMEM(fa.shape, BF16),
            pltpu.VMEM((2,) + probs.shape[1:], F32),
            DMA((2,)),
            DMA((3,)),
        ]
        + reduce_scratch(rows, width) * 3
        + [DMA((7,)), DMA((7,)), DMA, DMA, DMA, DMA]
        + scatter_scratch(mid, w_rows, gu.shape[1], g_waves)
        + scatter_scratch(mid, w_rows, down.shape[1], d_waves)
        + scatter_scratch(mid, w_rows, fa.shape[1], a_waves),
        compiler_params=pltpu.CompilerParams(
            collective_id=1, has_side_effects=True, vmem_limit_bytes=60 << 20
        ),
    )(part_two, out_part, n1, probs, hid, cot, x, qkv, mixture, fa, tabg, gu, down)


def token_table(segments):
    length = segments.shape[0]
    places = jnp.arange(length, dtype=jnp.int32)
    earlier = jnp.concatenate([segments[:1], segments[:-1]])
    begins = jnp.where(segments != earlier, places, 0)
    begin = jnp.max(jnp.where(places[:, None] >= places[None, :], begins[None, :], 0), axis=-1)
    halves = HEAD_DIM // 2
    inverse = THETA ** (-2.0 * jnp.arange(halves, dtype=F32) / HEAD_DIM)
    angles = (places - begin).astype(F32)[:, None] * inverse
    wide = jnp.broadcast_to(begin.astype(F32)[:, None], (length, 128 - 2 * halves))
    return jnp.concatenate([jnp.cos(angles), jnp.sin(angles), wide], axis=-1)


def dot(a, b, dims):
    return lax.dot_general(a, b, (dims, ((), ())), preferred_element_type=F32)


def local(
    mid, tokens, attn_gain, w_query, w_key, w_value, w_out, mlp_gain, w_gate, w_up, w_down, segment_ids, cotangent
):
    length, width = tokens.shape
    half = length // 2
    rows = w_query.shape[0]
    x_at = lax.axis_index("tensor")

    def blocks(w):
        return w.reshape(rows, 4, w.shape[1] // 4).transpose(1, 0, 2)

    gain_one, gain_two = attn_gain.astype(F32)[:, None], mlp_gain.astype(F32)[:, None]

    def scaled(w, gain):
        return blocks((w.astype(F32) * gain).astype(BF16))

    wg, wu, wd = scaled(w_gate, gain_two), scaled(w_up, gain_two), blocks(w_down.T)
    wa = jnp.concatenate(
        [scaled(w_query, gain_one), scaled(w_key, gain_one), scaled(w_value, gain_one), blocks(w_out.T)], axis=-1
    )
    units = w_gate.shape[1] // 4
    qw, kw = w_query.shape[1] // 4, w_key.shape[1] // 4
    heads = qw // HEAD_DIM
    cotg, tabg, fa, gate_w, up_w, down_t, normed, qkv, probs, mixture, hidden, n2 = first(
        mid, tokens, cotangent, token_table(segment_ids), wa, wg, wu, wd, qw
    )
    own_x = lax.dynamic_slice_in_dim(tokens, x_at * half, half, 0)
    own_cot = lax.dynamic_slice_in_dim(cotangent, x_at * half, half, 0)
    n2 = n2.reshape(4 * length, width)

    gate = dot(n2, gate_w, ((1,), (0,)))
    up = dot(n2, up_w, ((1,), (0,)))
    sigmoid = 1.0 / (1.0 + jnp.exp(-gate))
    silu = gate / (1.0 + jnp.exp(-gate))
    activated = (silu * up).astype(BF16)
    out_part = dot(activated, down_t, ((1,), (1,))).astype(BF16)
    cots = cotg.reshape(4 * length, width)
    grad_act = dot(cots, down_t, ((1,), (0,)))
    grad_gate = (grad_act * up * sigmoid * (1.0 + gate * (1.0 - sigmoid))).astype(BF16)
    grad_up = (grad_act * silu).astype(BF16)
    part_two = (dot(grad_gate, gate_w, ((1,), (1,))) + dot(grad_up, up_w, ((1,), (1,)))).astype(BF16)
    down_g = dot(cots, activated, ((0,), (0,))).astype(BF16)
    gu_g = dot(n2, jnp.concatenate([grad_gate, grad_up], axis=1), ((0,), (0,))).astype(BF16)

    eight = (8, half, width)
    output, input_grad, gu_parts, down_parts, a_parts = last(
        mid, part_two.reshape(eight), out_part.reshape(eight), normed.reshape(eight), probs, hidden, own_cot, own_x,
        qkv, mixture, fa, tabg, gu_g, down_g
    )

    def total(parts):
        parts = parts.reshape(2, 4, rows, -1).astype(F32)
        return parts[0] + parts[1]

    def across(block):
        return block.transpose(1, 0, 2).reshape(rows, -1)

    def down(block):
        return block.transpose(0, 2, 1).reshape(-1, rows)

    t_gate, t_up = jnp.split(total(gu_parts), 2, axis=-1)
    t_q, t_k, t_v, t_out = jnp.split(total(a_parts), [qw, qw + kw, qw + 2 * kw], axis=-1)
    t_gate, t_up, t_q, t_k, t_v = (across(t) for t in (t_gate, t_up, t_q, t_k, t_v))

    def gain_grad(*pairs):
        return sum(jnp.sum(w.astype(F32) * g, axis=1) for w, g in pairs)

    gain_grads = jnp.stack(
        [gain_grad((w_query, t_q), (w_key, t_k), (w_value, t_v)), gain_grad((w_gate, t_gate), (w_up, t_up))]
    )
    gain_grads = lax.psum(gain_grads, "tensor")
    return (
        output,
        input_grad.astype(F32),
        gain_grads[0],
        t_q * gain_one,
        t_k * gain_one,
        t_v * gain_one,
        down(t_out),
        gain_grads[1],
        t_gate * gain_two,
        t_up * gain_two,
        down(total(down_parts)),
    )


def solution(mesh):
    in_specs = (
        P("dp", None), P("dp"), P("dp", "tensor"), P("dp", "tensor"), P("dp", "tensor"), P("tensor", "dp"),
        P("dp"), P("dp", "tensor"), P("dp", "tensor"), P("tensor", "dp"), P("dp"), P("dp", None),
    )
    out_specs = (
        P("dp", None), P("dp", None), P("dp"), P("dp", "tensor"), P("dp", "tensor"), P("dp", "tensor"),
        P("tensor", "dp"), P("dp"), P("dp", "tensor"), P("dp", "tensor"), P("tensor", "dp"),
    )
    return jax.shard_map(
        functools.partial(local, mesh.shape["dp"] // 8),
        mesh=mesh, in_specs=in_specs, out_specs=out_specs, check_vma=False,
    )
```

```python
import functools

import jax
import jax.numpy as jnp
from jax import lax
from jax.experimental import pallas as pl
from jax.experimental.pallas import tpu as pltpu
from jax.sharding import PartitionSpec as P

HEAD_DIM = 64
EPSILON = 1e-05
THETA = 500000.0
MESH = pl.DeviceIdType.MESH
ANY = pl.BlockSpec(memory_space=pl.ANY)
VMEM = pl.BlockSpec(memory_space=pltpu.VMEM)
F32 = jnp.float32
BF16 = jnp.bfloat16
DMA = pltpu.SemaphoreType.DMA
COT_AT = 7
OUT_AT = 4


class Place:
    def __init__(self, mid):
        self.mid = mid
        self.d = lax.axis_index("dp")
        self.x = lax.axis_index("tensor")
        self.c = self.d % 2
        self.m = (self.d // 2) % mid
        self.z = self.d // (2 * mid)
        self.lo = self.z % 2

    def dp(self, z, m, c):
        return (z * self.mid + m) * 2 + c

    def peer(self, k):
        return xor(self.z, k // 2), xor(self.c, k % 2)

    def other_m(self, j):
        return (self.m + 1 + j) % self.mid


def xor(a, k):
    if k == 0:
        return a
    low = a % 2
    high = a // 2
    if k % 2:
        low = 1 - low
    if k // 2:
        high = 1 - high
    return high * 2 + low


def remote(src, dst, send, recv, device):
    copy = pltpu.make_async_remote_copy(
        src_ref=src, dst_ref=dst, send_sem=send, recv_sem=recv, device_id=device, device_id_type=MESH
    )
    return copy


def greet(devices):
    barrier = pltpu.get_barrier_semaphore()
    for device in devices:
        pl.semaphore_signal(barrier, inc=1, device_id=device, device_id_type=MESH)
    pl.semaphore_wait(barrier, len(devices))


def arrived(dst, sem):
    pltpu.make_async_copy(dst, dst, sem).wait()


class Gather:
    def __init__(self, p, w, full, sems, waves):
        self.p, self.w, self.full, self.waves = p, w, full, waves
        self.z_s, self.r, self.f_s, self.loc = sems
        self.rows = w.shape[1] // waves
        self.block = p.lo * 2 + p.c
        self.order = list(range(7, 0, -1))
        self.pushes, self.sends = {}, []

    def at(self, wave):
        return pl.ds(wave * self.rows, self.rows)

    def there(self, d, wave):
        return self.full.at[pl.ds(pl.multiple_of(d * self.w.shape[1] + wave * self.rows, 16), self.rows)]

    def push(self, wave):
        p, at = self.p, self.at(wave)
        for k in self.order:
            z, c = p.peer(k)
            copy = remote(
                self.w.at[(z % 2) * 2 + c, at], self.there(p.d, wave), self.z_s.at[k, wave], self.r.at[p.d, wave],
                (p.dp(z, p.m, c), p.x),
            )
            copy.start()
            self.pushes[k, wave] = copy
        self.forward_one(self.w.at[self.block, at], p.d, wave, 0)

    def forward_one(self, src, d, wave, k):
        p = self.p
        for j in range(p.mid - 1):
            copy = remote(
                src, self.there(d, wave), self.f_s.at[k, wave, j], self.r.at[d, wave],
                (p.dp(p.z, p.other_m(j), p.c), p.x),
            )
            copy.start()
            self.sends.append(copy)

    def forward(self, wave):
        p = self.p
        for k in self.order:
            z, c = p.peer(k)
            d = p.dp(z, p.m, c)
            here = self.there(d, wave)
            arrived(here, self.r.at[d, wave])
            self.forward_one(here, d, wave, k)
        if wave == self.waves - 1:
            self.all_forwarded = True

    def start_own(self):
        self.all_forwarded = False
        rows = self.w.shape[1]
        at = pl.ds(pl.multiple_of(self.p.d * rows, 16), rows)
        self.own = pltpu.make_async_copy(self.w.at[self.block], self.full.at[at], self.loc)
        self.own.start()

    def pushed(self, wave):
        for k in self.order:
            self.pushes[k, wave].wait_send()

    def landed(self):
        p = self.p
        for wave in range(self.waves):
            for k in range(8):
                z, c = p.peer(k)
                for j in range(p.mid - 1):
                    d = p.dp(z, p.other_m(j), c)
                    arrived(self.there(d, wave), self.r.at[d, wave])
        self.own.wait()
        self.done = True

    def finish(self):
        if not getattr(self, "done", False):
            self.landed()
        for copy in self.sends:
            copy.wait_send()


def gather_steps(*gathers, lag=2):
    for g in gathers:
        g.start_own()
    items = [(g, wave) for g in gathers for wave in range(g.waves)]
    for n, (g, wave) in enumerate(items):
        if n >= lag:
            before, old = items[n - lag]
            before.pushed(old)
            before.forward(old)
        g.push(wave)
        yield
    for g, wave in items[max(0, len(items) - lag) :]:
        g.pushed(wave)
        g.forward(wave)
        yield
    for g in gathers:
        g.finish()


def gather_sems(mid, waves):
    return [DMA((8, waves)), DMA((8 * mid, waves)), DMA((8, waves, mid - 1)), DMA]


class Scatter:
    def __init__(self, p, g, own, other, out, sems, waves):
        self.p, self.g, self.own, self.other, self.out, self.waves = p, g, own, other, out, waves
        self.y_s, self.y_r, self.z_s, self.z_r, self.load, self.loc = sems
        self.full_rows = own.shape[1]
        self.rows = self.full_rows // waves
        self.order = list(range(7, -1, -1))
        self.y_sends, self.z_sends, self.loads = {}, [], {}
        self.ready = True

    def piece(self, d, wave):
        return self.g.at[pl.ds(pl.multiple_of(d * self.full_rows + wave * self.rows, 16), self.rows)]

    def at(self, wave):
        return pl.ds(wave * self.rows, self.rows)

    def start_loads(self):
        p = self.p
        for wave in range(self.waves):
            for k in self.order:
                z, c = p.peer(k)
                copy = pltpu.make_async_copy(
                    self.piece(p.dp(z, p.m, c), wave), self.own.at[k, self.at(wave)], self.load.at[k, wave]
                )
                copy.start()
                self.loads[k, wave] = copy

    def y_send(self, wave):
        p = self.p
        for k in self.order:
            z, c = p.peer(k)
            for j in range(p.mid - 1):
                m = p.other_m(j)
                there = p.mid - 2 - j
                copy = remote(
                    self.piece(p.dp(z, m, c), wave), self.other.at[there, k, self.at(wave)],
                    self.y_s.at[k, wave, j], self.y_r.at[k, wave, there], (p.dp(p.z, m, p.c), p.x),
                )
                copy.start()
                self.y_sends[k, wave, j] = copy

    def z_push(self, wave):
        p = self.p
        at = self.at(wave)
        me = p.z * 2 + p.c
        for k in self.order:
            z, c = p.peer(k)
            for j in range(p.mid - 1):
                arrived(self.other.at[j, k, at], self.y_r.at[k, wave, j])
            self.loads[k, wave].wait()

            def add(i, carry):
                here = pl.ds(pl.multiple_of(wave * self.rows + i * 16, 16), 16)
                total = self.own[k, here, :].astype(F32)
                for j in range(p.mid - 1):
                    total = total + self.other[j, k, here, :].astype(F32)
                self.own[k, here, :] = total.astype(BF16)
                return carry

            lax.fori_loop(0, self.rows // 16, add, 0)
            src, dst = self.own.at[k, at], self.out.at[me, at]
            if k == 0:
                copy = pltpu.make_async_copy(src, dst, self.loc.at[wave])
                copy.start()
                self.z_sends.append((copy, True))
            else:
                copy = remote(src, dst, self.z_s.at[k, wave], self.z_r.at[me, wave], (p.dp(z, p.m, c), p.x))
                copy.start()
                self.z_sends.append((copy, False))

    def y_sent(self, wave):
        for k in self.order:
            for j in range(self.p.mid - 1):
                self.y_sends[k, wave, j].wait_send()

    def finish(self):
        p = self.p
        for wave in range(self.waves):
            for k in range(1, 8):
                z, c = p.peer(k)
                src = z * 2 + c
                arrived(self.out.at[src, self.at(wave)], self.z_r.at[src, wave])
        for copy, here in self.z_sends:
            copy.wait() if here else copy.wait_send()


def scatter_steps(*scatters, lag=2):
    items = [(s, wave) for s in scatters for wave in range(s.waves)]
    pushed = 0
    for n, (s, wave) in enumerate(items):
        if not s.ready:
            while pushed < n:
                before, old = items[pushed]
                before.z_push(old)
                pushed += 1
            while not s.ready:
                yield
        if wave == 0:
            s.start_loads()
        if n >= lag:
            before, old = items[n - lag]
            before.y_sent(old)
        s.y_send(wave)
        while pushed < n:
            before, old = items[pushed]
            before.z_push(old)
            pushed += 1
        yield
    s, wave = items[-1]
    s.z_push(wave)
    yield
    for s, wave in items[max(0, len(items) - lag) :]:
        s.y_sent(wave)
    for s in scatters:
        s.finish()


def scatter_scratch(mid, rows, width, waves):
    return [
        pltpu.VMEM((8, rows, width), BF16),
        pltpu.VMEM((mid - 1, 8, rows, width), BF16),
        DMA((8, waves, mid - 1)), DMA((8, waves, mid - 1)), DMA((8, waves)), DMA((8, waves)), DMA((8, waves)),
        DMA((waves,)),
    ]


def waves_of(rows, most):
    return max(w for w in range(1, most + 1) if rows % (16 * w) == 0)


def drive(*streams):
    left = list(streams)
    while left:
        for stream in list(left):
            try:
                next(stream)
            except StopIteration:
                left.remove(stream)


def after(steps, stream):
    for _ in range(steps):
        yield
    yield from stream


def chain(*streams):
    for stream in streams:
        yield from stream


def all_devices(p):
    return (
        [(p.dp(z, p.m, c), p.x) for z, c in map(p.peer, range(1, 8))]
        + [(p.dp(p.z, p.other_m(j), p.c), p.x) for j in range(p.mid - 1)]
        + [(p.d, 1 - p.x)]
    )


def token_steps(p, tok, tokg, t_s, t_r, loc, whole):
    rows = tok.shape[0]
    half = rows // 2
    seq = p.lo * 2 + p.c
    z_near = (p.dp(xor(p.z, 1), p.m, p.c), p.x)
    c_near = (p.dp(p.z, p.m, 1 - p.c), p.x)
    x_near = (p.d, 1 - p.x)
    mine = pl.ds(pl.multiple_of(p.x * half, 16), half)
    theirs = pl.ds(pl.multiple_of((1 - p.x) * half, 16), half)
    if whole:
        mine = pl.ds(0, rows)
    far_seq = (1 - p.lo) * 2 + p.c
    c_seq = p.lo * 2 + 1 - p.c
    cc_seq = (1 - p.lo) * 2 + 1 - p.c
    sends = []

    def go(copy):
        copy.start()
        sends.append(copy)

    go(remote(tok.at[mine], tokg.at[seq, mine], t_s.at[0], t_r.at[0], z_near))
    go(remote(tok, tokg.at[seq], t_s.at[1], t_r.at[1], c_near))
    here = pltpu.make_async_copy(tok, tokg.at[seq], loc)
    here.start()
    yield
    arrived(tokg.at[far_seq, mine], t_r.at[0])
    if not whole:
        go(remote(tokg.at[far_seq, mine], tokg.at[far_seq, mine], t_s.at[2], t_r.at[2], x_near))
    go(remote(tokg.at[far_seq, mine], tokg.at[far_seq, mine], t_s.at[3], t_r.at[3], c_near))
    yield
    if not whole:
        arrived(tokg.at[far_seq, theirs], t_r.at[2])
        go(remote(tokg.at[far_seq, theirs], tokg.at[far_seq, theirs], t_s.at[4], t_r.at[4], c_near))
        yield
    here.wait()
    arrived(tokg.at[c_seq], t_r.at[1])
    arrived(tokg.at[cc_seq, mine], t_r.at[3])
    if not whole:
        arrived(tokg.at[cc_seq, theirs], t_r.at[4])
    for copy in sends:
        copy.wait_send()


def token_sems():
    return [DMA((5,)), DMA((5,)), DMA]


def lanes_of(shape):
    return lax.broadcasted_iota(jnp.int32, shape, 1)


def wide_tables(table):
    lanes = lanes_of(table.shape)
    half = HEAD_DIM // 2
    cosine = jnp.where(lanes < half, table, 0.0)
    sine = pltpu.roll(jnp.where((lanes >= half) & (lanes < 2 * half), table, 0.0), 128 - half, 1)
    spread = cosine + pltpu.roll(cosine, half, 1)
    spread = spread + pltpu.roll(spread, 2 * half, 1)
    signed = pltpu.roll(sine, half, 1) - sine
    signed = signed + pltpu.roll(signed, 2 * half, 1)
    return spread, signed


def turn(values, cosine, signed):
    half = HEAD_DIM // 2
    lanes = lanes_of(values.shape) % HEAD_DIM
    swapped = jnp.where(lanes < half, pltpu.roll(values, 128 - half, 1), pltpu.roll(values, half, 1))
    return values * cosine + swapped * signed


def attention_steps(p, tokg, tabg, fa, n1, qkv, probs, mixture, part, gather_a):
    length = tokg.shape[1]
    qw = mixture.shape[1]
    heads = qw // HEAD_DIM
    scaling = HEAD_DIM ** (-0.5)
    for s in range(4):

        def norm(i, carry):
            at = pl.ds(pl.multiple_of(i * 32, 32), 32)
            value = tokg[s, at, :].astype(F32)
            n1[pl.ds(pl.multiple_of(s * length + i * 32, 32), 32), :] = (value * norm_root(value)).astype(BF16)
            return carry

        lax.fori_loop(0, length // 32, norm, 0)
    yield
    while not gather_a.all_forwarded:
        yield
    gather_a.landed()
    for s in range(4):
        here = pl.ds(s * length, length)
        table = tabg[s]
        cosine, signed = wide_tables(table)
        pre = dot(n1[here, :], fa[:, : qw + 128], ((1,), (0,)))
        for b in range(qw // 128):
            at = slice(128 * b, 128 * b + 128)
            qkv[here, at] = turn(pre[:, at], cosine, signed).astype(BF16)
        last = pre[:, qw:]
        keys = turn(last, cosine, signed)
        lanes = lanes_of(last.shape)
        qkv[here, qw:] = jnp.where(lanes < HEAD_DIM, keys, last).astype(BF16)
        key = qkv[here, qw : qw + HEAD_DIM]
        value = qkv[here, qw + HEAD_DIM :]
        begin = table[:, 2 * HEAD_DIM // 2 : 2 * HEAD_DIM // 2 + 1]
        columns = lanes_of((length, length))
        allowed = (columns.astype(F32) >= begin) & (
            columns <= lax.broadcasted_iota(jnp.int32, (length, length), 0)
        )
        for h in range(heads):
            at = slice(HEAD_DIM * h, HEAD_DIM * h + HEAD_DIM)
            scores = dot(qkv[here, at], key, ((1,), (1,))) * scaling
            scores = jnp.where(allowed, scores, -1e30)
            exponent = jnp.exp(scores - jnp.max(scores, axis=-1, keepdims=True))
            share = exponent / jnp.sum(exponent, axis=-1, keepdims=True)
            probs[s, h] = share
            mixture[here, at] = dot(share.astype(BF16), value, ((1,), (0,))).astype(BF16)
        half = length // 2
        for x in range(2):
            rows = pl.ds(s * length + x * half, half)
            part[s * 2 + x] = dot(mixture[rows, :], fa[:, qw + 128 :], ((1,), (1,))).astype(BF16)
        yield


class Flag:
    def __init__(self):
        self.up = False


def then(stream, flag):
    yield from stream
    flag.up = True


def gated_steps(n2, fg, fu, cotg, act, by_gate, by_up, down, gate_up, cot_here):
    while not (gate_up[0].all_forwarded and gate_up[1].all_forwarded):
        yield
    for g in gate_up:
        g.landed()
    width = n2.shape[2]
    tokens, units = act.shape
    tile, rows = 256, 512

    for m in range(tokens // rows):

        def body(i, carry, m=m):
            at = pl.ds(pl.multiple_of(i * tile, tile), tile)
            here = pl.ds(m * rows, rows)
            each = n2.shape[1]
            lines = n2[m * rows // each : (m + 1) * rows // each].reshape(rows, width)
            gate = dot(lines, fg[:, at], ((1,), (0,)))
            up = dot(lines, fu[:, at], ((1,), (0,)))
            sigmoid = 1.0 / (1.0 + jnp.exp(-gate))
            silu = gate * sigmoid
            act[here, at] = (silu * up).astype(BF16)
            by_up[here, at] = silu.astype(BF16)
            by_gate[here, at] = (up * sigmoid * (1.0 + gate * (1.0 - sigmoid))).astype(BF16)
            return carry

        lax.fori_loop(0, units // tile, body, 0)
        yield
    while not cot_here.up:
        yield
    for part in range(2):

        def body(i, carry):
            at = pl.ds(pl.multiple_of(i * tile, tile), tile)
            lines = cotg[:, :, at].reshape(tokens, tile)
            down[at, :] = dot(lines, act[...], ((0,), (0,))).astype(BF16)
            return carry

        each = width // tile // 2
        lax.fori_loop(part * each, part * each + each, body, 0)
        yield


def first_kernel(mid, a_waves, waves, tok, cot, table, wa, wg, wu, wd, *refs):
    p = Place(mid)
    refs = list(refs)

    def take(count):
        taken = refs[:count]
        del refs[:count]
        return taken

    outs = take(FIRST_OUTS)
    fd = take(1)[0]
    kept = take(FIRST_OUTS)
    cotg, tabg, fa, fg, fu, n1, qkv, probs, mixture, hidden, n2, act, by_gate, by_up, down = kept
    tokg, part, out_sems = take(3)
    tok_sems, cot_sems, tab_sems = take(3), take(3), take(3)
    reduce_refs, share_refs = take(10), take(2)
    greet(all_devices(p))
    gather_a = Gather(p, wa, fa, take(4), a_waves)
    rest = [Gather(p, w, f, take(4), waves) for w, f in ((wg, fg), (wu, fu), (wd, fd))]
    seq = p.lo * 2 + p.c
    mine = seq * 2 + p.x
    half = hidden.shape[0]
    cot_here = Flag()
    leaving = []

    def leave(*numbers):
        for n in numbers:
            copy = pltpu.make_async_copy(kept[n], outs[n], out_sems.at[n])
            copy.start()
            leaving.append(copy)

    def finish(at, total):
        there = pl.ds(pl.multiple_of(p.x * half + at.start, 16), 16)
        value = tokg[seq, there, :].astype(F32) + total
        hidden[at, :] = value
        n2[mine, at, :] = (value * norm_root(value)).astype(BF16)

    def chained():
        yield from tokens
        yield from attention_steps(p, tokg, tabg, fa, n1, qkv, probs, mixture, part, gather_a)
        leave(1, 2, 5, 6, 7, 8)
        yield from reduce_steps(p, part, reduce_refs, finish)
        leave(9)
        yield from share_steps(p, n2, *share_refs)
        leave(10)
        yield from gated_steps(n2, fg, fu, cotg, act, by_gate, by_up, down, rest[:2], cot_here)
        leave(0, 3, 4, 11, 12, 13, 14)

    tab = token_steps(p, table, tabg, *tab_sems, whole=True)
    tokens = token_steps(p, tok, tokg, *tok_sems, whole=False)
    next(tokens)
    next(tab)
    drive(
        gather_steps(gather_a, *rest),
        chained(),
        tab,
        after(COT_AT, then(token_steps(p, cot, cotg, *cot_sems, whole=False), cot_here)),
    )
    for copy in leaving:
        copy.wait()


FIRST_OUTS = 15


def first(mid, tok, cot, table, wa, wg, wu, wd, qw):
    a_waves, waves = waves_of(wa.shape[1], 4), waves_of(wg.shape[1], 4)
    length, width = tok.shape
    n = 8 * mid
    heads = qw // HEAD_DIM
    tokens, units = 4 * length, wg.shape[2]

    def full(w):
        return ((n * w.shape[1], w.shape[2]), BF16)

    outs = [
        ((4,) + cot.shape, BF16),
        ((4,) + table.shape, F32),
        full(wa), full(wg), full(wu),
        ((tokens, width), BF16),
        ((tokens, qw + 128), BF16),
        ((4, heads, length, length), F32),
        ((tokens, qw), BF16),
        ((length // 2, width), F32),
        ((8, length // 2, width), BF16),
        ((tokens, units), BF16), ((tokens, units), BF16), ((tokens, units), BF16),
        ((width, units), BF16),
    ]
    return pl.pallas_call(
        functools.partial(first_kernel, mid, a_waves, waves),
        out_shape=[jax.ShapeDtypeStruct(*out) for out in outs + [full(wd)]],
        in_specs=[ANY] * 7,
        out_specs=[ANY] * (FIRST_OUTS + 1),
        scratch_shapes=[pltpu.VMEM(*out) for out in outs]
        + [
            pltpu.VMEM((4, length, width), BF16),
            pltpu.VMEM((8, length // 2, width), BF16),
            DMA((FIRST_OUTS,)),
        ]
        + token_sems() * 3
        + reduce_scratch(length // 2, width)
        + [DMA((7,)), DMA((7,))]
        + gather_sems(mid, a_waves)
        + gather_sems(mid, waves) * 3,
        compiler_params=pltpu.CompilerParams(
            collective_id=0, has_side_effects=True, vmem_limit_bytes=60 << 20
        ),
    )(tok, cot, table, wa, wg, wu, wd)


def reduce_steps(p, part, scratch, finish):
    abuf, sums, bbuf, cbuf, a_s, a_r, b_s, b_r, c_s, c_r = scratch
    sibling = (p.dp(p.z, p.m, 1 - p.c), p.x)
    x_near = (p.d, 1 - p.x)
    z_near = (p.dp(xor(p.z, 1), p.m, p.c), p.x)
    order = ((1, 1), (0, 1), (1, 0), (0, 0))
    sends = []

    def owner(n, c):
        fz, fx = order[n]
        return (xor(p.lo, fz) * 2 + c) * 2 + xor(p.x, fx)

    def go(copy):
        copy.start()
        sends.append(copy)

    for n in range(4):
        go(remote(part.at[owner(n, 1 - p.c)], abuf.at[n], a_s.at[n], a_r.at[n], sibling))
    yield
    rows = part.shape[1]
    step = 16

    def add(n, *more):
        own = owner(n, p.c)

        def body(i, carry):
            at = pl.ds(pl.multiple_of(i * step, step), step)
            total = part[own, at, :].astype(F32) + abuf[n, at, :].astype(F32)
            for other in more:
                total = total + other[at, :].astype(F32)
            sums[n, at, :] = total.astype(BF16)
            return carry

        lax.fori_loop(0, rows // step, body, 0)

    for n in range(2):
        arrived(abuf.at[n], a_r.at[n])
        add(n)
        go(remote(sums.at[n], bbuf.at[n], b_s.at[n], b_r.at[n], x_near))
    yield
    arrived(abuf.at[2], a_r.at[2])
    arrived(bbuf.at[0], b_r.at[0])
    add(2, bbuf.at[0])
    go(remote(sums.at[2], cbuf, c_s, c_r, z_near))
    yield
    arrived(abuf.at[3], a_r.at[3])
    arrived(bbuf.at[1], b_r.at[1])
    arrived(cbuf, c_r)
    mine = owner(3, p.c)

    def last(i, carry):
        at = pl.ds(pl.multiple_of(i * step, step), step)
        total = part[mine, at, :].astype(F32) + abuf[3, at, :].astype(F32)
        finish(at, total + bbuf[1, at, :].astype(F32) + cbuf[at, :].astype(F32))
        return carry

    lax.fori_loop(0, rows // step, last, 0)
    for copy in sends:
        copy.wait_send()


def share_steps(p, gathered, s, r):
    sibling = (p.dp(p.z, p.m, 1 - p.c), p.x)
    x_near = (p.d, 1 - p.x)
    z_near = (p.dp(xor(p.z, 1), p.m, p.c), p.x)
    sends = []

    def at(fz, fx, c):
        return gathered.at[(xor(p.lo, fz) * 2 + c) * 2 + xor(p.x, fx)]

    def go(ref, number, device):
        copy = remote(ref, ref, s.at[number], r.at[number], device)
        copy.start()
        sends.append(copy)

    own = at(0, 0, p.c)
    go(own, 0, z_near)
    go(own, 1, x_near)
    go(own, 2, sibling)
    yield
    far = at(1, 0, p.c)
    arrived(far, r.at[0])
    go(far, 3, x_near)
    go(far, 4, sibling)
    beside = at(0, 1, p.c)
    arrived(beside, r.at[1])
    go(beside, 5, sibling)
    yield
    across = at(1, 1, p.c)
    arrived(across, r.at[3])
    go(across, 6, sibling)
    yield
    for number, (fz, fx) in ((2, (0, 0)), (4, (1, 0)), (5, (0, 1)), (6, (1, 1))):
        arrived(at(fz, fx, 1 - p.c), r.at[number])
    for copy in sends:
        copy.wait_send()


def swap_steps(p, both, o_s, o_r):
    rows = both.shape[0] // 2
    half = pl.ds(pl.multiple_of(p.x * rows, 16), rows)
    copy = remote(both.at[half], both.at[half], o_s, o_r, (p.d, 1 - p.x))
    copy.start()
    yield
    copy.wait()


def norm_root(value):
    return lax.rsqrt(jnp.mean(value * value, axis=-1, keepdims=True) + EPSILON)


def norm_back(value, scaled):
    root = norm_root(value)
    return root * scaled - value * root**3 * jnp.mean(value * scaled, axis=-1, keepdims=True)


def reduce_scratch(rows, width):
    return [
        pltpu.VMEM((4, rows, width), BF16),
        pltpu.VMEM((3, rows, width), BF16),
        pltpu.VMEM((2, rows, width), BF16),
        pltpu.VMEM((rows, width), BF16),
        DMA((4,)), DMA((4,)), DMA((2,)), DMA((2,)), DMA, DMA,
    ]


def attention_back_steps(p, low, qkv, probs, p_buf, p_sem, mixture, fa, tabg, n1, n1_copy, gqkv, part, ga, a_scatter):
    length = qkv.shape[0] // 4
    half = length // 2
    qw = mixture.shape[1]
    heads = qw // HEAD_DIM
    scaling = HEAD_DIM ** (-0.5)

    def fetch(s):
        return pltpu.make_async_copy(probs.at[s], p_buf.at[s % 2], p_sem.at[s % 2])

    fetch(0).start()
    for s in range(4):
        if s < 3:
            fetch(s + 1).start()
        fetch(s).wait()
        here = pl.ds(s * length, length)
        cosine, signed = wide_tables(tabg[s])
        grads = low[2 * s : 2 * s + 2].reshape(length, low.shape[2])
        grad_mix = dot(grads, fa[:, qw + 128 :], ((1,), (0,))).astype(BF16)
        key = qkv[here, qw : qw + HEAD_DIM]
        value = qkv[here, qw + HEAD_DIM :]
        grad_value = jnp.zeros((length, HEAD_DIM), F32)
        grad_key = jnp.zeros((length, HEAD_DIM), F32)
        grad_query = []
        for h in range(heads):
            at = slice(HEAD_DIM * h, HEAD_DIM * h + HEAD_DIM)
            share = p_buf[s % 2, h]
            gm = grad_mix[:, at]
            gp = dot(gm, value, ((1,), (1,)))
            grad_value = grad_value + dot(share.astype(BF16), gm, ((0,), (0,)))
            centered = jnp.sum(share * gp, axis=-1, keepdims=True)
            gs = (share * (gp - centered)).astype(BF16)
            grad_query.append(dot(gs, key, ((1,), (0,))) * scaling)
            grad_key = grad_key + dot(gs, qkv[here, at], ((0,), (0,))) * scaling
        for b in range(qw // 128):
            pair = jnp.concatenate(grad_query[2 * b : 2 * b + 2], axis=1)
            gqkv[here, 128 * b : 128 * b + 128] = turn(pair, cosine, -signed).astype(BF16)
        pair = jnp.concatenate([grad_key, grad_value], axis=1)
        lanes = lanes_of(pair.shape)
        gqkv[here, qw:] = jnp.where(lanes < HEAD_DIM, turn(pair, cosine, -signed), pair).astype(BF16)
        for x in range(2):
            rows = pl.ds(s * length + x * half, half)
            part[s * 2 + x] = dot(gqkv[rows, :], fa[:, : qw + 128], ((1,), (1,))).astype(BF16)
        yield


def weight_grad_steps(low, mixture, n1, n1_copy, gqkv, ga, a_scatter):
    qw = mixture.shape[1]
    n1_copy.wait()
    width = low.shape[2]
    tile = 256

    def body(i, carry):
        at = pl.ds(pl.multiple_of(i * tile, tile), tile)
        rows = n1[:, :, at].reshape(-1, tile)
        ga[at, : qw + 128] = dot(rows, gqkv[...], ((0,), (0,))).astype(BF16)
        rows = low[:, :, at].reshape(-1, tile)
        ga[at, qw + 128 :] = dot(rows, mixture[...], ((0,), (0,))).astype(BF16)
        return carry

    lax.fori_loop(0, width // tile, body, 0)
    a_scatter.ready = True
    yield


def last_kernel(
    mid, a_waves, d_waves, g_waves, part_two, out_part, n1, probs, hid, cot, x, qkv, mixture, fa, tabg, gu, down,
    output, result, gu_out, down_out, ga_out, *scratch
):
    p = Place(mid)
    scratch = list(scratch)

    def take(count):
        taken = scratch[:count]
        del scratch[:count]
        return taken

    first_buf, second_buf, grad_hidden, low, gqkv, ga, p_buf, p_sem, in_sems = take(9)
    r1, r2, r3 = take(10), take(10), take(10)
    g_sems, o_sems, i_sems = take(2), take(2), take(2)
    gu_s, down_s, ga_s = take(8), take(8), take(8)
    loads = [
        pltpu.make_async_copy(part_two, first_buf, in_sems.at[0]),
        pltpu.make_async_copy(out_part, second_buf, in_sems.at[1]),
        pltpu.make_async_copy(n1, second_buf, in_sems.at[2]),
    ]
    loads[0].start()
    loads[1].start()
    greet(all_devices(p))
    mine = (p.lo * 2 + p.c) * 2 + p.x
    rows = hid.shape[0]

    def there(at):
        return pl.ds(pl.multiple_of(p.x * rows + at.start, 16), 16)

    def finish(at, total):
        grads = cot[at, :].astype(F32) + norm_back(hid[at, :], total)
        grad_hidden[at, :] = grads
        low[mine, at, :] = grads.astype(BF16)

    def finish_out(at, total):
        output[there(at), :] = (hid[at, :] + total).astype(BF16)

    def finish_in(at, total):
        result[there(at), :] = (grad_hidden[at, :] + norm_back(x[at, :].astype(F32), total)).astype(BF16)

    scatter_d = Scatter(p, down, down_s[0], down_s[1], down_out, down_s[2:], d_waves)
    scatter_g = Scatter(p, gu, gu_s[0], gu_s[1], gu_out, gu_s[2:], g_waves)
    scatter_a = Scatter(p, ga, ga_s[0], ga_s[1], ga_out, ga_s[2:], a_waves)
    scatter_a.ready = False

    def outputs():
        loads[1].wait()
        yield from reduce_steps(p, second_buf, r2, finish_out)
        loads[2].start()
        yield from swap_steps(p, output, *o_sems)

    out = outputs()

    def chained():
        loads[0].wait()
        yield from reduce_steps(p, first_buf, r1, finish)
        yield from share_steps(p, low, *g_sems)
        yield from attention_back_steps(
            p, low, qkv, probs, p_buf, p_sem, mixture, fa, tabg, second_buf, loads[2], gqkv, first_buf, ga, scatter_a
        )
        for _ in out:
            pass
        last = reduce_steps(p, first_buf, r3, finish_in)
        next(last)
        yield from weight_grad_steps(low, mixture, second_buf, loads[2], gqkv, ga, scatter_a)
        yield from last
        yield from swap_steps(p, result, *i_sems)

    drive(scatter_steps(scatter_d, scatter_g, scatter_a), chained(), after(OUT_AT, out))


def last(mid, part_two, out_part, n1, probs, hid, cot, x, qkv, mixture, fa, tabg, gu, down):
    eight, rows, width = part_two.shape
    n = 8 * mid
    w_rows = gu.shape[0] // n
    a_waves, d_waves, g_waves = waves_of(w_rows, 4), waves_of(w_rows, 4), waves_of(w_rows, 8)
    return pl.pallas_call(
        functools.partial(last_kernel, mid, a_waves, d_waves, g_waves),
        out_shape=(
            jax.ShapeDtypeStruct((2 * rows, width), BF16),
            jax.ShapeDtypeStruct((2 * rows, width), BF16),
            jax.ShapeDtypeStruct((8, w_rows, gu.shape[1]), BF16),
            jax.ShapeDtypeStruct((8, w_rows, down.shape[1]), BF16),
            jax.ShapeDtypeStruct((8, w_rows, fa.shape[1]), BF16),
        ),
        in_specs=[ANY] * 4 + [VMEM] * 7 + [ANY] * 2,
        out_specs=(VMEM,) * 2 + (ANY,) * 3,
        scratch_shapes=[
            pltpu.VMEM((eight, rows, width), BF16),
            pltpu.VMEM((eight, rows, width), BF16),
            pltpu.VMEM((rows, width), F32),
            pltpu.VMEM((eight, rows, width), BF16),
            pltpu.VMEM(qkv.shape, BF16),
            pltpu.VMEM(fa.shape, BF16),
            pltpu.VMEM((2,) + probs.shape[1:], F32),
            DMA((2,)),
            DMA((3,)),
        ]
        + reduce_scratch(rows, width) * 3
        + [DMA((7,)), DMA((7,)), DMA, DMA, DMA, DMA]
        + scatter_scratch(mid, w_rows, gu.shape[1], g_waves)
        + scatter_scratch(mid, w_rows, down.shape[1], d_waves)
        + scatter_scratch(mid, w_rows, fa.shape[1], a_waves),
        compiler_params=pltpu.CompilerParams(
            collective_id=1, has_side_effects=True, vmem_limit_bytes=60 << 20
        ),
    )(part_two, out_part, n1, probs, hid, cot, x, qkv, mixture, fa, tabg, gu, down)


def settle_kernel(
    gu, down, own, gains, low, w_gate, w_up, w_query, w_key, w_value,
    gate_o, up_o, down_o, query_o, key_o, value_o, out_o, gain_o, wide_o
):
    u = pl.program_id(0)
    units, qw = gate_o.shape[1], query_o.shape[1]
    kw = key_o.shape[1] // 4
    gain_one, gain_two = gains[:, 0:1], gains[:, 1:2]
    wide_o[...] = low[...].astype(F32)

    def total(ref, first, width):
        at = slice(first, first + width)
        return ref[0, 0, :, at].astype(F32) + ref[1, 0, :, at].astype(F32)

    def weigh(w, grad):
        return jnp.sum(w.astype(F32) * grad, axis=1, keepdims=True)

    gate, up = total(gu, 0, units), total(gu, units, units)
    gate_o[...] = gate * gain_two
    up_o[...] = up * gain_two
    two = weigh(w_gate[...], gate) + weigh(w_up[...], up)
    down_o[...] = total(down, 0, units).T
    query = total(own, 0, qw)
    query_o[...] = query * gain_one
    out_o[...] = total(own, qw + 2 * kw, out_o.shape[0]).T
    both = total(own, qw, 2 * kw)
    one = weigh(w_query[...], query)

    @pl.when(u == 0)
    def _():
        gain_o[...] = jnp.zeros_like(gain_o)

    lanes = lanes_of(gain_o.shape)
    for i in range(4):

        @pl.when(u == i)
        def _(i=i):
            at = slice(i * kw, i * kw + kw)
            key_o[:, at] = both[:, :kw] * gain_one
            value_o[:, at] = both[:, kw:] * gain_one
            more = weigh(w_key[:, at], both[:, :kw]) + weigh(w_value[:, at], both[:, kw:])
            gain_o[...] += jnp.where(lanes == 0, one + more, jnp.where(lanes == 1, two, 0.0))


def settle(gu, down, own, gains, low, w_gate, w_up, w_query, w_key, w_value):
    rows = gu.shape[1]
    length, width = low.shape
    units, qw, kw = w_gate.shape[1] // 4, w_query.shape[1] // 4, w_key.shape[1] // 4

    def parts(ref):
        return ref.reshape(2, 4, rows, ref.shape[2])

    def part_spec(ref):
        return pl.BlockSpec((2, 1, rows, ref.shape[2]), lambda u: (0, u, 0, 0))

    def column(w):
        return pl.BlockSpec((rows, w), lambda u: (0, u))

    def row(w):
        return pl.BlockSpec((w, rows), lambda u: (u, 0))

    def whole(*shape):
        return pl.BlockSpec(shape, lambda u: (0, 0))

    def out(*shape):
        return jax.ShapeDtypeStruct(shape, F32)

    lines = pl.BlockSpec((length // 4, width), lambda u: (u, 0))
    return pl.pallas_call(
        settle_kernel,
        grid=(4,),
        out_shape=(
            out(rows, 4 * units), out(rows, 4 * units), out(4 * units, rows), out(rows, 4 * qw), out(rows, 4 * kw),
            out(rows, 4 * kw), out(4 * qw, rows), out(rows, 128), out(length, width),
        ),
        in_specs=[
            part_spec(gu), part_spec(down), part_spec(own), whole(rows, 2), lines,
            column(units), column(units), column(qw), whole(rows, 4 * kw), whole(rows, 4 * kw),
        ],
        out_specs=(
            column(units), column(units), row(units), column(qw), whole(rows, 4 * kw), whole(rows, 4 * kw), row(qw),
            whole(rows, 128), lines,
        ),
        compiler_params=pltpu.CompilerParams(vmem_limit_bytes=48 << 20),
    )(parts(gu), parts(down), parts(own), gains, low, w_gate, w_up, w_query, w_key, w_value)


def token_table(segments):
    length = segments.shape[0]
    places = jnp.arange(length, dtype=jnp.int32)
    earlier = jnp.concatenate([segments[:1], segments[:-1]])
    begins = jnp.where(segments != earlier, places, 0)
    begin = jnp.max(jnp.where(places[:, None] >= places[None, :], begins[None, :], 0), axis=-1)
    halves = HEAD_DIM // 2
    inverse = THETA ** (-2.0 * jnp.arange(halves, dtype=F32) / HEAD_DIM)
    angles = (places - begin).astype(F32)[:, None] * inverse
    wide = jnp.broadcast_to(begin.astype(F32)[:, None], (length, 128 - 2 * halves))
    return jnp.concatenate([jnp.cos(angles), jnp.sin(angles), wide], axis=-1)


def dot(a, b, dims):
    return lax.dot_general(a, b, (dims, ((), ())), preferred_element_type=F32)


def local(
    mid, tokens, attn_gain, w_query, w_key, w_value, w_out, mlp_gain, w_gate, w_up, w_down, segment_ids, cotangent
):
    length, width = tokens.shape
    half = length // 2
    rows = w_query.shape[0]
    x_at = lax.axis_index("tensor")

    def blocks(w):
        return w.reshape(rows, 4, w.shape[1] // 4).transpose(1, 0, 2)

    gain_one, gain_two = attn_gain.astype(F32)[:, None], mlp_gain.astype(F32)[:, None]

    def scaled(w, gain):
        return blocks((w.astype(F32) * gain).astype(BF16))

    wg, wu, wd = scaled(w_gate, gain_two), scaled(w_up, gain_two), blocks(w_down.T)
    wa = jnp.concatenate(
        [scaled(w_query, gain_one), scaled(w_key, gain_one), scaled(w_value, gain_one), blocks(w_out.T)], axis=-1
    )
    qw = w_query.shape[1] // 4
    (
        cotg, tabg, fa, gate_w, up_w, normed, qkv, probs, mixture, hidden, n2, activated, by_gate, by_up, down_g, down_t
    ) = first(mid, tokens, cotangent, token_table(segment_ids), wa, wg, wu, wd, qw)
    own_x = lax.dynamic_slice_in_dim(tokens, x_at * half, half, 0)
    own_cot = lax.dynamic_slice_in_dim(cotangent, x_at * half, half, 0)
    n2 = n2.reshape(4 * length, width)

    out_part = dot(activated, down_t, ((1,), (1,))).astype(BF16)
    cots = cotg.reshape(4 * length, width)
    grad_act = dot(cots, down_t, ((1,), (0,)))
    grad_gate = (grad_act * by_gate.astype(F32)).astype(BF16)
    grad_up = (grad_act * by_up.astype(F32)).astype(BF16)
    part_two = (dot(grad_gate, gate_w, ((1,), (1,))) + dot(grad_up, up_w, ((1,), (1,)))).astype(BF16)
    gu_g = dot(n2, jnp.concatenate([grad_gate, grad_up], axis=1), ((0,), (0,))).astype(BF16)

    eight = (8, half, width)
    output, input_grad, gu_parts, down_parts, a_parts = last(
        mid, part_two.reshape(eight), out_part.reshape(eight), normed.reshape(eight), probs, hidden, own_cot, own_x,
        qkv, mixture, fa, tabg, gu_g, down_g
    )

    gains = jnp.stack([attn_gain, mlp_gain], axis=1).astype(F32)
    gate_g, up_g, down_g, query_g, key_g, value_g, out_g, gain_sums, input_grad = settle(
        gu_parts, down_parts, a_parts, gains, input_grad, w_gate, w_up, w_query, w_key, w_value
    )
    gain_g = lax.psum(gain_sums[:, :2], "tensor")
    return (
        output, input_grad, gain_g[:, 0], query_g, key_g, value_g, out_g, gain_g[:, 1], gate_g, up_g, down_g
    )


def solution(mesh):
    in_specs = (
        P("dp", None), P("dp"), P("dp", "tensor"), P("dp", "tensor"), P("dp", "tensor"), P("tensor", "dp"),
        P("dp"), P("dp", "tensor"), P("dp", "tensor"), P("tensor", "dp"), P("dp"), P("dp", None),
    )
    out_specs = (
        P("dp", None), P("dp", None), P("dp"), P("dp", "tensor"), P("dp", "tensor"), P("dp", "tensor"),
        P("tensor", "dp"), P("dp"), P("dp", "tensor"), P("dp", "tensor"), P("tensor", "dp"),
    )
    return jax.shard_map(
        functools.partial(local, mesh.shape["dp"] // 8),
        mesh=mesh, in_specs=in_specs, out_specs=out_specs, check_vma=False,
    )
```

```python
import functools

import jax
import jax.numpy as jnp
from jax import lax
from jax.experimental import pallas as pl
from jax.experimental.pallas import tpu as pltpu
from jax.sharding import PartitionSpec as P

HEAD_DIM = 64
EPSILON = 1e-05
THETA = 500000.0
MESH = pl.DeviceIdType.MESH
ANY = pl.BlockSpec(memory_space=pl.ANY)
VMEM = pl.BlockSpec(memory_space=pltpu.VMEM)
F32 = jnp.float32
BF16 = jnp.bfloat16
DMA = pltpu.SemaphoreType.DMA
COT_AT = 7
OUT_AT = 1


class Place:
    def __init__(self, mid):
        self.mid = mid
        self.d = lax.axis_index("dp")
        self.x = lax.axis_index("tensor")
        self.c = self.d % 2
        self.m = (self.d // 2) % mid
        self.z = self.d // (2 * mid)
        self.lo = self.z % 2

    def dp(self, z, m, c):
        return (z * self.mid + m) * 2 + c

    def peer(self, k):
        return xor(self.z, k // 2), xor(self.c, k % 2)

    def other_m(self, j):
        return (self.m + 1 + j) % self.mid


def xor(a, k):
    if k == 0:
        return a
    low = a % 2
    high = a // 2
    if k % 2:
        low = 1 - low
    if k // 2:
        high = 1 - high
    return high * 2 + low


def remote(src, dst, send, recv, device):
    copy = pltpu.make_async_remote_copy(
        src_ref=src, dst_ref=dst, send_sem=send, recv_sem=recv, device_id=device, device_id_type=MESH
    )
    return copy


def greet(devices):
    barrier = pltpu.get_barrier_semaphore()
    for device in devices:
        pl.semaphore_signal(barrier, inc=1, device_id=device, device_id_type=MESH)
    pl.semaphore_wait(barrier, len(devices))


def arrived(dst, sem):
    pltpu.make_async_copy(dst, dst, sem).wait()


class Gather:
    def __init__(self, p, w, full, sems, waves):
        self.p, self.w, self.full, self.waves = p, w, full, waves
        self.z_s, self.r, self.f_s, self.loc = sems
        self.rows = w.shape[1] // waves
        self.block = p.lo * 2 + p.c
        self.order = list(range(7, 0, -1))
        self.pushes, self.sends = {}, []

    def at(self, wave):
        return pl.ds(wave * self.rows, self.rows)

    def there(self, d, wave):
        return self.full.at[pl.ds(pl.multiple_of(d * self.w.shape[1] + wave * self.rows, 16), self.rows)]

    def push(self, wave):
        p, at = self.p, self.at(wave)
        for k in self.order:
            z, c = p.peer(k)
            copy = remote(
                self.w.at[(z % 2) * 2 + c, at], self.there(p.d, wave), self.z_s.at[k, wave], self.r.at[p.d, wave],
                (p.dp(z, p.m, c), p.x),
            )
            copy.start()
            self.pushes[k, wave] = copy
        self.forward_one(self.w.at[self.block, at], p.d, wave, 0)

    def forward_one(self, src, d, wave, k):
        p = self.p
        for j in range(p.mid - 1):
            copy = remote(
                src, self.there(d, wave), self.f_s.at[k, wave, j], self.r.at[d, wave],
                (p.dp(p.z, p.other_m(j), p.c), p.x),
            )
            copy.start()
            self.sends.append(copy)

    def forward(self, wave):
        p = self.p
        for k in self.order:
            z, c = p.peer(k)
            d = p.dp(z, p.m, c)
            here = self.there(d, wave)
            arrived(here, self.r.at[d, wave])
            self.forward_one(here, d, wave, k)
        if wave == self.waves - 1:
            self.all_forwarded = True

    def start_own(self):
        self.all_forwarded = False
        rows = self.w.shape[1]
        at = pl.ds(pl.multiple_of(self.p.d * rows, 16), rows)
        self.own = pltpu.make_async_copy(self.w.at[self.block], self.full.at[at], self.loc)
        self.own.start()

    def pushed(self, wave):
        for k in self.order:
            self.pushes[k, wave].wait_send()

    def landed(self):
        p = self.p
        for wave in range(self.waves):
            for k in range(8):
                z, c = p.peer(k)
                for j in range(p.mid - 1):
                    d = p.dp(z, p.other_m(j), c)
                    arrived(self.there(d, wave), self.r.at[d, wave])
        self.own.wait()
        self.done = True

    def finish(self):
        if not getattr(self, "done", False):
            self.landed()
        for copy in self.sends:
            copy.wait_send()


def gather_steps(*gathers, lag=2):
    for g in gathers:
        g.start_own()
    items = [(g, wave) for g in gathers for wave in range(g.waves)]
    for n, (g, wave) in enumerate(items):
        if n >= lag:
            before, old = items[n - lag]
            before.pushed(old)
            before.forward(old)
        g.push(wave)
        yield
    for g, wave in items[max(0, len(items) - lag) :]:
        g.pushed(wave)
        g.forward(wave)
        yield
    for g in gathers:
        g.finish()


def gather_sems(mid, waves):
    return [DMA((8, waves)), DMA((8 * mid, waves)), DMA((8, waves, mid - 1)), DMA]


class Scatter:
    def __init__(self, p, g, own, other, out, sems, waves):
        self.p, self.g, self.own, self.other, self.out, self.waves = p, g, own, other, out, waves
        self.y_s, self.y_r, self.z_s, self.z_r, self.load, self.loc = sems
        self.full_rows = own.shape[1]
        self.rows = self.full_rows // waves
        self.order = list(range(7, -1, -1))
        self.y_sends, self.z_sends, self.loads = {}, [], {}
        self.ready = True

    def piece(self, d, wave):
        return self.g.at[pl.ds(pl.multiple_of(d * self.full_rows + wave * self.rows, 16), self.rows)]

    def at(self, wave):
        return pl.ds(wave * self.rows, self.rows)

    def start_loads(self):
        p = self.p
        for wave in range(self.waves):
            for k in self.order:
                z, c = p.peer(k)
                copy = pltpu.make_async_copy(
                    self.piece(p.dp(z, p.m, c), wave), self.own.at[k, self.at(wave)], self.load.at[k, wave]
                )
                copy.start()
                self.loads[k, wave] = copy

    def y_send(self, wave):
        p = self.p
        for k in self.order:
            z, c = p.peer(k)
            for j in range(p.mid - 1):
                m = p.other_m(j)
                there = p.mid - 2 - j
                copy = remote(
                    self.piece(p.dp(z, m, c), wave), self.other.at[there, k, self.at(wave)],
                    self.y_s.at[k, wave, j], self.y_r.at[k, wave, there], (p.dp(p.z, m, p.c), p.x),
                )
                copy.start()
                self.y_sends[k, wave, j] = copy

    def z_push(self, wave):
        p = self.p
        at = self.at(wave)
        me = p.z * 2 + p.c
        for k in self.order:
            z, c = p.peer(k)
            for j in range(p.mid - 1):
                arrived(self.other.at[j, k, at], self.y_r.at[k, wave, j])
            self.loads[k, wave].wait()

            def add(i, carry):
                here = pl.ds(pl.multiple_of(wave * self.rows + i * 16, 16), 16)
                total = self.own[k, here, :].astype(F32)
                for j in range(p.mid - 1):
                    total = total + self.other[j, k, here, :].astype(F32)
                self.own[k, here, :] = total.astype(BF16)
                return carry

            lax.fori_loop(0, self.rows // 16, add, 0)
            src, dst = self.own.at[k, at], self.out.at[me, at]
            if k == 0:
                copy = pltpu.make_async_copy(src, dst, self.loc.at[wave])
                copy.start()
                self.z_sends.append((copy, True))
            else:
                copy = remote(src, dst, self.z_s.at[k, wave], self.z_r.at[me, wave], (p.dp(z, p.m, c), p.x))
                copy.start()
                self.z_sends.append((copy, False))

    def y_sent(self, wave):
        for k in self.order:
            for j in range(self.p.mid - 1):
                self.y_sends[k, wave, j].wait_send()

    def finish(self):
        p = self.p
        for wave in range(self.waves):
            for k in range(1, 8):
                z, c = p.peer(k)
                src = z * 2 + c
                arrived(self.out.at[src, self.at(wave)], self.z_r.at[src, wave])
        for copy, here in self.z_sends:
            copy.wait() if here else copy.wait_send()


def scatter_steps(*scatters, lag=2):
    items = [(s, wave) for s in scatters for wave in range(s.waves)]
    pushed = 0
    for n, (s, wave) in enumerate(items):
        if not s.ready:
            while pushed < n:
                before, old = items[pushed]
                before.z_push(old)
                pushed += 1
            while not s.ready:
                yield
        if wave == 0:
            s.start_loads()
        if n >= lag:
            before, old = items[n - lag]
            before.y_sent(old)
        s.y_send(wave)
        while pushed < n:
            before, old = items[pushed]
            before.z_push(old)
            pushed += 1
        yield
    s, wave = items[-1]
    s.z_push(wave)
    yield
    for s, wave in items[max(0, len(items) - lag) :]:
        s.y_sent(wave)
    for s in scatters:
        s.finish()


def scatter_scratch(mid, rows, width, waves):
    return [
        pltpu.VMEM((8, rows, width), BF16),
        pltpu.VMEM((mid - 1, 8, rows, width), BF16),
        DMA((8, waves, mid - 1)), DMA((8, waves, mid - 1)), DMA((8, waves)), DMA((8, waves)), DMA((8, waves)),
        DMA((waves,)),
    ]


def waves_of(rows, most):
    return max(w for w in range(1, most + 1) if rows % (16 * w) == 0)


def drive(*streams):
    left = list(streams)
    while left:
        for stream in list(left):
            try:
                next(stream)
            except StopIteration:
                left.remove(stream)


def after(steps, stream):
    for _ in range(steps):
        yield
    yield from stream


def chain(*streams):
    for stream in streams:
        yield from stream


def all_devices(p):
    return (
        [(p.dp(z, p.m, c), p.x) for z, c in map(p.peer, range(1, 8))]
        + [(p.dp(p.z, p.other_m(j), p.c), p.x) for j in range(p.mid - 1)]
        + [(p.d, 1 - p.x)]
    )


def token_steps(p, tok, tokg, t_s, t_r, loc, whole):
    rows = tok.shape[0]
    half = rows // 2
    seq = p.lo * 2 + p.c
    z_near = (p.dp(xor(p.z, 1), p.m, p.c), p.x)
    c_near = (p.dp(p.z, p.m, 1 - p.c), p.x)
    x_near = (p.d, 1 - p.x)
    mine = pl.ds(pl.multiple_of(p.x * half, 16), half)
    theirs = pl.ds(pl.multiple_of((1 - p.x) * half, 16), half)
    if whole:
        mine = pl.ds(0, rows)
    far_seq = (1 - p.lo) * 2 + p.c
    c_seq = p.lo * 2 + 1 - p.c
    cc_seq = (1 - p.lo) * 2 + 1 - p.c
    sends = []

    def go(copy):
        copy.start()
        sends.append(copy)

    go(remote(tok.at[mine], tokg.at[seq, mine], t_s.at[0], t_r.at[0], z_near))
    go(remote(tok, tokg.at[seq], t_s.at[1], t_r.at[1], c_near))
    here = pltpu.make_async_copy(tok, tokg.at[seq], loc)
    here.start()
    yield
    arrived(tokg.at[far_seq, mine], t_r.at[0])
    if not whole:
        go(remote(tokg.at[far_seq, mine], tokg.at[far_seq, mine], t_s.at[2], t_r.at[2], x_near))
    go(remote(tokg.at[far_seq, mine], tokg.at[far_seq, mine], t_s.at[3], t_r.at[3], c_near))
    yield
    if not whole:
        arrived(tokg.at[far_seq, theirs], t_r.at[2])
        go(remote(tokg.at[far_seq, theirs], tokg.at[far_seq, theirs], t_s.at[4], t_r.at[4], c_near))
        yield
    here.wait()
    arrived(tokg.at[c_seq], t_r.at[1])
    arrived(tokg.at[cc_seq, mine], t_r.at[3])
    if not whole:
        arrived(tokg.at[cc_seq, theirs], t_r.at[4])
    for copy in sends:
        copy.wait_send()


def token_sems():
    return [DMA((5,)), DMA((5,)), DMA]


def lanes_of(shape):
    return lax.broadcasted_iota(jnp.int32, shape, 1)


def wide_tables(table):
    lanes = lanes_of(table.shape)
    half = HEAD_DIM // 2
    cosine = jnp.where(lanes < half, table, 0.0)
    sine = pltpu.roll(jnp.where((lanes >= half) & (lanes < 2 * half), table, 0.0), 128 - half, 1)
    spread = cosine + pltpu.roll(cosine, half, 1)
    spread = spread + pltpu.roll(spread, 2 * half, 1)
    signed = pltpu.roll(sine, half, 1) - sine
    signed = signed + pltpu.roll(signed, 2 * half, 1)
    return spread, signed


def turn(values, cosine, signed):
    half = HEAD_DIM // 2
    lanes = lanes_of(values.shape) % HEAD_DIM
    swapped = jnp.where(lanes < half, pltpu.roll(values, 128 - half, 1), pltpu.roll(values, half, 1))
    return values * cosine + swapped * signed


def attention_steps(p, tokg, tabg, fa, n1, qkv, probs, mixture, part, gather_a):
    length = tokg.shape[1]
    qw = mixture.shape[1]
    heads = qw // HEAD_DIM
    scaling = HEAD_DIM ** (-0.5)
    for s in range(4):

        def norm(i, carry):
            at = pl.ds(pl.multiple_of(i * 32, 32), 32)
            value = tokg[s, at, :].astype(F32)
            n1[pl.ds(pl.multiple_of(s * length + i * 32, 32), 32), :] = (value * norm_root(value)).astype(BF16)
            return carry

        lax.fori_loop(0, length // 32, norm, 0)
    yield
    while not gather_a.all_forwarded:
        yield
    gather_a.landed()
    for s in range(4):
        here = pl.ds(s * length, length)
        table = tabg[s]
        cosine, signed = wide_tables(table)
        pre = dot(n1[here, :], fa[:, : qw + 128], ((1,), (0,)))
        for b in range(qw // 128):
            at = slice(128 * b, 128 * b + 128)
            qkv[here, at] = turn(pre[:, at], cosine, signed).astype(BF16)
        last = pre[:, qw:]
        keys = turn(last, cosine, signed)
        lanes = lanes_of(last.shape)
        qkv[here, qw:] = jnp.where(lanes < HEAD_DIM, keys, last).astype(BF16)
        key = qkv[here, qw : qw + HEAD_DIM]
        value = qkv[here, qw + HEAD_DIM :]
        begin = table[:, 2 * HEAD_DIM // 2 : 2 * HEAD_DIM // 2 + 1]
        columns = lanes_of((length, length))
        allowed = (columns.astype(F32) >= begin) & (
            columns <= lax.broadcasted_iota(jnp.int32, (length, length), 0)
        )
        for h in range(heads):
            at = slice(HEAD_DIM * h, HEAD_DIM * h + HEAD_DIM)
            scores = dot(qkv[here, at], key, ((1,), (1,))) * scaling
            scores = jnp.where(allowed, scores, -1e30)
            exponent = jnp.exp(scores - jnp.max(scores, axis=-1, keepdims=True))
            share = exponent / jnp.sum(exponent, axis=-1, keepdims=True)
            probs[s, h] = share
            mixture[here, at] = dot(share.astype(BF16), value, ((1,), (0,))).astype(BF16)
        half = length // 2
        for x in range(2):
            rows = pl.ds(s * length + x * half, half)
            part[s * 2 + x] = dot(mixture[rows, :], fa[:, qw + 128 :], ((1,), (1,))).astype(BF16)
        yield


class Flag:
    def __init__(self):
        self.up = False


def then(stream, flag):
    yield from stream
    flag.up = True


def gated_steps(n2, fg, fu, cotg, act, by_gate, by_up, down, gate_up, cot_here):
    while not (gate_up[0].all_forwarded and gate_up[1].all_forwarded):
        yield
    for g in gate_up:
        g.landed()
    width = n2.shape[2]
    tokens, units = act.shape
    tile, rows = 256, 512

    for m in range(tokens // rows):

        def body(i, carry, m=m):
            at = pl.ds(pl.multiple_of(i * tile, tile), tile)
            here = pl.ds(m * rows, rows)
            each = n2.shape[1]
            lines = n2[m * rows // each : (m + 1) * rows // each].reshape(rows, width)
            gate = dot(lines, fg[:, at], ((1,), (0,)))
            up = dot(lines, fu[:, at], ((1,), (0,)))
            sigmoid = 1.0 / (1.0 + jnp.exp(-gate))
            silu = gate * sigmoid
            act[here, at] = (silu * up).astype(BF16)
            by_up[here, at] = silu.astype(BF16)
            by_gate[here, at] = (up * sigmoid * (1.0 + gate * (1.0 - sigmoid))).astype(BF16)
            return carry

        lax.fori_loop(0, units // tile, body, 0)
        yield
    while not cot_here.up:
        yield
    for part in range(2):

        def body(i, carry):
            at = pl.ds(pl.multiple_of(i * tile, tile), tile)
            lines = cotg[:, :, at].reshape(tokens, tile)
            down[at, :] = dot(lines, act[...], ((0,), (0,))).astype(BF16)
            return carry

        each = width // tile // 2
        lax.fori_loop(part * each, part * each + each, body, 0)
        yield


def first_kernel(mid, a_waves, waves, tok, cot, table, wa, wg, wu, wd, *refs):
    p = Place(mid)
    refs = list(refs)

    def take(count):
        taken = refs[:count]
        del refs[:count]
        return taken

    outs = take(FIRST_OUTS)
    fd = take(1)[0]
    kept = take(FIRST_OUTS)
    cotg, tabg, fa, fg, fu, n1, qkv, probs, mixture, hidden, n2, act, by_gate, by_up, down = kept
    tokg, part, out_sems = take(3)
    tok_sems, cot_sems, tab_sems = take(3), take(3), take(3)
    reduce_refs, share_refs = take(10), take(2)
    greet(all_devices(p))
    gather_a = Gather(p, wa, fa, take(4), a_waves)
    rest = [Gather(p, w, f, take(4), waves) for w, f in ((wg, fg), (wu, fu), (wd, fd))]
    seq = p.lo * 2 + p.c
    mine = seq * 2 + p.x
    half = hidden.shape[0]
    cot_here = Flag()
    leaving = []

    def leave(*numbers):
        for n in numbers:
            copy = pltpu.make_async_copy(kept[n], outs[n], out_sems.at[n])
            copy.start()
            leaving.append(copy)

    def finish(at, total):
        there = pl.ds(pl.multiple_of(p.x * half + at.start, 16), 16)
        value = tokg[seq, there, :].astype(F32) + total
        hidden[at, :] = value
        n2[mine, at, :] = (value * norm_root(value)).astype(BF16)

    def chained():
        yield from tokens
        yield from attention_steps(p, tokg, tabg, fa, n1, qkv, probs, mixture, part, gather_a)
        leave(1, 2, 5, 6, 7, 8)
        yield from reduce_steps(p, part, reduce_refs, finish)
        leave(9)
        yield from share_steps(p, n2, *share_refs)
        leave(10)
        yield from gated_steps(n2, fg, fu, cotg, act, by_gate, by_up, down, rest[:2], cot_here)
        leave(0, 3, 4, 11, 12, 13, 14)

    tab = token_steps(p, table, tabg, *tab_sems, whole=True)
    tokens = token_steps(p, tok, tokg, *tok_sems, whole=False)
    next(tokens)
    next(tab)
    drive(
        gather_steps(gather_a, *rest),
        chained(),
        tab,
        after(COT_AT, then(token_steps(p, cot, cotg, *cot_sems, whole=False), cot_here)),
    )
    for copy in leaving:
        copy.wait()


FIRST_OUTS = 15


def first(mid, tok, cot, table, wa, wg, wu, wd, qw):
    a_waves, waves = waves_of(wa.shape[1], 4), waves_of(wg.shape[1], 4)
    length, width = tok.shape
    n = 8 * mid
    heads = qw // HEAD_DIM
    tokens, units = 4 * length, wg.shape[2]

    def full(w):
        return ((n * w.shape[1], w.shape[2]), BF16)

    outs = [
        ((4,) + cot.shape, BF16),
        ((4,) + table.shape, F32),
        full(wa), full(wg), full(wu),
        ((tokens, width), BF16),
        ((tokens, qw + 128), BF16),
        ((4, heads, length, length), F32),
        ((tokens, qw), BF16),
        ((length // 2, width), F32),
        ((8, length // 2, width), BF16),
        ((tokens, units), BF16), ((tokens, units), BF16), ((tokens, units), BF16),
        ((width, units), BF16),
    ]
    return pl.pallas_call(
        functools.partial(first_kernel, mid, a_waves, waves),
        out_shape=[jax.ShapeDtypeStruct(*out) for out in outs + [full(wd)]],
        in_specs=[ANY] * 7,
        out_specs=[ANY] * (FIRST_OUTS + 1),
        scratch_shapes=[pltpu.VMEM(*out) for out in outs]
        + [
            pltpu.VMEM((4, length, width), BF16),
            pltpu.VMEM((8, length // 2, width), BF16),
            DMA((FIRST_OUTS,)),
        ]
        + token_sems() * 3
        + reduce_scratch(length // 2, width)
        + [DMA((7,)), DMA((7,))]
        + gather_sems(mid, a_waves)
        + gather_sems(mid, waves) * 3,
        compiler_params=pltpu.CompilerParams(
            collective_id=0, has_side_effects=True, vmem_limit_bytes=62 << 20
        ),
    )(tok, cot, table, wa, wg, wu, wd)


def reduce_steps(p, part, scratch, finish):
    abuf, sums, bbuf, cbuf, a_s, a_r, b_s, b_r, c_s, c_r = scratch
    sibling = (p.dp(p.z, p.m, 1 - p.c), p.x)
    x_near = (p.d, 1 - p.x)
    z_near = (p.dp(xor(p.z, 1), p.m, p.c), p.x)
    order = ((1, 1), (0, 1), (1, 0), (0, 0))
    sends = []

    def owner(n, c):
        fz, fx = order[n]
        return (xor(p.lo, fz) * 2 + c) * 2 + xor(p.x, fx)

    def go(copy):
        copy.start()
        sends.append(copy)

    for n in range(4):
        go(remote(part.at[owner(n, 1 - p.c)], abuf.at[n], a_s.at[n], a_r.at[n], sibling))
    yield
    rows = part.shape[1]
    step = 16

    def add(n, *more):
        own = owner(n, p.c)

        def body(i, carry):
            at = pl.ds(pl.multiple_of(i * step, step), step)
            total = part[own, at, :].astype(F32) + abuf[n, at, :].astype(F32)
            for other in more:
                total = total + other[at, :].astype(F32)
            sums[n, at, :] = total.astype(BF16)
            return carry

        lax.fori_loop(0, rows // step, body, 0)

    for n in range(2):
        arrived(abuf.at[n], a_r.at[n])
        add(n)
        go(remote(sums.at[n], bbuf.at[n], b_s.at[n], b_r.at[n], x_near))
    yield
    arrived(abuf.at[2], a_r.at[2])
    arrived(bbuf.at[0], b_r.at[0])
    add(2, bbuf.at[0])
    go(remote(sums.at[2], cbuf, c_s, c_r, z_near))
    yield
    arrived(abuf.at[3], a_r.at[3])
    arrived(bbuf.at[1], b_r.at[1])
    arrived(cbuf, c_r)
    mine = owner(3, p.c)

    def last(i, carry):
        at = pl.ds(pl.multiple_of(i * step, step), step)
        total = part[mine, at, :].astype(F32) + abuf[3, at, :].astype(F32)
        finish(at, total + bbuf[1, at, :].astype(F32) + cbuf[at, :].astype(F32))
        return carry

    lax.fori_loop(0, rows // step, last, 0)
    for copy in sends:
        copy.wait_send()


def share_steps(p, gathered, s, r):
    sibling = (p.dp(p.z, p.m, 1 - p.c), p.x)
    x_near = (p.d, 1 - p.x)
    z_near = (p.dp(xor(p.z, 1), p.m, p.c), p.x)
    sends = []

    def at(fz, fx, c):
        return gathered.at[(xor(p.lo, fz) * 2 + c) * 2 + xor(p.x, fx)]

    def go(ref, number, device):
        copy = remote(ref, ref, s.at[number], r.at[number], device)
        copy.start()
        sends.append(copy)

    own = at(0, 0, p.c)
    go(own, 0, z_near)
    go(own, 1, x_near)
    go(own, 2, sibling)
    yield
    far = at(1, 0, p.c)
    arrived(far, r.at[0])
    go(far, 3, x_near)
    go(far, 4, sibling)
    beside = at(0, 1, p.c)
    arrived(beside, r.at[1])
    go(beside, 5, sibling)
    yield
    across = at(1, 1, p.c)
    arrived(across, r.at[3])
    go(across, 6, sibling)
    yield
    for number, (fz, fx) in ((2, (0, 0)), (4, (1, 0)), (5, (0, 1)), (6, (1, 1))):
        arrived(at(fz, fx, 1 - p.c), r.at[number])
    for copy in sends:
        copy.wait_send()


def swap_steps(p, both, o_s, o_r):
    rows = both.shape[0] // 2
    half = pl.ds(pl.multiple_of(p.x * rows, 16), rows)
    copy = remote(both.at[half], both.at[half], o_s, o_r, (p.d, 1 - p.x))
    copy.start()
    yield
    copy.wait()


def norm_root(value):
    return lax.rsqrt(jnp.mean(value * value, axis=-1, keepdims=True) + EPSILON)


def norm_back(value, scaled):
    root = norm_root(value)
    return root * scaled - value * root**3 * jnp.mean(value * scaled, axis=-1, keepdims=True)


def reduce_scratch(rows, width):
    return [
        pltpu.VMEM((4, rows, width), BF16),
        pltpu.VMEM((3, rows, width), BF16),
        pltpu.VMEM((2, rows, width), BF16),
        pltpu.VMEM((rows, width), BF16),
        DMA((4,)), DMA((4,)), DMA((2,)), DMA((2,)), DMA, DMA,
    ]


def attention_back_steps(p, low, qkv, probs, p_buf, p_sem, mixture, fa, tabg, n1, n1_copy, gqkv, part, ga, a_scatter):
    length = qkv.shape[0] // 4
    half = length // 2
    qw = mixture.shape[1]
    heads = qw // HEAD_DIM
    scaling = HEAD_DIM ** (-0.5)

    def fetch(n):
        return pltpu.make_async_copy(probs.at[n // heads, n % heads], p_buf.at[n % 4], p_sem.at[n % 4])

    for n in range(3):
        fetch(n).start()
    for s in range(4):
        here = pl.ds(s * length, length)
        cosine, signed = wide_tables(tabg[s])
        grads = low[2 * s : 2 * s + 2].reshape(length, low.shape[2])
        grad_mix = dot(grads, fa[:, qw + 128 :], ((1,), (0,))).astype(BF16)
        key = qkv[here, qw : qw + HEAD_DIM]
        value = qkv[here, qw + HEAD_DIM :]
        grad_value = jnp.zeros((length, HEAD_DIM), F32)
        grad_key = jnp.zeros((length, HEAD_DIM), F32)
        grad_query = []
        for h in range(heads):
            at = slice(HEAD_DIM * h, HEAD_DIM * h + HEAD_DIM)
            number = s * heads + h
            if number + 3 < 4 * heads:
                fetch(number + 3).start()
            fetch(number).wait()
            share = p_buf[number % 4]
            gm = grad_mix[:, at]
            gp = dot(gm, value, ((1,), (1,)))
            grad_value = grad_value + dot(share.astype(BF16), gm, ((0,), (0,)))
            centered = jnp.sum(share * gp, axis=-1, keepdims=True)
            gs = (share * (gp - centered)).astype(BF16)
            grad_query.append(dot(gs, key, ((1,), (0,))) * scaling)
            grad_key = grad_key + dot(gs, qkv[here, at], ((0,), (0,))) * scaling
        for b in range(qw // 128):
            pair = jnp.concatenate(grad_query[2 * b : 2 * b + 2], axis=1)
            gqkv[here, 128 * b : 128 * b + 128] = turn(pair, cosine, -signed).astype(BF16)
        pair = jnp.concatenate([grad_key, grad_value], axis=1)
        lanes = lanes_of(pair.shape)
        gqkv[here, qw:] = jnp.where(lanes < HEAD_DIM, turn(pair, cosine, -signed), pair).astype(BF16)
        for x in range(2):
            rows = pl.ds(s * length + x * half, half)
            part[s * 2 + x] = dot(gqkv[rows, :], fa[:, : qw + 128], ((1,), (1,))).astype(BF16)
        if s % 2:
            yield


def weight_grad_steps(low, mixture, n1, n1_copy, gqkv, ga, a_scatter):
    qw = mixture.shape[1]
    n1_copy.wait()
    width = low.shape[2]
    tile = 256

    def body(i, carry):
        at = pl.ds(pl.multiple_of(i * tile, tile), tile)
        rows = n1[:, :, at].reshape(-1, tile)
        ga[at, : qw + 128] = dot(rows, gqkv[...], ((0,), (0,))).astype(BF16)
        rows = low[:, :, at].reshape(-1, tile)
        ga[at, qw + 128 :] = dot(rows, mixture[...], ((0,), (0,))).astype(BF16)
        return carry

    lax.fori_loop(0, width // tile, body, 0)
    a_scatter.ready = True
    yield


def last_kernel(
    mid, a_waves, d_waves, g_waves, both, act, n2, n1, probs, hid, cot, x, qkv, mixture, fa, tabg, fg, fu, fd, down,
    output, result, gu_out, down_out, ga_out, gu, *scratch
):
    p = Place(mid)
    scratch = list(scratch)

    def take(count):
        taken = scratch[:count]
        del scratch[:count]
        return taken

    first_buf, second_buf, grad_hidden, low, gqkv, ga, p_buf, p_sem, in_sems = take(9)
    act_buf, w_buf, n_buf, g_buf, w_sem, n_sem, g_sem, low_free = take(8)
    r1, r2 = take(10), take(10)
    g_sems, o_sems, i_sems = take(2), take(2), take(2)
    gu_s, down_s, ga_s = take(8), take(8), take(8)
    loads = [
        pltpu.make_async_copy(both, low, in_sems.at[0]),
        pltpu.make_async_copy(act, act_buf, in_sems.at[1]),
        pltpu.make_async_copy(n1, second_buf, in_sems.at[2]),
    ]
    loads[0].start()
    loads[1].start()
    greet(all_devices(p))
    mine = (p.lo * 2 + p.c) * 2 + p.x
    rows = hid.shape[0]

    def there(at):
        return pl.ds(pl.multiple_of(p.x * rows + at.start, 16), 16)

    def finish(at, total):
        grads = cot[at, :].astype(F32) + norm_back(hid[at, :], total)
        grad_hidden[at, :] = grads
        low[mine, at, :] = grads.astype(BF16)

    def finish_out(at, total):
        output[there(at), :] = (hid[at, :] + total).astype(BF16)

    def finish_in(at, total):
        result[there(at), :] = (grad_hidden[at, :] + norm_back(x[at, :].astype(F32), total)).astype(BF16)

    scatter_d = Scatter(p, down, down_s[0], down_s[1], down_out, down_s[2:], d_waves)
    scatter_g = Scatter(p, gu, gu_s[0], gu_s[1], gu_out, gu_s[2:], g_waves)
    scatter_a = Scatter(p, ga, ga_s[0], ga_s[1], ga_out, ga_s[2:], a_waves)
    scatter_a.ready = scatter_g.ready = False

    def outputs():
        while not scatter_g.ready:
            yield
        yield from reduce_steps(p, second_buf, r2, finish_out)
        loads[2].start()
        yield from swap_steps(p, output, *o_sems)

    out = outputs()
    width = low.shape[2]
    tokens, units = act_buf.shape
    tile = w_buf.shape[2]
    tiles = width // tile

    def lines(i):
        return pl.ds(pl.multiple_of(i * tile, tile), tile)

    def weight(i, number, ref):
        slot = lax.rem(i, 2)
        return pltpu.make_async_copy(ref.at[lines(i)], w_buf.at[slot, number], w_sem.at[slot, number])

    def rows_in(i):
        slot = lax.rem(i, 2)
        return pltpu.make_async_copy(n2.at[:, :, lines(i)], n_buf.at[slot], n_sem.at[slot])

    def grad_out(i):
        slot = lax.rem(i, 2)
        return pltpu.make_async_copy(g_buf.at[slot], gu.at[lines(i)], g_sem.at[slot])

    def norm_part():
        def step(i, carry):
            weight(i, 0, fg).wait()
            weight(i, 1, fu).wait()

            @pl.when(i + 1 < tiles)
            def _():
                weight(i + 1, 0, fg).start()
                weight(i + 1, 1, fu).start()

            slot = lax.rem(i, 2)
            gate = low[:, :, :units].reshape(tokens, units)
            up = low[:, :, units:].reshape(tokens, units)
            value = dot(gate, w_buf[slot, 0], ((1,), (1,))) + dot(up, w_buf[slot, 1], ((1,), (1,)))
            first_buf[:, :, lines(i)] = value.astype(BF16).reshape(8, tokens // 8, tile)
            return carry

        weight(0, 0, fg).start()
        weight(0, 1, fu).start()
        loads[0].wait()
        lax.fori_loop(0, tiles, step, 0)

    def weight_part():
        def step(i, carry):
            weight(i, 0, fd).wait()
            rows_in(i).wait()

            @pl.when(i + 1 < tiles)
            def _():
                weight(i + 1, 0, fd).start()
                rows_in(i + 1).start()

            slot = lax.rem(i, 2)
            value = dot(act_buf[...], w_buf[slot, 0], ((1,), (1,)))
            second_buf[:, :, lines(i)] = value.astype(BF16).reshape(8, tokens // 8, tile)

            @pl.when(i >= 2)
            def _():
                grad_out(i - 2).wait()

            grads = low[...].reshape(tokens, 2 * units)
            g_buf[slot] = dot(n_buf[slot].reshape(tokens, tile), grads, ((0,), (0,))).astype(BF16)
            grad_out(i).start()
            return carry

        weight(0, 0, fd).start()
        rows_in(0).start()
        loads[1].wait()
        lax.fori_loop(0, tiles // 2, step, 0)
        yield
        lax.fori_loop(tiles // 2, tiles, step, 0)
        grad_out(tiles - 2).wait()
        grad_out(tiles - 1).wait()
        scatter_g.ready = True

    def chained():
        norm_part()
        summed = reduce_steps(p, first_buf, r1, finish)
        next(summed)
        yield
        next(summed)
        yield from weight_part()
        for device in (
            (p.dp(p.z, p.m, 1 - p.c), p.x),
            (p.d, 1 - p.x),
            (p.dp(xor(p.z, 1), p.m, p.c), p.x),
        ):
            pl.semaphore_signal(low_free, inc=1, device_id=device, device_id_type=MESH)
        yield from summed
        pl.semaphore_wait(low_free, 3)
        yield from share_steps(p, low, *g_sems)
        yield from attention_back_steps(
            p, low, qkv, probs, p_buf, p_sem, mixture, fa, tabg, second_buf, loads[2], gqkv, first_buf, ga, scatter_a
        )
        for _ in out:
            pass
        last = reduce_steps(p, first_buf, r1, finish_in)
        next(last)
        yield from weight_grad_steps(low, mixture, second_buf, loads[2], gqkv, ga, scatter_a)
        yield from last
        yield from swap_steps(p, result, *i_sems)

    drive(scatter_steps(scatter_d, scatter_g, scatter_a), chained(), after(OUT_AT, out))


def last(mid, both, act, n2, n1, probs, hid, cot, x, qkv, mixture, fa, tabg, fg, fu, fd, down):
    eight, rows, width = n2.shape
    n = 8 * mid
    units = act.shape[1]
    w_rows = width // n
    tile = 256
    a_waves, d_waves, g_waves = waves_of(w_rows, 4), waves_of(w_rows, 4), waves_of(w_rows, 8)
    return pl.pallas_call(
        functools.partial(last_kernel, mid, a_waves, d_waves, g_waves),
        out_shape=(
            jax.ShapeDtypeStruct((2 * rows, width), BF16),
            jax.ShapeDtypeStruct((2 * rows, width), BF16),
            jax.ShapeDtypeStruct((8, w_rows, 2 * units), BF16),
            jax.ShapeDtypeStruct((8, w_rows, down.shape[1]), BF16),
            jax.ShapeDtypeStruct((8, w_rows, fa.shape[1]), BF16),
            jax.ShapeDtypeStruct((width, 2 * units), BF16),
        ),
        in_specs=[ANY] * 5 + [VMEM] * 7 + [ANY] * 4,
        out_specs=(VMEM,) * 2 + (ANY,) * 4,
        scratch_shapes=[
            pltpu.VMEM((eight, rows, width), BF16),
            pltpu.VMEM((eight, rows, width), BF16),
            pltpu.VMEM((rows, width), F32),
            pltpu.VMEM((eight, rows, width), BF16),
            pltpu.VMEM(qkv.shape, BF16),
            pltpu.VMEM(fa.shape, BF16),
            pltpu.VMEM((4,) + probs.shape[2:], F32),
            DMA((4,)),
            DMA((3,)),
            pltpu.VMEM(act.shape, BF16),
            pltpu.VMEM((2, 2, tile, units), BF16),
            pltpu.VMEM((2, eight, rows, tile), BF16),
            pltpu.VMEM((2, tile, 2 * units), BF16),
            DMA((2, 2)), DMA((2,)), DMA((2,)), pltpu.SemaphoreType.REGULAR,
        ]
        + reduce_scratch(rows, width) * 2
        + [DMA((7,)), DMA((7,)), DMA, DMA, DMA, DMA]
        + scatter_scratch(mid, w_rows, 2 * units, g_waves)
        + scatter_scratch(mid, w_rows, down.shape[1], d_waves)
        + scatter_scratch(mid, w_rows, fa.shape[1], a_waves),
        compiler_params=pltpu.CompilerParams(
            collective_id=1, has_side_effects=True, vmem_limit_bytes=62 << 20
        ),
    )(both, act, n2, n1, probs, hid, cot, x, qkv, mixture, fa, tabg, fg, fu, fd, down)[:5]


def settle_kernel(
    gu, down, own, gains, low, w_gate, w_up, w_query, w_key, w_value,
    gate_o, up_o, down_o, query_o, key_o, value_o, out_o, gain_o, wide_o
):
    u = pl.program_id(0)
    units, qw = gate_o.shape[1], query_o.shape[1]
    kw = key_o.shape[1] // 4
    gain_one, gain_two = gains[:, 0:1], gains[:, 1:2]
    wide_o[...] = low[...].astype(F32)

    def total(ref, first, width):
        at = slice(first, first + width)
        return ref[0, 0, :, at].astype(F32) + ref[1, 0, :, at].astype(F32)

    def weigh(w, grad):
        return jnp.sum(w.astype(F32) * grad, axis=1, keepdims=True)

    gate, up = total(gu, 0, units), total(gu, units, units)
    gate_o[...] = gate * gain_two
    up_o[...] = up * gain_two
    two = weigh(w_gate[...], gate) + weigh(w_up[...], up)
    down_o[...] = total(down, 0, units).T
    query = total(own, 0, qw)
    query_o[...] = query * gain_one
    out_o[...] = total(own, qw + 2 * kw, out_o.shape[0]).T
    both = total(own, qw, 2 * kw)
    one = weigh(w_query[...], query)

    @pl.when(u == 0)
    def _():
        gain_o[...] = jnp.zeros_like(gain_o)

    lanes = lanes_of(gain_o.shape)
    for i in range(4):

        @pl.when(u == i)
        def _(i=i):
            at = slice(i * kw, i * kw + kw)
            key_o[:, at] = both[:, :kw] * gain_one
            value_o[:, at] = both[:, kw:] * gain_one
            more = weigh(w_key[:, at], both[:, :kw]) + weigh(w_value[:, at], both[:, kw:])
            gain_o[...] += jnp.where(lanes == 0, one + more, jnp.where(lanes == 1, two, 0.0))


def settle(gu, down, own, gains, low, w_gate, w_up, w_query, w_key, w_value):
    rows = gu.shape[1]
    length, width = low.shape
    units, qw, kw = w_gate.shape[1] // 4, w_query.shape[1] // 4, w_key.shape[1] // 4

    def parts(ref):
        return ref.reshape(2, 4, rows, ref.shape[2])

    def part_spec(ref):
        return pl.BlockSpec((2, 1, rows, ref.shape[2]), lambda u: (0, u, 0, 0))

    def column(w):
        return pl.BlockSpec((rows, w), lambda u: (0, u))

    def row(w):
        return pl.BlockSpec((w, rows), lambda u: (u, 0))

    def whole(*shape):
        return pl.BlockSpec(shape, lambda u: (0, 0))

    def out(*shape):
        return jax.ShapeDtypeStruct(shape, F32)

    lines = pl.BlockSpec((length // 4, width), lambda u: (u, 0))
    return pl.pallas_call(
        settle_kernel,
        grid=(4,),
        out_shape=(
            out(rows, 4 * units), out(rows, 4 * units), out(4 * units, rows), out(rows, 4 * qw), out(rows, 4 * kw),
            out(rows, 4 * kw), out(4 * qw, rows), out(rows, 128), out(length, width),
        ),
        in_specs=[
            part_spec(gu), part_spec(down), part_spec(own), whole(rows, 2), lines,
            column(units), column(units), column(qw), whole(rows, 4 * kw), whole(rows, 4 * kw),
        ],
        out_specs=(
            column(units), column(units), row(units), column(qw), whole(rows, 4 * kw), whole(rows, 4 * kw), row(qw),
            whole(rows, 128), lines,
        ),
        compiler_params=pltpu.CompilerParams(vmem_limit_bytes=48 << 20),
    )(parts(gu), parts(down), parts(own), gains, low, w_gate, w_up, w_query, w_key, w_value)


def token_table(segments):
    length = segments.shape[0]
    places = jnp.arange(length, dtype=jnp.int32)
    earlier = jnp.concatenate([segments[:1], segments[:-1]])
    begins = jnp.where(segments != earlier, places, 0)
    begin = jnp.max(jnp.where(places[:, None] >= places[None, :], begins[None, :], 0), axis=-1)
    halves = HEAD_DIM // 2
    inverse = THETA ** (-2.0 * jnp.arange(halves, dtype=F32) / HEAD_DIM)
    angles = (places - begin).astype(F32)[:, None] * inverse
    wide = jnp.broadcast_to(begin.astype(F32)[:, None], (length, 128 - 2 * halves))
    return jnp.concatenate([jnp.cos(angles), jnp.sin(angles), wide], axis=-1)


def dot(a, b, dims):
    return lax.dot_general(a, b, (dims, ((), ())), preferred_element_type=F32)


def local(
    mid, tokens, attn_gain, w_query, w_key, w_value, w_out, mlp_gain, w_gate, w_up, w_down, segment_ids, cotangent
):
    length, width = tokens.shape
    half = length // 2
    rows = w_query.shape[0]
    x_at = lax.axis_index("tensor")

    def blocks(w):
        return w.reshape(rows, 4, w.shape[1] // 4).transpose(1, 0, 2)

    gain_one, gain_two = attn_gain.astype(F32)[:, None], mlp_gain.astype(F32)[:, None]

    def scaled(w, gain):
        return blocks((w.astype(F32) * gain).astype(BF16))

    wg, wu, wd = scaled(w_gate, gain_two), scaled(w_up, gain_two), blocks(w_down.T)
    wa = jnp.concatenate(
        [scaled(w_query, gain_one), scaled(w_key, gain_one), scaled(w_value, gain_one), blocks(w_out.T)], axis=-1
    )
    qw = w_query.shape[1] // 4
    (
        cotg, tabg, fa, gate_w, up_w, normed, qkv, probs, mixture, hidden, n2, activated, by_gate, by_up, down_g, down_t
    ) = first(mid, tokens, cotangent, token_table(segment_ids), wa, wg, wu, wd, qw)
    own_x = lax.dynamic_slice_in_dim(tokens, x_at * half, half, 0)
    own_cot = lax.dynamic_slice_in_dim(cotangent, x_at * half, half, 0)
    cots = cotg.reshape(4 * length, width)
    grad_act = dot(cots, down_t, ((1,), (0,)))
    both = jnp.concatenate(
        [(grad_act * by_gate.astype(F32)).astype(BF16), (grad_act * by_up.astype(F32)).astype(BF16)], axis=1
    )
    eight = (8, half, width)
    output, input_grad, gu_parts, down_parts, a_parts = last(
        mid, both.reshape(8, half, -1), activated, n2, normed.reshape(eight), probs, hidden, own_cot, own_x,
        qkv, mixture, fa, tabg, gate_w, up_w, down_t, down_g
    )

    gains = jnp.stack([attn_gain, mlp_gain], axis=1).astype(F32)
    gate_g, up_g, down_g, query_g, key_g, value_g, out_g, gain_sums, input_grad = settle(
        gu_parts, down_parts, a_parts, gains, input_grad, w_gate, w_up, w_query, w_key, w_value
    )
    gain_g = lax.psum(gain_sums[:, :2], "tensor")
    return (
        output, input_grad, gain_g[:, 0], query_g, key_g, value_g, out_g, gain_g[:, 1], gate_g, up_g, down_g
    )


def solution(mesh):
    in_specs = (
        P("dp", None), P("dp"), P("dp", "tensor"), P("dp", "tensor"), P("dp", "tensor"), P("tensor", "dp"),
        P("dp"), P("dp", "tensor"), P("dp", "tensor"), P("tensor", "dp"), P("dp"), P("dp", None),
    )
    out_specs = (
        P("dp", None), P("dp", None), P("dp"), P("dp", "tensor"), P("dp", "tensor"), P("dp", "tensor"),
        P("tensor", "dp"), P("dp"), P("dp", "tensor"), P("dp", "tensor"), P("tensor", "dp"),
    )
    return jax.shard_map(
        functools.partial(local, mesh.shape["dp"] // 8),
        mesh=mesh, in_specs=in_specs, out_specs=out_specs, check_vma=False,
    )
```

```python
import functools

import jax
import jax.numpy as jnp
from jax import lax
from jax.experimental import pallas as pl
from jax.experimental.pallas import tpu as pltpu
from jax.sharding import PartitionSpec as P

HEAD_DIM = 64
EPSILON = 1e-05
THETA = 500000.0
MESH = pl.DeviceIdType.MESH
ANY = pl.BlockSpec(memory_space=pl.ANY)
VMEM = pl.BlockSpec(memory_space=pltpu.VMEM)
F32 = jnp.float32
BF16 = jnp.bfloat16
DMA = pltpu.SemaphoreType.DMA
COT_AT = 7
OUT_AT = 4


class Place:
    def __init__(self, mid):
        self.mid = mid
        self.d = lax.axis_index("dp")
        self.x = lax.axis_index("tensor")
        self.c = self.d % 2
        self.m = (self.d // 2) % mid
        self.z = self.d // (2 * mid)
        self.lo = self.z % 2

    def dp(self, z, m, c):
        return (z * self.mid + m) * 2 + c

    def peer(self, k):
        return xor(self.z, k // 2), xor(self.c, k % 2)

    def other_m(self, j):
        return (self.m + 1 + j) % self.mid


def xor(a, k):
    if k == 0:
        return a
    low = a % 2
    high = a // 2
    if k % 2:
        low = 1 - low
    if k // 2:
        high = 1 - high
    return high * 2 + low


def remote(src, dst, send, recv, device):
    copy = pltpu.make_async_remote_copy(
        src_ref=src, dst_ref=dst, send_sem=send, recv_sem=recv, device_id=device, device_id_type=MESH
    )
    return copy


def greet(devices):
    barrier = pltpu.get_barrier_semaphore()
    for device in devices:
        pl.semaphore_signal(barrier, inc=1, device_id=device, device_id_type=MESH)
    pl.semaphore_wait(barrier, len(devices))


def arrived(dst, sem):
    pltpu.make_async_copy(dst, dst, sem).wait()


class Gather:
    def __init__(self, p, w, full, sems, waves):
        self.p, self.w, self.full, self.waves = p, w, full, waves
        self.z_s, self.r, self.f_s, self.loc = sems
        self.rows = w.shape[1] // waves
        self.block = p.lo * 2 + p.c
        self.order = list(range(7, 0, -1))
        self.pushes, self.sends = {}, []

    def at(self, wave):
        return pl.ds(wave * self.rows, self.rows)

    def there(self, d, wave):
        return self.full.at[pl.ds(pl.multiple_of(d * self.w.shape[1] + wave * self.rows, 16), self.rows)]

    def push(self, wave):
        p, at = self.p, self.at(wave)
        for k in self.order:
            z, c = p.peer(k)
            copy = remote(
                self.w.at[(z % 2) * 2 + c, at], self.there(p.d, wave), self.z_s.at[k, wave], self.r.at[p.d, wave],
                (p.dp(z, p.m, c), p.x),
            )
            copy.start()
            self.pushes[k, wave] = copy
        self.forward_one(self.w.at[self.block, at], p.d, wave, 0)

    def forward_one(self, src, d, wave, k):
        p = self.p
        for j in range(p.mid - 1):
            copy = remote(
                src, self.there(d, wave), self.f_s.at[k, wave, j], self.r.at[d, wave],
                (p.dp(p.z, p.other_m(j), p.c), p.x),
            )
            copy.start()
            self.sends.append(copy)

    def forward(self, wave):
        p = self.p
        for k in self.order:
            z, c = p.peer(k)
            d = p.dp(z, p.m, c)
            here = self.there(d, wave)
            arrived(here, self.r.at[d, wave])
            self.forward_one(here, d, wave, k)
        if wave == self.waves - 1:
            self.all_forwarded = True

    def start_own(self):
        self.all_forwarded = False
        rows = self.w.shape[1]
        at = pl.ds(pl.multiple_of(self.p.d * rows, 16), rows)
        self.own = pltpu.make_async_copy(self.w.at[self.block], self.full.at[at], self.loc)
        self.own.start()

    def pushed(self, wave):
        for k in self.order:
            self.pushes[k, wave].wait_send()

    def landed(self):
        p = self.p
        for wave in range(self.waves):
            for k in range(8):
                z, c = p.peer(k)
                for j in range(p.mid - 1):
                    d = p.dp(z, p.other_m(j), c)
                    arrived(self.there(d, wave), self.r.at[d, wave])
        self.own.wait()
        self.done = True

    def finish(self):
        if not getattr(self, "done", False):
            self.landed()
        for copy in self.sends:
            copy.wait_send()


def gather_steps(*gathers, lag=2):
    for g in gathers:
        g.start_own()
    items = [(g, wave) for g in gathers for wave in range(g.waves)]
    for n, (g, wave) in enumerate(items):
        if n >= lag:
            before, old = items[n - lag]
            before.pushed(old)
            before.forward(old)
        g.push(wave)
        yield
    for g, wave in items[max(0, len(items) - lag) :]:
        g.pushed(wave)
        g.forward(wave)
        yield
    for g in gathers:
        g.finish()


def gather_sems(mid, waves):
    return [DMA((8, waves)), DMA((8 * mid, waves)), DMA((8, waves, mid - 1)), DMA]


class Scatter:
    def __init__(self, p, g, own, other, out, sems, waves):
        self.p, self.g, self.own, self.other, self.out, self.waves = p, g, own, other, out, waves
        self.y_s, self.y_r, self.z_s, self.z_r, self.load, self.loc = sems
        self.full_rows = own.shape[1]
        self.rows = self.full_rows // waves
        self.order = list(range(7, -1, -1))
        self.y_sends, self.z_sends, self.loads = {}, [], {}
        self.ready = True

    def piece(self, d, wave):
        return self.g.at[pl.ds(pl.multiple_of(d * self.full_rows + wave * self.rows, 16), self.rows)]

    def at(self, wave):
        return pl.ds(wave * self.rows, self.rows)

    def start_loads(self):
        p = self.p
        for k in self.order:
            z, c = p.peer(k)
            at = pl.ds(pl.multiple_of(p.dp(z, p.m, c) * self.full_rows, 16), self.full_rows)
            copy = pltpu.make_async_copy(self.g.at[at], self.own.at[k], self.load.at[k])
            copy.start()
            self.loads[k] = copy

    def y_send(self, wave):
        p = self.p
        for k in self.order:
            z, c = p.peer(k)
            for j in range(p.mid - 1):
                m = p.other_m(j)
                there = p.mid - 2 - j
                copy = remote(
                    self.piece(p.dp(z, m, c), wave), self.other.at[there, k, self.at(wave)],
                    self.y_s.at[k, wave, j], self.y_r.at[k, wave, there], (p.dp(p.z, m, p.c), p.x),
                )
                copy.start()
                self.y_sends[k, wave, j] = copy

    def z_push(self, wave):
        p = self.p
        at = self.at(wave)
        me = p.z * 2 + p.c
        for k in self.order:
            z, c = p.peer(k)
            for j in range(p.mid - 1):
                arrived(self.other.at[j, k, at], self.y_r.at[k, wave, j])
            if wave == 0:
                self.loads[k].wait()

            def add(i, carry):
                here = pl.ds(pl.multiple_of(wave * self.rows + i * 16, 16), 16)
                total = self.own[k, here, :].astype(F32)
                for j in range(p.mid - 1):
                    total = total + self.other[j, k, here, :].astype(F32)
                self.own[k, here, :] = total.astype(BF16)
                return carry

            lax.fori_loop(0, self.rows // 16, add, 0)
            src, dst = self.own.at[k, at], self.out.at[me, at]
            if k == 0:
                copy = pltpu.make_async_copy(src, dst, self.loc.at[wave])
                copy.start()
                self.z_sends.append((copy, True))
            else:
                copy = remote(src, dst, self.z_s.at[k, wave], self.z_r.at[me, wave], (p.dp(z, p.m, c), p.x))
                copy.start()
                self.z_sends.append((copy, False))

    def y_sent(self, wave):
        for k in self.order:
            for j in range(self.p.mid - 1):
                self.y_sends[k, wave, j].wait_send()

    def finish(self):
        p = self.p
        for wave in range(self.waves):
            for k in range(1, 8):
                z, c = p.peer(k)
                src = z * 2 + c
                arrived(self.out.at[src, self.at(wave)], self.z_r.at[src, wave])
        for copy, here in self.z_sends:
            copy.wait() if here else copy.wait_send()


def scatter_steps(*scatters, lag=2):
    items = [(s, wave) for s in scatters for wave in range(s.waves)]
    pushed = 0
    for n, (s, wave) in enumerate(items):
        if not s.ready:
            while pushed < n:
                before, old = items[pushed]
                before.z_push(old)
                pushed += 1
            while not s.ready:
                yield
        if wave == 0:
            s.start_loads()
        if n >= lag:
            before, old = items[n - lag]
            before.y_sent(old)
        s.y_send(wave)
        while pushed < n:
            before, old = items[pushed]
            before.z_push(old)
            pushed += 1
        yield
    s, wave = items[-1]
    s.z_push(wave)
    yield
    for s, wave in items[max(0, len(items) - lag) :]:
        s.y_sent(wave)
    for s in scatters:
        s.finish()


def scatter_scratch(mid, rows, width, waves):
    return [
        pltpu.VMEM((8, rows, width), BF16),
        pltpu.VMEM((mid - 1, 8, rows, width), BF16),
        DMA((8, waves, mid - 1)), DMA((8, waves, mid - 1)), DMA((8, waves)), DMA((8, waves)), DMA((8,)),
        DMA((waves,)),
    ]


def waves_of(rows, most):
    return max(w for w in range(1, most + 1) if rows % (16 * w) == 0)


def drive(*streams):
    left = list(streams)
    while left:
        for stream in list(left):
            try:
                next(stream)
            except StopIteration:
                left.remove(stream)


def after(steps, stream):
    for _ in range(steps):
        yield
    yield from stream


def chain(*streams):
    for stream in streams:
        yield from stream


def all_devices(p):
    return (
        [(p.dp(z, p.m, c), p.x) for z, c in map(p.peer, range(1, 8))]
        + [(p.dp(p.z, p.other_m(j), p.c), p.x) for j in range(p.mid - 1)]
        + [(p.d, 1 - p.x)]
    )


def token_steps(p, tok, tokg, t_s, t_r, loc, whole):
    rows = tok.shape[0]
    half = rows // 2
    seq = p.lo * 2 + p.c
    z_near = (p.dp(xor(p.z, 1), p.m, p.c), p.x)
    c_near = (p.dp(p.z, p.m, 1 - p.c), p.x)
    x_near = (p.d, 1 - p.x)
    mine = pl.ds(pl.multiple_of(p.x * half, 16), half)
    theirs = pl.ds(pl.multiple_of((1 - p.x) * half, 16), half)
    if whole:
        mine = pl.ds(0, rows)
    far_seq = (1 - p.lo) * 2 + p.c
    c_seq = p.lo * 2 + 1 - p.c
    cc_seq = (1 - p.lo) * 2 + 1 - p.c
    sends = []

    def go(copy):
        copy.start()
        sends.append(copy)

    go(remote(tok.at[mine], tokg.at[seq, mine], t_s.at[0], t_r.at[0], z_near))
    go(remote(tok, tokg.at[seq], t_s.at[1], t_r.at[1], c_near))
    here = pltpu.make_async_copy(tok, tokg.at[seq], loc)
    here.start()
    yield
    arrived(tokg.at[far_seq, mine], t_r.at[0])
    if not whole:
        go(remote(tokg.at[far_seq, mine], tokg.at[far_seq, mine], t_s.at[2], t_r.at[2], x_near))
    go(remote(tokg.at[far_seq, mine], tokg.at[far_seq, mine], t_s.at[3], t_r.at[3], c_near))
    yield
    if not whole:
        arrived(tokg.at[far_seq, theirs], t_r.at[2])
        go(remote(tokg.at[far_seq, theirs], tokg.at[far_seq, theirs], t_s.at[4], t_r.at[4], c_near))
        yield
    here.wait()
    arrived(tokg.at[c_seq], t_r.at[1])
    arrived(tokg.at[cc_seq, mine], t_r.at[3])
    if not whole:
        arrived(tokg.at[cc_seq, theirs], t_r.at[4])
    for copy in sends:
        copy.wait_send()


def token_sems():
    return [DMA((5,)), DMA((5,)), DMA]


def lanes_of(shape):
    return lax.broadcasted_iota(jnp.int32, shape, 1)


def wide_tables(table):
    lanes = lanes_of(table.shape)
    half = HEAD_DIM // 2
    cosine = jnp.where(lanes < half, table, 0.0)
    sine = pltpu.roll(jnp.where((lanes >= half) & (lanes < 2 * half), table, 0.0), 128 - half, 1)
    spread = cosine + pltpu.roll(cosine, half, 1)
    spread = spread + pltpu.roll(spread, 2 * half, 1)
    signed = pltpu.roll(sine, half, 1) - sine
    signed = signed + pltpu.roll(signed, 2 * half, 1)
    return spread, signed


def turn(values, cosine, signed):
    half = HEAD_DIM // 2
    lanes = lanes_of(values.shape) % HEAD_DIM
    swapped = jnp.where(lanes < half, pltpu.roll(values, 128 - half, 1), pltpu.roll(values, half, 1))
    return values * cosine + swapped * signed


def attention_steps(p, tokg, tabg, fa, n1, qkv, probs, mixture, part, gather_a):
    length = tokg.shape[1]
    qw = mixture.shape[1]
    heads = qw // HEAD_DIM
    scaling = HEAD_DIM ** (-0.5)
    for s in range(4):

        def norm(i, carry):
            at = pl.ds(pl.multiple_of(i * 32, 32), 32)
            value = tokg[s, at, :].astype(F32)
            n1[pl.ds(pl.multiple_of(s * length + i * 32, 32), 32), :] = (value * norm_root(value)).astype(BF16)
            return carry

        lax.fori_loop(0, length // 32, norm, 0)
    yield
    while not gather_a.all_forwarded:
        yield
    gather_a.landed()
    for s in range(4):
        here = pl.ds(s * length, length)
        table = tabg[s]
        cosine, signed = wide_tables(table)
        pre = dot(n1[here, :], fa[:, : qw + 128], ((1,), (0,)))
        for b in range(qw // 128):
            at = slice(128 * b, 128 * b + 128)
            qkv[here, at] = turn(pre[:, at], cosine, signed).astype(BF16)
        last = pre[:, qw:]
        keys = turn(last, cosine, signed)
        lanes = lanes_of(last.shape)
        qkv[here, qw:] = jnp.where(lanes < HEAD_DIM, keys, last).astype(BF16)
        key = qkv[here, qw : qw + HEAD_DIM]
        value = qkv[here, qw + HEAD_DIM :]
        begin = table[:, 2 * HEAD_DIM // 2 : 2 * HEAD_DIM // 2 + 1]
        columns = lanes_of((length, length))
        allowed = (columns.astype(F32) >= begin) & (
            columns <= lax.broadcasted_iota(jnp.int32, (length, length), 0)
        )
        for h in range(heads):
            at = slice(HEAD_DIM * h, HEAD_DIM * h + HEAD_DIM)
            scores = dot(qkv[here, at], key, ((1,), (1,))) * scaling
            scores = jnp.where(allowed, scores, -1e30)
            exponent = jnp.exp(scores - jnp.max(scores, axis=-1, keepdims=True))
            share = exponent / jnp.sum(exponent, axis=-1, keepdims=True)
            probs[s, h] = share
            mixture[here, at] = dot(share.astype(BF16), value, ((1,), (0,))).astype(BF16)
        half = length // 2
        for x in range(2):
            rows = pl.ds(s * length + x * half, half)
            part[s * 2 + x] = dot(mixture[rows, :], fa[:, qw + 128 :], ((1,), (1,))).astype(BF16)
        yield


class Flag:
    def __init__(self):
        self.up = False


def then(stream, flag):
    yield from stream
    flag.up = True


def gated_steps(n2, fg, fu, cotg, act, by_gate, by_up, down, gate_up, cot_here):
    while not (gate_up[0].all_forwarded and gate_up[1].all_forwarded):
        yield
    for g in gate_up:
        g.landed()
    width = n2.shape[2]
    tokens, units = act.shape
    tile, rows = 256, 512

    for m in range(tokens // rows):

        def body(i, carry, m=m):
            at = pl.ds(pl.multiple_of(i * tile, tile), tile)
            here = pl.ds(m * rows, rows)
            each = n2.shape[1]
            lines = n2[m * rows // each : (m + 1) * rows // each].reshape(rows, width)
            gate = dot(lines, fg[:, at], ((1,), (0,)))
            up = dot(lines, fu[:, at], ((1,), (0,)))
            sigmoid = 1.0 / (1.0 + jnp.exp(-gate))
            silu = gate * sigmoid
            act[here, at] = (silu * up).astype(BF16)
            by_up[here, at] = silu.astype(BF16)
            by_gate[here, at] = (up * sigmoid * (1.0 + gate * (1.0 - sigmoid))).astype(BF16)
            return carry

        lax.fori_loop(0, units // tile, body, 0)
        yield
    while not cot_here.up:
        yield
    for part in range(2):

        def body(i, carry):
            at = pl.ds(pl.multiple_of(i * tile, tile), tile)
            lines = cotg[:, :, at].reshape(tokens, tile)
            down[at, :] = dot(lines, act[...], ((0,), (0,))).astype(BF16)
            return carry

        each = width // tile // 2
        lax.fori_loop(part * each, part * each + each, body, 0)
        yield


def first_kernel(mid, a_waves, waves, tok, cot, table, wa, wg, wu, wd, *refs):
    p = Place(mid)
    refs = list(refs)

    def take(count):
        taken = refs[:count]
        del refs[:count]
        return taken

    outs = take(FIRST_OUTS)
    fd = take(1)[0]
    kept = take(FIRST_OUTS)
    cotg, tabg, fa, fg, fu, n1, qkv, probs, mixture, hidden, n2, act, by_gate, by_up, down = kept
    tokg, part, out_sems = take(3)
    tok_sems, cot_sems, tab_sems = take(3), take(3), take(3)
    reduce_refs, share_refs = take(10), take(2)
    greet(all_devices(p))
    gather_a = Gather(p, wa, fa, take(4), a_waves)
    rest = [Gather(p, w, f, take(4), waves) for w, f in ((wg, fg), (wu, fu), (wd, fd))]
    seq = p.lo * 2 + p.c
    mine = seq * 2 + p.x
    half = hidden.shape[0]
    cot_here = Flag()
    leaving = []

    def leave(*numbers):
        for n in numbers:
            copy = pltpu.make_async_copy(kept[n], outs[n], out_sems.at[n])
            copy.start()
            leaving.append(copy)

    def finish(at, total):
        there = pl.ds(pl.multiple_of(p.x * half + at.start, 16), 16)
        value = tokg[seq, there, :].astype(F32) + total
        hidden[at, :] = value
        n2[mine, at, :] = (value * norm_root(value)).astype(BF16)

    def chained():
        yield from tokens
        yield from attention_steps(p, tokg, tabg, fa, n1, qkv, probs, mixture, part, gather_a)
        leave(1, 2, 5, 6, 7, 8)
        yield from reduce_steps(p, part, reduce_refs, finish)
        leave(9)
        yield from share_steps(p, n2, *share_refs)
        leave(10)
        yield from gated_steps(n2, fg, fu, cotg, act, by_gate, by_up, down, rest[:2], cot_here)
        leave(0, 3, 4, 11, 12, 13, 14)

    tab = token_steps(p, table, tabg, *tab_sems, whole=True)
    tokens = token_steps(p, tok, tokg, *tok_sems, whole=False)
    next(tokens)
    next(tab)
    drive(
        gather_steps(gather_a, *rest),
        chained(),
        tab,
        after(COT_AT, then(token_steps(p, cot, cotg, *cot_sems, whole=False), cot_here)),
    )
    for copy in leaving:
        copy.wait()


FIRST_OUTS = 15


def first(mid, tok, cot, table, wa, wg, wu, wd, qw):
    a_waves, waves = waves_of(wa.shape[1], 4), waves_of(wg.shape[1], 4)
    length, width = tok.shape
    n = 8 * mid
    heads = qw // HEAD_DIM
    tokens, units = 4 * length, wg.shape[2]

    def full(w):
        return ((n * w.shape[1], w.shape[2]), BF16)

    outs = [
        ((4,) + cot.shape, BF16),
        ((4,) + table.shape, F32),
        full(wa), full(wg), full(wu),
        ((tokens, width), BF16),
        ((tokens, qw + 128), BF16),
        ((4, heads, length, length), F32),
        ((tokens, qw), BF16),
        ((length // 2, width), F32),
        ((8, length // 2, width), BF16),
        ((tokens, units), BF16), ((tokens, units), BF16), ((tokens, units), BF16),
        ((width, units), BF16),
    ]
    return pl.pallas_call(
        functools.partial(first_kernel, mid, a_waves, waves),
        out_shape=[jax.ShapeDtypeStruct(*out) for out in outs + [full(wd)]],
        in_specs=[ANY] * 7,
        out_specs=[ANY] * (FIRST_OUTS + 1),
        scratch_shapes=[pltpu.VMEM(*out) for out in outs]
        + [
            pltpu.VMEM((4, length, width), BF16),
            pltpu.VMEM((8, length // 2, width), BF16),
            DMA((FIRST_OUTS,)),
        ]
        + token_sems() * 3
        + reduce_scratch(length // 2, width)
        + [DMA((7,)), DMA((7,))]
        + gather_sems(mid, a_waves)
        + gather_sems(mid, waves) * 3,
        compiler_params=pltpu.CompilerParams(
            collective_id=0, has_side_effects=True, vmem_limit_bytes=62 << 20
        ),
    )(tok, cot, table, wa, wg, wu, wd)


def reduce_steps(p, part, scratch, finish):
    abuf, sums, bbuf, cbuf, a_s, a_r, b_s, b_r, c_s, c_r = scratch
    sibling = (p.dp(p.z, p.m, 1 - p.c), p.x)
    x_near = (p.d, 1 - p.x)
    z_near = (p.dp(xor(p.z, 1), p.m, p.c), p.x)
    order = ((1, 1), (0, 1), (1, 0), (0, 0))
    sends = []

    def owner(n, c):
        fz, fx = order[n]
        return (xor(p.lo, fz) * 2 + c) * 2 + xor(p.x, fx)

    def go(copy):
        copy.start()
        sends.append(copy)

    for n in range(4):
        go(remote(part.at[owner(n, 1 - p.c)], abuf.at[n], a_s.at[n], a_r.at[n], sibling))
    yield
    rows = part.shape[1]
    step = 16

    def add(n, *more):
        own = owner(n, p.c)

        def body(i, carry):
            at = pl.ds(pl.multiple_of(i * step, step), step)
            total = part[own, at, :].astype(F32) + abuf[n, at, :].astype(F32)
            for other in more:
                total = total + other[at, :].astype(F32)
            sums[n, at, :] = total.astype(BF16)
            return carry

        lax.fori_loop(0, rows // step, body, 0)

    for n in range(2):
        arrived(abuf.at[n], a_r.at[n])
        add(n)
        go(remote(sums.at[n], bbuf.at[n], b_s.at[n], b_r.at[n], x_near))
    yield
    arrived(abuf.at[2], a_r.at[2])
    arrived(bbuf.at[0], b_r.at[0])
    add(2, bbuf.at[0])
    go(remote(sums.at[2], cbuf, c_s, c_r, z_near))
    yield
    arrived(abuf.at[3], a_r.at[3])
    arrived(bbuf.at[1], b_r.at[1])
    arrived(cbuf, c_r)
    mine = owner(3, p.c)

    def last(i, carry):
        at = pl.ds(pl.multiple_of(i * step, step), step)
        total = part[mine, at, :].astype(F32) + abuf[3, at, :].astype(F32)
        finish(at, total + bbuf[1, at, :].astype(F32) + cbuf[at, :].astype(F32))
        return carry

    lax.fori_loop(0, rows // step, last, 0)
    for copy in sends:
        copy.wait_send()


def share_steps(p, gathered, s, r):
    sibling = (p.dp(p.z, p.m, 1 - p.c), p.x)
    x_near = (p.d, 1 - p.x)
    z_near = (p.dp(xor(p.z, 1), p.m, p.c), p.x)
    sends = []

    def at(fz, fx, c):
        return gathered.at[(xor(p.lo, fz) * 2 + c) * 2 + xor(p.x, fx)]

    def go(ref, number, device):
        copy = remote(ref, ref, s.at[number], r.at[number], device)
        copy.start()
        sends.append(copy)

    own = at(0, 0, p.c)
    go(own, 0, z_near)
    go(own, 1, x_near)
    go(own, 2, sibling)
    yield
    far = at(1, 0, p.c)
    arrived(far, r.at[0])
    go(far, 3, x_near)
    go(far, 4, sibling)
    beside = at(0, 1, p.c)
    arrived(beside, r.at[1])
    go(beside, 5, sibling)
    yield
    across = at(1, 1, p.c)
    arrived(across, r.at[3])
    go(across, 6, sibling)
    yield
    for number, (fz, fx) in ((2, (0, 0)), (4, (1, 0)), (5, (0, 1)), (6, (1, 1))):
        arrived(at(fz, fx, 1 - p.c), r.at[number])
    for copy in sends:
        copy.wait_send()


def swap_steps(p, both, o_s, o_r):
    rows = both.shape[0] // 2
    half = pl.ds(pl.multiple_of(p.x * rows, 16), rows)
    copy = remote(both.at[half], both.at[half], o_s, o_r, (p.d, 1 - p.x))
    copy.start()
    yield
    copy.wait()


def norm_root(value):
    return lax.rsqrt(jnp.mean(value * value, axis=-1, keepdims=True) + EPSILON)


def norm_back(value, scaled):
    root = norm_root(value)
    return root * scaled - value * root**3 * jnp.mean(value * scaled, axis=-1, keepdims=True)


def reduce_scratch(rows, width):
    return [
        pltpu.VMEM((4, rows, width), BF16),
        pltpu.VMEM((3, rows, width), BF16),
        pltpu.VMEM((2, rows, width), BF16),
        pltpu.VMEM((rows, width), BF16),
        DMA((4,)), DMA((4,)), DMA((2,)), DMA((2,)), DMA, DMA,
    ]


def attention_back_steps(p, low, qkv, probs, p_buf, p_sem, mixture, fa, tabg, n1, n1_copy, gqkv, part, ga, a_scatter):
    length = qkv.shape[0] // 4
    half = length // 2
    qw = mixture.shape[1]
    heads = qw // HEAD_DIM
    scaling = HEAD_DIM ** (-0.5)

    def fetch(n):
        return pltpu.make_async_copy(probs.at[n // heads, n % heads], p_buf.at[n % 4], p_sem.at[n % 4])

    for n in range(3):
        fetch(n).start()
    for s in range(4):
        here = pl.ds(s * length, length)
        cosine, signed = wide_tables(tabg[s])
        grads = low[2 * s : 2 * s + 2].reshape(length, low.shape[2])
        grad_mix = dot(grads, fa[:, qw + 128 :], ((1,), (0,))).astype(BF16)
        key = qkv[here, qw : qw + HEAD_DIM]
        value = qkv[here, qw + HEAD_DIM :]
        grad_value = jnp.zeros((length, HEAD_DIM), F32)
        grad_key = jnp.zeros((length, HEAD_DIM), F32)
        grad_query = []
        for h in range(heads):
            at = slice(HEAD_DIM * h, HEAD_DIM * h + HEAD_DIM)
            number = s * heads + h
            if number + 3 < 4 * heads:
                fetch(number + 3).start()
            fetch(number).wait()
            share = p_buf[number % 4]
            gm = grad_mix[:, at]
            gp = dot(gm, value, ((1,), (1,)))
            grad_value = grad_value + dot(share.astype(BF16), gm, ((0,), (0,)))
            centered = jnp.sum(share * gp, axis=-1, keepdims=True)
            gs = (share * (gp - centered)).astype(BF16)
            grad_query.append(dot(gs, key, ((1,), (0,))) * scaling)
            grad_key = grad_key + dot(gs, qkv[here, at], ((0,), (0,))) * scaling
        for b in range(qw // 128):
            pair = jnp.concatenate(grad_query[2 * b : 2 * b + 2], axis=1)
            gqkv[here, 128 * b : 128 * b + 128] = turn(pair, cosine, -signed).astype(BF16)
        pair = jnp.concatenate([grad_key, grad_value], axis=1)
        lanes = lanes_of(pair.shape)
        gqkv[here, qw:] = jnp.where(lanes < HEAD_DIM, turn(pair, cosine, -signed), pair).astype(BF16)
        for x in range(2):
            rows = pl.ds(s * length + x * half, half)
            part[s * 2 + x] = dot(gqkv[rows, :], fa[:, : qw + 128], ((1,), (1,))).astype(BF16)
        if s % 2:
            yield


def weight_grad_steps(low, mixture, n1, n1_copy, gqkv, ga, a_scatter):
    qw = mixture.shape[1]
    n1_copy.wait()
    width = low.shape[2]
    tile = 256

    def body(i, carry):
        at = pl.ds(pl.multiple_of(i * tile, tile), tile)
        rows = n1[:, :, at].reshape(-1, tile)
        ga[at, : qw + 128] = dot(rows, gqkv[...], ((0,), (0,))).astype(BF16)
        rows = low[:, :, at].reshape(-1, tile)
        ga[at, qw + 128 :] = dot(rows, mixture[...], ((0,), (0,))).astype(BF16)
        return carry

    lax.fori_loop(0, width // tile, body, 0)
    a_scatter.ready = True
    yield


def last_kernel(
    mid, a_waves, d_waves, g_waves, both, act, n2, n1, probs, hid, cot_all, x_all, qkv, mixture, fa, tabg, fg, fu, fd, down,
    output, result, gu_out, down_out, ga_out, gu, *scratch
):
    p = Place(mid)
    scratch = list(scratch)

    def take(count):
        taken = scratch[:count]
        del scratch[:count]
        return taken

    first_buf, second_buf, grad_hidden, low, gqkv, ga, p_buf, p_sem, in_sems, cot, x = take(11)
    act_buf, w_buf, n_buf, g_buf, w_sem, n_sem, g_sem, low_free = take(8)
    r1, r2 = take(10), take(10)
    g_sems, o_sems, i_sems = take(2), take(2), take(2)
    gu_s, down_s, ga_s = take(8), take(8), take(8)
    loads = [
        pltpu.make_async_copy(both, low, in_sems.at[0]),
        pltpu.make_async_copy(act, act_buf, in_sems.at[1]),
        pltpu.make_async_copy(n1, second_buf, in_sems.at[2]),
    ]
    own_rows = pl.ds(pl.multiple_of(p.x * hid.shape[0], 16), hid.shape[0])
    for copy in (
        pltpu.make_async_copy(cot_all.at[own_rows], cot, in_sems.at[3]),
        pltpu.make_async_copy(x_all.at[own_rows], x, in_sems.at[4]),
    ):
        copy.start()
        loads.append(copy)
    loads[0].start()
    loads[1].start()
    greet(all_devices(p))
    mine = (p.lo * 2 + p.c) * 2 + p.x
    rows = hid.shape[0]

    def there(at):
        return pl.ds(pl.multiple_of(p.x * rows + at.start, 16), 16)

    def finish(at, total):
        grads = cot[at, :].astype(F32) + norm_back(hid[at, :], total)
        grad_hidden[at, :] = grads
        low[mine, at, :] = grads.astype(BF16)

    def finish_out(at, total):
        output[there(at), :] = (hid[at, :] + total).astype(BF16)

    def finish_in(at, total):
        result[there(at), :] = (grad_hidden[at, :] + norm_back(x[at, :].astype(F32), total)).astype(BF16)

    scatter_d = Scatter(p, down, down_s[0], down_s[1], down_out, down_s[2:], d_waves)
    scatter_g = Scatter(p, gu, gu_s[0], gu_s[1], gu_out, gu_s[2:], g_waves)
    scatter_a = Scatter(p, ga, ga_s[0], ga_s[1], ga_out, ga_s[2:], a_waves)
    scatter_a.ready = scatter_g.ready = False

    def outputs():
        while not scatter_g.ready:
            yield
        yield from reduce_steps(p, second_buf, r2, finish_out)
        loads[2].start()
        yield from swap_steps(p, output, *o_sems)

    out = outputs()
    width = low.shape[2]
    tokens, units = act_buf.shape
    tile = w_buf.shape[2]
    tiles = width // tile

    def lines(i):
        return pl.ds(pl.multiple_of(i * tile, tile), tile)

    def weight(i, number, ref):
        slot = lax.rem(i, 2)
        return pltpu.make_async_copy(ref.at[lines(i)], w_buf.at[slot, number], w_sem.at[slot, number])

    def rows_in(i):
        slot = lax.rem(i, 2)
        return pltpu.make_async_copy(n2.at[:, :, lines(i)], n_buf.at[slot], n_sem.at[slot])

    def grad_out(i):
        slot = lax.rem(i, 2)
        return pltpu.make_async_copy(g_buf.at[slot], gu.at[lines(i)], g_sem.at[slot])

    def norm_part():
        def step(i, carry):
            weight(i, 0, fg).wait()
            weight(i, 1, fu).wait()

            @pl.when(i + 1 < tiles)
            def _():
                weight(i + 1, 0, fg).start()
                weight(i + 1, 1, fu).start()

            slot = lax.rem(i, 2)
            gate = low[:, :, :units].reshape(tokens, units)
            up = low[:, :, units:].reshape(tokens, units)
            value = dot(gate, w_buf[slot, 0], ((1,), (1,))) + dot(up, w_buf[slot, 1], ((1,), (1,)))
            first_buf[:, :, lines(i)] = value.astype(BF16).reshape(8, tokens // 8, tile)
            return carry

        weight(0, 0, fg).start()
        weight(0, 1, fu).start()
        loads[0].wait()
        loads[3].wait()
        loads[4].wait()
        lax.fori_loop(0, tiles, step, 0)

    def weight_part():
        def step(i, carry):
            weight(i, 0, fd).wait()
            rows_in(i).wait()

            @pl.when(i + 1 < tiles)
            def _():
                weight(i + 1, 0, fd).start()
                rows_in(i + 1).start()

            slot = lax.rem(i, 2)
            value = dot(act_buf[...], w_buf[slot, 0], ((1,), (1,)))
            second_buf[:, :, lines(i)] = value.astype(BF16).reshape(8, tokens // 8, tile)

            @pl.when(i >= 2)
            def _():
                grad_out(i - 2).wait()

            grads = low[...].reshape(tokens, 2 * units)
            g_buf[slot] = dot(n_buf[slot].reshape(tokens, tile), grads, ((0,), (0,))).astype(BF16)
            grad_out(i).start()
            return carry

        weight(0, 0, fd).start()
        rows_in(0).start()
        loads[1].wait()
        lax.fori_loop(0, tiles // 2, step, 0)
        yield
        lax.fori_loop(tiles // 2, tiles, step, 0)
        grad_out(tiles - 2).wait()
        grad_out(tiles - 1).wait()
        scatter_g.ready = True

    def chained():
        norm_part()
        summed = reduce_steps(p, first_buf, r1, finish)
        next(summed)
        yield
        next(summed)
        yield from weight_part()
        for device in (
            (p.dp(p.z, p.m, 1 - p.c), p.x),
            (p.d, 1 - p.x),
            (p.dp(xor(p.z, 1), p.m, p.c), p.x),
        ):
            pl.semaphore_signal(low_free, inc=1, device_id=device, device_id_type=MESH)
        yield from summed
        pl.semaphore_wait(low_free, 3)
        yield from share_steps(p, low, *g_sems)
        yield from attention_back_steps(
            p, low, qkv, probs, p_buf, p_sem, mixture, fa, tabg, second_buf, loads[2], gqkv, first_buf, ga, scatter_a
        )
        for _ in out:
            pass
        last = reduce_steps(p, first_buf, r1, finish_in)
        next(last)
        yield from weight_grad_steps(low, mixture, second_buf, loads[2], gqkv, ga, scatter_a)
        yield from last
        yield from swap_steps(p, result, *i_sems)

    drive(scatter_steps(scatter_d, scatter_g, scatter_a), chained(), after(OUT_AT, out))


def last(mid, both, act, n2, n1, probs, hid, cot, x, qkv, mixture, fa, tabg, fg, fu, fd, down):
    eight, rows, width = n2.shape
    n = 8 * mid
    units = act.shape[1]
    w_rows = width // n
    tile = 256
    a_waves, d_waves, g_waves = waves_of(w_rows, 4), waves_of(w_rows, 4), waves_of(w_rows, 8)
    return pl.pallas_call(
        functools.partial(last_kernel, mid, a_waves, d_waves, g_waves),
        out_shape=(
            jax.ShapeDtypeStruct((2 * rows, width), BF16),
            jax.ShapeDtypeStruct((2 * rows, width), BF16),
            jax.ShapeDtypeStruct((8, w_rows, 2 * units), BF16),
            jax.ShapeDtypeStruct((8, w_rows, down.shape[1]), BF16),
            jax.ShapeDtypeStruct((8, w_rows, fa.shape[1]), BF16),
            jax.ShapeDtypeStruct((width, 2 * units), BF16),
        ),
        in_specs=[ANY] * 5 + [VMEM] + [ANY] * 2 + [VMEM] * 4 + [ANY] * 4,
        out_specs=(VMEM,) * 2 + (ANY,) * 4,
        scratch_shapes=[
            pltpu.VMEM((eight, rows, width), BF16),
            pltpu.VMEM((eight, rows, width), BF16),
            pltpu.VMEM((rows, width), F32),
            pltpu.VMEM((eight, rows, width), BF16),
            pltpu.VMEM(qkv.shape, BF16),
            pltpu.VMEM(fa.shape, BF16),
            pltpu.VMEM((4,) + probs.shape[2:], F32),
            DMA((4,)),
            DMA((5,)),
            pltpu.VMEM((rows, width), BF16),
            pltpu.VMEM((rows, width), BF16),
            pltpu.VMEM(act.shape, BF16),
            pltpu.VMEM((2, 2, tile, units), BF16),
            pltpu.VMEM((2, eight, rows, tile), BF16),
            pltpu.VMEM((2, tile, 2 * units), BF16),
            DMA((2, 2)), DMA((2,)), DMA((2,)), pltpu.SemaphoreType.REGULAR,
        ]
        + reduce_scratch(rows, width) * 2
        + [DMA((7,)), DMA((7,)), DMA, DMA, DMA, DMA]
        + scatter_scratch(mid, w_rows, 2 * units, g_waves)
        + scatter_scratch(mid, w_rows, down.shape[1], d_waves)
        + scatter_scratch(mid, w_rows, fa.shape[1], a_waves),
        compiler_params=pltpu.CompilerParams(
            collective_id=1, has_side_effects=True, vmem_limit_bytes=62 << 20
        ),
    )(both, act, n2, n1, probs, hid, cot, x, qkv, mixture, fa, tabg, fg, fu, fd, down)[:5]


def settle_kernel(
    gu, down, own, gains, low, w_gate, w_up, w_query, w_key, w_value,
    gate_o, up_o, down_o, query_o, key_o, value_o, out_o, gain_o, wide_o
):
    u = pl.program_id(0)
    units, qw = gate_o.shape[1], query_o.shape[1]
    kw = key_o.shape[1] // 4
    gain_one, gain_two = gains[:, 0:1], gains[:, 1:2]
    wide_o[...] = low[...].astype(F32)

    def total(ref, first, width):
        at = slice(first, first + width)
        return ref[0, 0, :, at].astype(F32) + ref[1, 0, :, at].astype(F32)

    def weigh(w, grad):
        return jnp.sum(w.astype(F32) * grad, axis=1, keepdims=True)

    gate, up = total(gu, 0, units), total(gu, units, units)
    gate_o[...] = gate * gain_two
    up_o[...] = up * gain_two
    two = weigh(w_gate[...], gate) + weigh(w_up[...], up)
    down_o[...] = total(down, 0, units).T
    query = total(own, 0, qw)
    query_o[...] = query * gain_one
    out_o[...] = total(own, qw + 2 * kw, out_o.shape[0]).T
    both = total(own, qw, 2 * kw)
    one = weigh(w_query[...], query)

    @pl.when(u == 0)
    def _():
        gain_o[...] = jnp.zeros_like(gain_o)

    lanes = lanes_of(gain_o.shape)
    for i in range(4):

        @pl.when(u == i)
        def _(i=i):
            at = slice(i * kw, i * kw + kw)
            key_o[:, at] = both[:, :kw] * gain_one
            value_o[:, at] = both[:, kw:] * gain_one
            more = weigh(w_key[:, at], both[:, :kw]) + weigh(w_value[:, at], both[:, kw:])
            gain_o[...] += jnp.where(lanes == 0, one + more, jnp.where(lanes == 1, two, 0.0))


def settle(gu, down, own, gains, low, w_gate, w_up, w_query, w_key, w_value):
    rows = gu.shape[1]
    length, width = low.shape
    units, qw, kw = w_gate.shape[1] // 4, w_query.shape[1] // 4, w_key.shape[1] // 4

    def parts(ref):
        return ref.reshape(2, 4, rows, ref.shape[2])

    def part_spec(ref):
        return pl.BlockSpec((2, 1, rows, ref.shape[2]), lambda u: (0, u, 0, 0))

    def column(w):
        return pl.BlockSpec((rows, w), lambda u: (0, u))

    def row(w):
        return pl.BlockSpec((w, rows), lambda u: (u, 0))

    def whole(*shape):
        return pl.BlockSpec(shape, lambda u: (0, 0))

    def out(*shape):
        return jax.ShapeDtypeStruct(shape, F32)

    lines = pl.BlockSpec((length // 4, width), lambda u: (u, 0))
    return pl.pallas_call(
        settle_kernel,
        grid=(4,),
        out_shape=(
            out(rows, 4 * units), out(rows, 4 * units), out(4 * units, rows), out(rows, 4 * qw), out(rows, 4 * kw),
            out(rows, 4 * kw), out(4 * qw, rows), out(rows, 128), out(length, width),
        ),
        in_specs=[
            part_spec(gu), part_spec(down), part_spec(own), whole(rows, 2), lines,
            column(units), column(units), column(qw), whole(rows, 4 * kw), whole(rows, 4 * kw),
        ],
        out_specs=(
            column(units), column(units), row(units), column(qw), whole(rows, 4 * kw), whole(rows, 4 * kw), row(qw),
            whole(rows, 128), lines,
        ),
        compiler_params=pltpu.CompilerParams(vmem_limit_bytes=48 << 20),
    )(parts(gu), parts(down), parts(own), gains, low, w_gate, w_up, w_query, w_key, w_value)


def token_table(segments):
    length = segments.shape[0]
    places = jnp.arange(length, dtype=jnp.int32)
    earlier = jnp.concatenate([segments[:1], segments[:-1]])
    begins = jnp.where(segments != earlier, places, 0)
    begin = jnp.max(jnp.where(places[:, None] >= places[None, :], begins[None, :], 0), axis=-1)
    halves = HEAD_DIM // 2
    inverse = THETA ** (-2.0 * jnp.arange(halves, dtype=F32) / HEAD_DIM)
    angles = (places - begin).astype(F32)[:, None] * inverse
    wide = jnp.broadcast_to(begin.astype(F32)[:, None], (length, 128 - 2 * halves))
    return jnp.concatenate([jnp.cos(angles), jnp.sin(angles), wide], axis=-1)


def dot(a, b, dims):
    return lax.dot_general(a, b, (dims, ((), ())), preferred_element_type=F32)


def local(
    mid, tokens, attn_gain, w_query, w_key, w_value, w_out, mlp_gain, w_gate, w_up, w_down, segment_ids, cotangent
):
    length, width = tokens.shape
    half = length // 2
    rows = w_query.shape[0]

    def blocks(w):
        return w.reshape(rows, 4, w.shape[1] // 4).transpose(1, 0, 2)

    gain_one, gain_two = attn_gain.astype(F32)[:, None], mlp_gain.astype(F32)[:, None]

    def scaled(w, gain):
        return blocks((w.astype(F32) * gain).astype(BF16))

    wg, wu, wd = scaled(w_gate, gain_two), scaled(w_up, gain_two), blocks(w_down.T)
    wa = jnp.concatenate(
        [scaled(w_query, gain_one), scaled(w_key, gain_one), scaled(w_value, gain_one), blocks(w_out.T)], axis=-1
    )
    qw = w_query.shape[1] // 4
    (
        cotg, tabg, fa, gate_w, up_w, normed, qkv, probs, mixture, hidden, n2, activated, by_gate, by_up, down_g, down_t
    ) = first(mid, tokens, cotangent, token_table(segment_ids), wa, wg, wu, wd, qw)
    cots = cotg.reshape(4 * length, width)
    grad_act = dot(cots, down_t, ((1,), (0,)))
    both = jnp.concatenate(
        [(grad_act * by_gate.astype(F32)).astype(BF16), (grad_act * by_up.astype(F32)).astype(BF16)], axis=1
    )
    eight = (8, half, width)
    output, input_grad, gu_parts, down_parts, a_parts = last(
        mid, both.reshape(8, half, -1), activated, n2, normed.reshape(eight), probs, hidden, cotangent, tokens,
        qkv, mixture, fa, tabg, gate_w, up_w, down_t, down_g
    )

    gains = jnp.stack([attn_gain, mlp_gain], axis=1).astype(F32)
    gate_g, up_g, down_g, query_g, key_g, value_g, out_g, gain_sums, input_grad = settle(
        gu_parts, down_parts, a_parts, gains, input_grad, w_gate, w_up, w_query, w_key, w_value
    )
    gain_g = lax.psum(gain_sums[:, :2], "tensor")
    return (
        output, input_grad, gain_g[:, 0], query_g, key_g, value_g, out_g, gain_g[:, 1], gate_g, up_g, down_g
    )


def solution(mesh):
    in_specs = (
        P("dp", None), P("dp"), P("dp", "tensor"), P("dp", "tensor"), P("dp", "tensor"), P("tensor", "dp"),
        P("dp"), P("dp", "tensor"), P("dp", "tensor"), P("tensor", "dp"), P("dp"), P("dp", None),
    )
    out_specs = (
        P("dp", None), P("dp", None), P("dp"), P("dp", "tensor"), P("dp", "tensor"), P("dp", "tensor"),
        P("tensor", "dp"), P("dp"), P("dp", "tensor"), P("dp", "tensor"), P("tensor", "dp"),
    )
    return jax.shard_map(
        functools.partial(local, mesh.shape["dp"] // 8),
        mesh=mesh, in_specs=in_specs, out_specs=out_specs, check_vma=False,
    )
```
